32 devices in a mesh: dp: 16 (over z, x, core), tensor: 2 (over y).
Axes of the slice: x: 2, y: 2, z: 4, core: 2. Of those that a mesh axis runs over, the one named last changes fastest.
Arguments:
- block_in: bfloat16 [4096, 768], P(('dp', 'tensor')), may hold values from -6 to 6
- attn_gain: float32 [768], replicated, may hold values from 0.5 to 1.5
- w_qkv: bfloat16 [768, 3, 768], P('dp', None, 'tensor'), may hold values from -0.21875 to 0.21875
- w_out: bfloat16 [768, 768], P('dp', 'tensor'), may hold values from -0.875 to 0.875
- rel_bias: float32 [32, 12], replicated, may hold values from -4 to 4
- moe_gain: float32 [768], replicated, may hold values from 0.5 to 1.5
- w_router: float32 [768, 2], replicated, may hold values from -0.15625 to 0.15625
- w_in: bfloat16 [768, 2, 3072], P('dp', None, 'tensor'), may hold values from -0.21875 to 0.21875
- w_down: bfloat16 [768, 2, 3072], P('dp', None, 'tensor'), may hold values from -0.3125 to 0.3125
- seq_lengths: int32 [16, 4], P('dp'), may hold values from 0 to 256, as said below
- expert_ids: int32 [4096, 1], P('dp'), may hold values from 0 to 1; in each aligned block of 256 rows (0 to 255, 256 to 511, ...) at most 168 rows name the same one
- rel_table: int32 [511], replicated, may hold values from 0 to 31
- out_grad: bfloat16 [4096, 768], P(('dp', 'tensor')), may hold values from -6 to 6
Outputs:
- block_out: bfloat16 [4096, 768], P(('dp', 'tensor'))
- grad_in: float32 [4096, 768], P(('dp', 'tensor'))
- grad_attn_gain: float32 [768], replicated
- grad_w_qkv: float32 [768, 3, 768], P('dp', None, 'tensor')
- grad_w_out: float32 [768, 768], P('dp', 'tensor')
- grad_rel_bias: float32 [32, 12], replicated
- grad_moe_gain: float32 [768], replicated
- grad_w_router: float32 [768, 2], replicated
- grad_w_in: float32 [768, 2, 3072], P('dp', None, 'tensor')
- grad_w_down: float32 [768, 2, 3072], P('dp', None, 'tensor')
The draws below stay inside these ranges and needn't reach their ends.
Inputs may be any that keep to these rules, and one draw needn't show every extreme that they name: `seq_lengths`: in each group the 4 lengths sum to 256, and the first is more than 128. In every draw some group holds one sequence of 256 tokens. `expert_ids`: among the 256 rows of one group no expert is named by more than 168 rows.
All inputs are finite; a program needn't handle non-finite values.
Results may differ from the reference program's by a relative error of at most 0.018.
Values may be sent and summed in bfloat16 or wider, within the bound.
No kernel may reach another device: no remote copies, remote signals or barrier semaphores. Data moves between devices by JAX's collectives and lax.ppermute only.
A program may use at most 192 MiB of HBM per device.

```python
import math
import jax
import jax.numpy as jnp
import numpy as np
from jax import lax

D = 768
HEADS = 12
HEAD_DIM = 64
FF = 3072
BUCKETS = 32
EXPERTS = 2
SEGS = 4
TOK_DEV = 256
CAP = 168
TOKENS = 4096
N_DP = 16


def draw_seq_lengths(key, part):
    key = jax.random.fold_in(key, 11)
    key_first, key_cuts, key_single = jax.random.split(key, 3)
    first = jax.random.randint(key_first, (N_DP, 1), TOK_DEV // 2 + 1, TOK_DEV + 1)
    rest = TOK_DEV - first
    cuts = jax.random.randint(key_cuts, (N_DP, SEGS - 2), 0, rest + 1)
    cuts = jnp.sort(cuts, axis=1)
    edges = jnp.concatenate([jnp.zeros((N_DP, 1), jnp.int32), cuts.astype(jnp.int32), rest.astype(jnp.int32)], axis=1)
    pieces = edges[:, 1:] - edges[:, :-1]
    lengths = jnp.concatenate([first.astype(jnp.int32), pieces], axis=1)
    single = jax.random.randint(key_single, (), 0, N_DP)
    whole_row = (jnp.arange(SEGS) == 0).astype(jnp.int32) * TOK_DEV
    chosen = (jnp.arange(N_DP) == single)[:, None]
    return jnp.where(chosen, whole_row[None, :], lengths).astype(jnp.int32)


def place_ends(values, own_key, smallest, high):
    longest = values.shape.index(max(values.shape))
    spots = []
    for shift in (0, 1):
        where = [jax.random.randint(jax.random.fold_in(own_key, axis), (), 0, length) for axis, length in enumerate(values.shape)]
        where[longest] = (where[longest] + shift) % values.shape[longest]
        spots.append(tuple(where))
    return values.at[spots[0]].set(smallest).at[spots[1]].set(high)


def levels(key, dims, cuts, low, high):
    factor_of = 1.0
    for axis_at, parts in cuts:
        steps = jax.random.uniform(jax.random.fold_in(jax.random.fold_in(key, 6), axis_at), (parts,), jnp.float32, low / len(cuts), high / len(cuts))
        factor_of = factor_of * jnp.repeat(jnp.exp(steps), dims[axis_at] // parts).reshape((-1,) + (1,) * (len(dims) - 1 - axis_at))
    return factor_of


def assign_block(own_key, own, number, rows, number_of, top, most, slope):
    ranking = jax.random.permutation(own_key, number_of)
    crowded, ordinary = load_shares(number_of, rows * top, most, slope, True), load_shares(number_of, rows * top, most, slope, False)
    places = jnp.arange(number_of)

    def named(sizes, rotation):
        used = int((sizes > 0).sum())
        fixed = max(1, used // 4)
        moved = fixed + (places - fixed + rotation * (used - fixed)) % max(1, number_of - fixed)
        return jnp.zeros((number_of,), jnp.int32).at[ranking[jnp.where(places < fixed, places, moved)]].set(jnp.asarray(sizes, jnp.int32))

    sizes = jnp.where(number % 4 == 0, named(crowded, number // 4), named(ordinary, number - number // 4 - 1))
    mixed = jax.random.permutation(jax.random.fold_in(own, 3), number_of)
    source_of, sink = mixed[0:number_of // 2 * 2:2], mixed[1:number_of // 2 * 2:2]
    room = jnp.minimum(sizes[source_of] - 1, most - sizes[sink]) // 2
    room = jnp.where((source_of == ranking[0]) | (sink == ranking[0]) | (sizes[sink] == 0), 0, jnp.maximum(room, 0))
    moved = jax.random.randint(jax.random.fold_in(own, 4), (number_of // 2,), 0, 1 << 20) % (room + 1)
    sizes = sizes.at[source_of].add(-moved).at[sink].add(moved)
    labels = jnp.searchsorted(jnp.cumsum(sizes), jnp.arange(rows * top), side="right").astype(jnp.int32)
    grid = labels.reshape(top, rows).T
    grid = grid[jax.random.permutation(jax.random.fold_in(own, 1), rows)]
    rotation = jax.random.randint(jax.random.fold_in(own, 2), (rows, 1), 0, top)
    return jnp.take_along_axis(grid, (jnp.arange(top)[None, :] + rotation) % top, axis=1)


def load_shares(number_of, total, reach, lean, full):
    loads = [(1 << 20) // math.isqrt(grade ** lean) + 1 for grade in range(1, number_of + 1)]
    largest = reach if full else min(reach, max(-(-total // number_of), total * loads[0] // sum(loads)))
    least = 1 if total - largest >= number_of - 1 else 0
    counts, spare = [largest] + [least] * (number_of - 1), total - largest - least * (number_of - 1)
    while spare > 0:
        movable = [i for i in range(1, number_of) if counts[i] < largest] or [i for i in range(1, number_of) if counts[i] < reach]
        whole, left = sum([loads[i] for i in movable]), spare
        for i in movable:
            addition = min(reach - counts[i], max(1, left * loads[i] // whole), spare)
            counts[i] = counts[i] + addition
            spare = spare - addition
    return np.array(counts)


def normal_values(own_key, extent, width, limit, shards=(), held_as=jnp.bfloat16):
    values = width * jax.random.normal(own_key, extent, jnp.float32)
    if shards:
        values = values * levels(own_key, extent, shards, -0.22, 0.18)
    return jnp.clip(values, -limit, limit).astype(held_as)


def setup_inputs(seed: int = 0) -> dict:
    arg_keys = jax.random.split(jax.random.key(seed), 14)
    block_in = normal_values(arg_keys[0], (TOKENS, D), 1.0, 6.0, ((0, 32),))
    attn_gain = jnp.clip(1.0 + 0.1 * jax.random.normal(arg_keys[1], (D,), jnp.float32), 0.5, 1.5)
    w_qkv = normal_values(arg_keys[2], (D, 3, D), D ** -0.5, 0.21875, ((0, 16), (2, 2)))
    w_out = normal_values(arg_keys[3], (D, D), (D // 16) ** -0.5, 0.875, ((0, 16), (1, 2)))
    rel_bias = normal_values(arg_keys[4], (BUCKETS, HEADS), 1.0, 4.0, (), jnp.float32)
    moe_gain = jnp.clip(1.0 + 0.1 * jax.random.normal(arg_keys[5], (D,), jnp.float32), 0.5, 1.5)
    w_router = normal_values(arg_keys[6], (D, EXPERTS), (2 * D) ** -0.5, 0.15625, (), jnp.float32)
    w_in = normal_values(arg_keys[7], (D, EXPERTS, FF), D ** -0.5, 0.21875, ((0, 16), (2, 2)))
    w_down = normal_values(arg_keys[8], (D, EXPERTS, FF), (FF // 8) ** -0.5, 0.3125, ((0, 16), (2, 2)))
    seq_lengths = draw_seq_lengths(jax.random.fold_in(arg_keys[13], 71), 0)
    expert_ids_keys = jax.random.split(jax.random.fold_in(arg_keys[10], 1), TOKENS // TOK_DEV)
    expert_ids_turns = jax.random.permutation(jax.random.fold_in(arg_keys[10], 3), TOKENS // TOK_DEV)
    expert_ids = jax.vmap(lambda own, number: assign_block(jax.random.fold_in(arg_keys[10], 2), own, number, TOK_DEV, EXPERTS, 1, CAP, 2))(expert_ids_keys, expert_ids_turns).reshape((TOKENS, 1))
    rel_table = place_ends(jax.random.randint(arg_keys[11], (2 * TOK_DEV - 1,), 0, BUCKETS), jax.random.fold_in(arg_keys[11], 1), 0, BUCKETS - 1).astype(jnp.int32)
    out_grad = normal_values(arg_keys[12], (TOKENS, D), 1.0, 6.0, ((0, 32),))
    return {"block_in": block_in, "attn_gain": attn_gain, "w_qkv": w_qkv, "w_out": w_out, "rel_bias": rel_bias, "moe_gain": moe_gain, "w_router": w_router, "w_in": w_in, "w_down": w_down, "seq_lengths": seq_lengths, "expert_ids": expert_ids, "rel_table": rel_table, "out_grad": out_grad}


EPS = 1e-06
NEG = -1e+30
HIGH = lax.Precision.HIGHEST

@jax.custom_vjp
def low(v):
    return lax.optimization_barrier(v.astype(jnp.bfloat16)).astype(jnp.float32)

@jax.custom_vjp
def low_back(v):
    return v

def low_keep(v):
    return (low(v), None)

def low_pass(kept, grad):
    return (grad,)

def back_keep(v):
    return (v, None)

def back_low(kept, grad):
    return (low(grad),)
low.defvjp(low_keep, low_pass)
low_back.defvjp(back_keep, back_low)

def rms_normed(rows, gain):
    return rows * lax.rsqrt(lax.optimization_barrier(jnp.mean(rows * rows, axis=-1, keepdims=True)) + EPS) * gain

def group_layer(params, block_rows, lengths, expert_col, rel_table):
    attn_gain, w_qkv, w_out, rel_bias, moe_gain, w_router, w_in, w_down = params
    count = block_rows.shape[0]
    places = jnp.arange(count, dtype=jnp.int32)
    ends = jnp.cumsum(lengths)
    seq_ids = lax.optimization_barrier(jnp.sum((places[:, None] >= ends[None, :]).astype(jnp.int32), axis=1))
    same_seq = seq_ids[:, None] == seq_ids[None, :]
    normed = low(rms_normed(block_rows, attn_gain))
    projected = low(low_back(jnp.einsum('td,dsk->stk', normed, w_qkv, precision=HIGH)))
    queries = projected[0].reshape(count, HEADS, HEAD_DIM)
    keys_all = projected[1].reshape(count, HEADS, HEAD_DIM)
    values_all = projected[2].reshape(count, HEADS, HEAD_DIM)
    buckets = rel_table[places[None, :] - places[:, None] + (count - 1)]
    bias = jnp.transpose(rel_bias[buckets], (2, 0, 1))
    raw = jnp.einsum('qhd,khd->hqk', queries, keys_all, precision=HIGH) * HEAD_DIM ** (-0.5) + bias
    scores = low_back(jnp.where(same_seq[None], raw, NEG))
    probs = low(jax.nn.softmax(scores, axis=-1))
    context = jnp.einsum('hqk,khd->qhd', probs, values_all, precision=HIGH).reshape(count, D)
    context = low(low_back(context))
    attended = low_back(jnp.einsum('tk,dk->td', context, w_out, precision=HIGH))
    hidden = block_rows + attended
    mixed = rms_normed(hidden, moe_gain)
    router_probs = jax.nn.softmax(jnp.dot(mixed, w_router, precision=HIGH), axis=-1)
    hits = expert_col[:, None] == jnp.arange(EXPERTS, dtype=jnp.int32)[None, :]
    gate = lax.optimization_barrier(jnp.sum(router_probs * hits.astype(jnp.float32), axis=1))
    running = jnp.cumsum(hits.astype(jnp.int32), axis=0)
    slot = lax.optimization_barrier(jnp.sum(running * hits.astype(jnp.int32), axis=1)) - 1
    flat = expert_col * CAP + slot
    source = jnp.full((EXPERTS * CAP,), count, jnp.int32).at[flat].set(places)
    filled = (source < count).astype(jnp.float32)
    source = jnp.minimum(source, count - 1)
    sent = low(mixed)
    blocks = (sent[source] * filled[:, None]).reshape(EXPERTS, CAP, D)
    pre = low_back(jnp.einsum('ecd,def->ecf', blocks, w_in, precision=HIGH))
    active = low(jax.nn.gelu(pre, approximate=True))
    returned = jnp.einsum('ecf,def->ecd', active, w_down, precision=HIGH).reshape(EXPERTS * CAP, D)
    routed = low_back(returned[flat])
    return hidden + gate[:, None] * routed

def reference(block_in, attn_gain, w_qkv, w_out, rel_bias, moe_gain, w_router, w_in, w_down, seq_lengths, expert_ids, rel_table, out_grad):
    params = tuple((array.astype(jnp.float32) for array in (attn_gain, w_qkv, w_out, rel_bias, moe_gain, w_router, w_in, w_down)))
    rows = block_in.astype(jnp.float32)
    experts_all = expert_ids[:, 0].reshape(N_DP, TOK_DEV)
    layer = jax.checkpoint(group_layer)

    def forward(rows, params):
        grouped = rows.reshape(N_DP, TOK_DEV, D)

        def group_result(pieces):
            block_rows, lengths, expert_col = pieces
            return layer(params, block_rows, lengths, expert_col, rel_table)
        results = lax.map(group_result, (grouped, seq_lengths, experts_all))
        return results.reshape(N_DP * TOK_DEV, D)
    result, pullback = jax.vjp(forward, rows, params)
    grad_rows, grad_params = pullback(out_grad.astype(jnp.float32))
    return (result.astype(jnp.bfloat16), grad_rows, grad_params[0], grad_params[1], grad_params[2], grad_params[3], grad_params[4], grad_params[5], grad_params[6], grad_params[7])
```

```python
import jax
import jax.numpy as jnp
from jax import lax
from jax.experimental import pallas as pl
from jax.experimental.pallas import tpu as pltpu
from jax.sharding import PartitionSpec as P

HEAD_DIM = 64
EXPERTS = 2
CAP = 176

LONGEST = 16

EPS = 1e-06
NEG = -1e30
HIGH = lax.Precision.HIGHEST
BF = jnp.bfloat16
F32 = jnp.float32


def ring_chip(place, chips):
    place = place % chips
    return jnp.where(place < chips // 2, 2 * place, 2 * (chips - 1 - place) + 1)


def ring_place(chip, chips):
    return jnp.where(chip % 2 == 0, chip // 2, chips - 1 - chip // 2)


class Ring:
    def __init__(self):
        self.n = lax.axis_size("dp")
        self.chips = self.n // 2
        order = [2 * i for i in range(self.chips // 2)]
        order = order + [c + 1 for c in reversed(order)]
        pairs = [
            (order[i] * 2 + k, order[(i + 1) % self.chips] * 2 + k)
            for i in range(self.chips)
            for k in (0, 1)
        ]
        self.right = pairs
        self.left = [(b, a) for a, b in pairs]
        self.swap = [(i, i ^ 1) for i in range(self.n)]
        index = lax.axis_index("dp")
        self.core = index % 2
        self.place = ring_place(index // 2, self.chips)
        reach = self.chips // 2
        self.distances = [0] + [d for s in range(1, reach) for d in (-s, s)] + [reach]

    def chip_at(self, distance):
        return ring_chip(self.place + distance + self.chips, self.chips)

    def gather(self, x):
        rows, width = x.shape
        if self.chips > LONGEST:
            return lax.all_gather(x, "dp", axis=0, tiled=True)
        reach = self.chips // 2
        r = l = x
        pieces = [x]
        for _ in range(reach - 1):
            r = lax.ppermute(r, "dp", self.right)
            l = lax.ppermute(l, "dp", self.left)
            pieces += [r, l]
        half = width // 2
        main = jnp.concatenate(pieces, axis=0)
        main_sib = lax.ppermute(main, "dp", self.swap)
        r = lax.ppermute(r[:, :half], "dp", self.right)
        l = lax.ppermute(l[:, half:], "dp", self.left)
        tail = jnp.concatenate([r, l], axis=1)
        tail_sib = lax.ppermute(tail, "dp", self.swap)
        chips = jnp.stack([self.chip_at(d) for d in self.distances])
        own = chips * 2 + self.core
        sib = chips * 2 + 1 - self.core
        return assemble(main, tail, main_sib, tail_sib, jnp.concatenate([own, sib]))

    def scatter(self, grads, rows):
        width = grads.shape[1]
        if self.chips > LONGEST:
            return lax.psum_scatter(grads, "dp", scatter_dimension=0, tiled=True).astype(F32)
        reach = self.chips // 2
        half = width // 2
        split = grads.reshape(self.chips, 2, rows, width)
        other = lax.dynamic_index_in_dim(split, 1 - self.core, 1, keepdims=False)
        mine = lax.dynamic_index_in_dim(split, self.core, 1, keepdims=False)
        got = lax.ppermute(other, "dp", self.swap)
        both = (mine.astype(F32) + got.astype(F32)).astype(BF)

        def local(distance):
            return lax.dynamic_index_in_dim(both, self.chip_at(distance), 0, keepdims=False)

        far = local(reach)
        r = lax.ppermute(far[:, :half], "dp", self.right)
        l = lax.ppermute(far[:, half:], "dp", self.left)
        for s in range(reach - 1, 0, -1):
            near_r, near_l = local(s), local(-s)
            if s == reach - 1:
                r = jnp.concatenate([add_low(r, near_r[:, :half]), near_r[:, half:]], axis=1)
                l = jnp.concatenate([near_l[:, :half], add_low(l, near_l[:, half:])], axis=1)
            else:
                r, l = add_low(r, near_r), add_low(l, near_l)
            r = lax.ppermute(r, "dp", self.right)
            l = lax.ppermute(l, "dp", self.left)
        return local(0).astype(F32) + r.astype(F32) + l.astype(F32)


def add_low(a, b):
    return (a.astype(F32) + b.astype(F32)).astype(BF)


def assemble(main, tail, main_sib, tail_sib, owners):
    rows, width = tail.shape
    chips = main.shape[0] // rows + 1
    if rows % 16:
        own = jnp.concatenate([main, tail]).reshape(chips, rows, width)
        sib = jnp.concatenate([main_sib, tail_sib]).reshape(chips, rows, width)
        out = jnp.zeros((2 * chips, rows, width), main.dtype).at[owners].set(
            jnp.concatenate([own, sib])
        )
        return out.reshape(2 * chips * rows, width)

    def kernel(owners_ref, main_ref, tail_ref, main_sib_ref, tail_sib_ref, out_ref, sems):
        copies = []
        for at, (big, small) in enumerate(((main_ref, tail_ref), (main_sib_ref, tail_sib_ref))):
            for i in range(chips):
                source = small if i == chips - 1 else big.at[pl.ds(i * rows, rows)]
                owner = owners_ref[at * chips + i]
                target = out_ref.at[pl.ds(pl.multiple_of(owner * rows, 16), rows)]
                copies.append(pltpu.make_async_copy(source, target, sems.at[at * chips + i]))
        for copy in copies:
            copy.start()
        for copy in copies:
            copy.wait()

    anywhere = pl.BlockSpec(memory_space=pl.ANY)
    return pl.pallas_call(
        kernel,
        out_shape=jax.ShapeDtypeStruct((2 * chips * rows, width), main.dtype),
        in_specs=[pl.BlockSpec(memory_space=pltpu.SMEM)] + [anywhere] * 4,
        out_specs=anywhere,
        scratch_shapes=[pltpu.SemaphoreType.DMA((2 * chips,))],
        cost_estimate=pl.CostEstimate(
            flops=0, bytes_accessed=8 * chips * rows * width, transcendentals=0
        ),
        name="assemble",
    )(owners, main, tail, main_sib, tail_sib)


def swap_tensor(x):
    return lax.ppermute(x, "tensor", [(0, 1), (1, 0)])


def whole_rows(own, other, rank):
    return jnp.where(
        rank == 0, jnp.concatenate([own, other], axis=0), jnp.concatenate([other, own], axis=0)
    )


def sum_everywhere(x):
    x = x + swap_tensor(x)
    step = 1
    while step < lax.axis_size("dp"):
        x = x + lax.ppermute(x, "dp", [(i, i ^ step) for i in range(lax.axis_size("dp"))])
        step *= 2
    return x


def rms_scale(rows):
    return lax.rsqrt(jnp.mean(rows * rows, axis=-1, keepdims=True) + EPS)


def norm_back(grad, normed, scale, gain):
    weighted = grad * gain
    return scale * (weighted - normed * jnp.mean(weighted * normed, axis=-1, keepdims=True))


def toeplitz_rows(by_offset_heads, count):
    heads_here = by_offset_heads.shape[0]
    padded = jnp.concatenate(
        [by_offset_heads, jnp.zeros((heads_here, 1), by_offset_heads.dtype)], axis=1
    )
    tiled = jnp.tile(padded, (1, count))
    window = tiled[:, count - 1 : count - 1 + count * (2 * count - 1)]
    return window.reshape(heads_here, count, 2 * count - 1)[:, :, :count]


def diagonal_sums(matrix):
    heads_here, count, _ = matrix.shape
    widened = jnp.concatenate(
        [matrix, jnp.zeros((heads_here, count, count - 1), matrix.dtype)], axis=2
    )
    line = widened.reshape(heads_here, count * (2 * count - 1))
    line = jnp.concatenate(
        [
            jnp.zeros((heads_here, count - 1), matrix.dtype),
            line,
            jnp.zeros((heads_here, 1), matrix.dtype),
        ],
        axis=1,
    )
    return jnp.sum(line.reshape(heads_here, count, 2 * count), axis=1)[:, : 2 * count - 1]


def dot32(a, b, dims):
    return lax.dot_general(a, b, (dims, ((), ())), preferred_element_type=F32)


NN = ((1,), (0,))
NT = ((1,), (1,))
TN = ((0,), (0,))


def body(
    block_in,
    attn_gain,
    w_qkv,
    w_out,
    rel_bias,
    moe_gain,
    w_router,
    w_in,
    w_down,
    seq_lengths,
    expert_ids,
    rel_table,
    out_grad,
):
    rows_local, width = block_in.shape
    rank = lax.axis_index("tensor")
    ring = Ring()
    shard = w_out.shape[0]
    head_cols = w_out.shape[1]
    units = w_in.shape[2]
    heads_local = head_cols // HEAD_DIM
    count = 2 * rows_local

    attn_shard = jnp.concatenate([w_qkv.reshape(shard, 3 * head_cols), w_out], axis=1)
    x_all = whole_rows(block_in, swap_tensor(block_in), rank).astype(F32)
    attn_all = ring.gather(attn_shard)
    in_all = ring.gather(w_in.reshape(shard, EXPERTS * units))
    down_all = ring.gather(w_down.reshape(shard, EXPERTS * units))
    qkv_all, out_all = attn_all[:, : 3 * head_cols], attn_all[:, 3 * head_cols :]
    grad_out = whole_rows(out_grad, swap_tensor(out_grad), rank).astype(F32)

    scale_one = rms_scale(x_all)
    n_one = x_all * scale_one
    normed_one = (n_one * attn_gain).astype(BF)
    projected = dot32(normed_one, qkv_all, NN).astype(BF).reshape(count, 3, heads_local, HEAD_DIM)
    queries, keys_all, values_all = projected[:, 0], projected[:, 1], projected[:, 2]

    places = jnp.arange(count, dtype=jnp.int32)
    ends = jnp.cumsum(seq_lengths[0])
    seq_ids = jnp.sum((places[:, None] >= ends[None, :]).astype(jnp.int32), axis=1)
    same_seq = seq_ids[:, None] == seq_ids[None, :]
    bias_local = lax.dynamic_slice_in_dim(rel_bias, rank * heads_local, heads_local, 1)
    bucket_hits = (
        rel_table[:, None] == jnp.arange(rel_bias.shape[0], dtype=jnp.int32)[None, :]
    ).astype(F32)
    by_offset = jnp.dot(bucket_hits, bias_local, precision=HIGH)
    bias = jnp.where(same_seq[None], toeplitz_rows(by_offset.T, count), NEG)
    scale = HEAD_DIM ** (-0.5)
    scores = (
        jnp.einsum("qhd,khd->hqk", queries, keys_all, preferred_element_type=F32) * scale + bias
    )
    row_max = jnp.max(scores, axis=-1, keepdims=True)
    expo = jnp.exp(scores - row_max)
    p_full = expo / jnp.sum(expo, axis=-1, keepdims=True)
    probs = p_full.astype(BF)
    context = jnp.einsum("hqk,khd->qhd", probs, values_all, preferred_element_type=F32)
    context = context.reshape(count, head_cols).astype(BF)
    attn_part = dot32(context, out_all, NT).astype(BF)
    hidden = x_all + (attn_part.astype(F32) + swap_tensor(attn_part).astype(F32))

    scale_two = rms_scale(hidden)
    n_two = hidden * scale_two
    mixed = n_two * moe_gain
    logits = jnp.stack([jnp.sum(mixed * w_router[:, e], axis=1) for e in range(EXPERTS)], axis=1)
    router_probs = jax.nn.softmax(logits, axis=-1)
    expert_col = expert_ids[:, 0]
    hits = expert_col[:, None] == jnp.arange(EXPERTS, dtype=jnp.int32)[None, :]
    hits_f = hits.astype(F32)
    gate = jnp.sum(router_probs * hits_f, axis=1, keepdims=True)
    hits_i = hits.astype(jnp.int32)
    slot = jnp.sum(jnp.cumsum(hits_i, axis=0) * hits_i, axis=1) - 1
    flat = expert_col * CAP + slot
    dispatch = (flat[:, None] == jnp.arange(EXPERTS * CAP, dtype=jnp.int32)[None, :]).astype(BF)
    grad_routed = (gate * grad_out).astype(BF)
    blocks = dot32(dispatch, mixed.astype(BF), TN).astype(BF)
    grad_blocks = dot32(dispatch, grad_routed, TN).astype(BF)

    def part(x, e):
        return x[e * CAP : (e + 1) * CAP]

    def cols(x, e):
        return x[:, e * units : (e + 1) * units]

    pre = [dot32(part(blocks, e), cols(in_all, e), NN) for e in range(EXPERTS)]
    active = [jax.nn.gelu(v, approximate=True).astype(BF) for v in pre]
    grad_w_down = jnp.concatenate(
        [dot32(part(grad_blocks, e), active[e], TN).astype(BF) for e in range(EXPERTS)], axis=1
    )
    returned = jnp.concatenate(
        [dot32(active[e], cols(down_all, e), NT).astype(BF) for e in range(EXPERTS)], axis=0
    )
    grad_pre = []
    for e in range(EXPERTS):
        grad_active = dot32(part(grad_blocks, e), cols(down_all, e), NN)
        _, pull = jax.vjp(lambda v: jax.nn.gelu(v, approximate=True), pre[e])
        grad_pre.append(pull(grad_active)[0].astype(BF))
    grad_sent = jnp.concatenate(
        [dot32(grad_pre[e], cols(in_all, e), NT).astype(BF) for e in range(EXPERTS)], axis=0
    )
    grad_w_in = jnp.concatenate(
        [dot32(part(blocks, e), grad_pre[e], TN).astype(BF) for e in range(EXPERTS)], axis=1
    )
    routed_part = dot32(dispatch, returned, NN)
    sent_part = dot32(dispatch, grad_sent, NN)
    gate_part = jnp.sum(grad_out * routed_part, axis=1, keepdims=True)
    logits_part = gate_part * gate * (hits_f - router_probs)
    mixed_part = sent_part + sum(
        logits_part[:, e : e + 1] * w_router[:, e] for e in range(EXPERTS)
    )
    mixed_low = mixed_part.astype(BF)
    grad_mixed = mixed_low.astype(F32) + swap_tensor(mixed_low).astype(F32)
    moe_gain_part = jnp.sum(mixed_part * n_two, axis=0)
    router_part = [jnp.sum(mixed * logits_part[:, e : e + 1], axis=0) for e in range(EXPERTS)]

    def own_rows(x):
        return lax.dynamic_slice_in_dim(x, rank * rows_local, rows_local, 0)

    def other_rows(x):
        return lax.dynamic_slice_in_dim(x, (1 - rank) * rows_local, rows_local, 0)

    routed_low = routed_part.astype(BF)
    routed = own_rows(routed_low).astype(F32) + swap_tensor(other_rows(routed_low)).astype(F32)
    result = own_rows(hidden) + own_rows(gate) * routed

    grad_w_down_mine = ring.scatter(grad_w_down, shard)
    grad_w_in_mine = ring.scatter(grad_w_in, shard)

    grad_hidden = grad_out + norm_back(grad_mixed, n_two, scale_two, moe_gain)
    grad_attended = grad_hidden.astype(BF)
    grad_context = dot32(grad_attended, out_all, NN).astype(BF)
    grad_w_out = dot32(grad_attended, context, TN).astype(BF)
    grad_context_heads = grad_context.reshape(count, heads_local, HEAD_DIM)
    grad_probs = jnp.einsum(
        "qhd,khd->hqk", grad_context_heads, values_all, preferred_element_type=F32
    )
    inner = jnp.sum(p_full * grad_probs, axis=-1, keepdims=True)
    grad_scores = (p_full * (grad_probs - inner)).astype(BF)
    grad_queries = (
        jnp.einsum("hqk,khd->qhd", grad_scores, keys_all, preferred_element_type=F32) * scale
    )
    grad_keys = (
        jnp.einsum("hqk,qhd->khd", grad_scores, queries, preferred_element_type=F32) * scale
    )
    grad_values = jnp.einsum(
        "hqk,qhd->khd", probs, grad_context_heads, preferred_element_type=F32
    )
    grad_projected = jnp.concatenate(
        [g.reshape(count, head_cols) for g in (grad_queries, grad_keys, grad_values)], axis=1
    ).astype(BF)
    grad_w_qkv = dot32(normed_one, grad_projected, TN).astype(BF)
    attn_mine = ring.scatter(jnp.concatenate([grad_w_qkv, grad_w_out], axis=1), shard)
    normed_part = dot32(grad_projected, qkv_all, NT)
    attn_gain_part = jnp.sum(normed_part * n_one, axis=0)
    normed_low = normed_part.astype(BF)
    grad_normed = own_rows(normed_low).astype(F32) + swap_tensor(other_rows(normed_low)).astype(F32)
    grad_block = own_rows(grad_hidden) + norm_back(
        grad_normed, own_rows(n_one), own_rows(scale_one), attn_gain
    )
    offset_sums = diagonal_sums(grad_scores.astype(F32))
    grad_bias_heads = jnp.dot(offset_sums, bucket_hits, precision=HIGH)
    grad_rel = lax.dynamic_update_slice_in_dim(
        jnp.zeros(rel_bias.shape, F32), grad_bias_heads.T, rank * heads_local, 1
    )
    small = [attn_gain_part, moe_gain_part] + router_part + [grad_rel.reshape(-1)]
    line = jnp.concatenate(small)
    summed = sum_everywhere(line.reshape(-1, 128)).reshape(-1)
    return (
        result.astype(BF),
        grad_block,
        summed[:width],
        attn_mine[:, : 3 * head_cols].reshape(w_qkv.shape),
        attn_mine[:, 3 * head_cols :],
        summed[4 * width :].reshape(rel_bias.shape),
        summed[width : 2 * width],
        jnp.stack([summed[2 * width : 3 * width], summed[3 * width : 4 * width]], axis=1),
        grad_w_in_mine.reshape(w_in.shape),
        grad_w_down_mine.reshape(w_down.shape),
    )


def solution(mesh):
    placed = (
        P(("dp", "tensor"), None),
        P(),
        P("dp", None, "tensor"),
        P("dp", "tensor"),
        P(),
        P(),
        P(),
        P("dp", None, "tensor"),
        P("dp", None, "tensor"),
        P("dp", None),
        P("dp", None),
        P(),
        P(("dp", "tensor"), None),
    )
    return jax.shard_map(
        body,
        mesh=mesh,
        in_specs=placed,
        out_specs=(
            P(("dp", "tensor"), None),
            P(("dp", "tensor"), None),
            P(),
            P("dp", None, "tensor"),
            P("dp", "tensor"),
            P(),
            P(),
            P(),
            P("dp", None, "tensor"),
            P("dp", None, "tensor"),
        ),
        check_vma=False,
    )
```

```python
import jax
import jax.numpy as jnp
from jax import lax
from jax.experimental import pallas as pl
from jax.experimental.pallas import tpu as pltpu
from jax.sharding import PartitionSpec as P

HEAD_DIM = 64
EXPERTS = 2
CAP = 176

LONGEST = 16

EPS = 1e-06
NEG = -1e30
HIGH = lax.Precision.HIGHEST
BF = jnp.bfloat16
F32 = jnp.float32


def ring_chip(place, chips):
    place = place % chips
    return jnp.where(place < chips // 2, 2 * place, 2 * (chips - 1 - place) + 1)


def ring_place(chip, chips):
    return jnp.where(chip % 2 == 0, chip // 2, chips - 1 - chip // 2)


class Ring:
    def __init__(self):
        self.n = lax.axis_size("dp")
        self.chips = self.n // 2
        order = [2 * i for i in range(self.chips // 2)]
        order = order + [c + 1 for c in reversed(order)]
        pairs = [
            (order[i] * 2 + k, order[(i + 1) % self.chips] * 2 + k)
            for i in range(self.chips)
            for k in (0, 1)
        ]
        self.right = pairs
        self.left = [(b, a) for a, b in pairs]
        self.swap = [(i, i ^ 1) for i in range(self.n)]
        index = lax.axis_index("dp")
        self.core = index % 2
        self.place = ring_place(index // 2, self.chips)
        reach = self.chips // 2
        self.distances = [0] + [d for s in range(1, reach) for d in (-s, s)] + [reach]

    def chip_at(self, distance):
        return ring_chip(self.place + distance + self.chips, self.chips)

    def gather(self, x):
        rows, width = x.shape
        if self.chips > LONGEST:
            return lax.all_gather(x, "dp", axis=0, tiled=True)
        reach = self.chips // 2
        r = l = x
        pieces = [x]
        for _ in range(reach - 1):
            r = lax.ppermute(r, "dp", self.right)
            l = lax.ppermute(l, "dp", self.left)
            pieces += [r, l]
        half = width // 2
        main = jnp.concatenate(pieces, axis=0)
        main_sib = lax.ppermute(main, "dp", self.swap)
        r = lax.ppermute(r[:, :half], "dp", self.right)
        l = lax.ppermute(l[:, half:], "dp", self.left)
        tail = jnp.concatenate([r, l], axis=1)
        tail_sib = lax.ppermute(tail, "dp", self.swap)
        chips = jnp.stack([self.chip_at(d) for d in self.distances])
        own = chips * 2 + self.core
        sib = chips * 2 + 1 - self.core
        return assemble(main, tail, main_sib, tail_sib, jnp.concatenate([own, sib]))

    def scatter(self, grads, rows):
        width = grads.shape[1]
        if self.chips > LONGEST:
            return lax.psum_scatter(grads, "dp", scatter_dimension=0, tiled=True).astype(F32)
        reach = self.chips // 2
        half = width // 2
        split = grads.reshape(self.chips, 2, rows, width)
        other = lax.dynamic_index_in_dim(split, 1 - self.core, 1, keepdims=False)
        mine = lax.dynamic_index_in_dim(split, self.core, 1, keepdims=False)
        got = lax.ppermute(other, "dp", self.swap)
        both = (mine.astype(F32) + got.astype(F32)).astype(BF)

        def local(distance):
            return lax.dynamic_index_in_dim(both, self.chip_at(distance), 0, keepdims=False)

        far = local(reach)
        r = lax.ppermute(far[:, :half], "dp", self.right)
        l = lax.ppermute(far[:, half:], "dp", self.left)
        for s in range(reach - 1, 0, -1):
            near_r, near_l = local(s), local(-s)
            if s == reach - 1:
                r = jnp.concatenate([add_low(r, near_r[:, :half]), near_r[:, half:]], axis=1)
                l = jnp.concatenate([near_l[:, :half], add_low(l, near_l[:, half:])], axis=1)
            else:
                r, l = add_low(r, near_r), add_low(l, near_l)
            r = lax.ppermute(r, "dp", self.right)
            l = lax.ppermute(l, "dp", self.left)
        return local(0).astype(F32) + r.astype(F32) + l.astype(F32)


def add_low(a, b):
    return (a.astype(F32) + b.astype(F32)).astype(BF)


def assemble(main, tail, main_sib, tail_sib, owners):
    rows, width = tail.shape
    chips = main.shape[0] // rows + 1
    if rows % 16:
        own = jnp.concatenate([main, tail]).reshape(chips, rows, width)
        sib = jnp.concatenate([main_sib, tail_sib]).reshape(chips, rows, width)
        out = jnp.zeros((2 * chips, rows, width), main.dtype).at[owners].set(
            jnp.concatenate([own, sib])
        )
        return out.reshape(2 * chips * rows, width)

    def kernel(owners_ref, main_ref, tail_ref, main_sib_ref, tail_sib_ref, out_ref):
        for at, (big, small) in enumerate(((main_ref, tail_ref), (main_sib_ref, tail_sib_ref))):
            for i in range(chips):
                owner = owners_ref[at * chips + i]
                target = pl.ds(pl.multiple_of(owner * rows, 16), rows)
                if i == chips - 1:
                    out_ref[target, :] = small[...]
                else:
                    out_ref[target, :] = big[pl.ds(i * rows, rows), :]

    inside = pl.BlockSpec(memory_space=pltpu.VMEM)
    return pl.pallas_call(
        kernel,
        out_shape=jax.ShapeDtypeStruct((2 * chips * rows, width), main.dtype),
        in_specs=[pl.BlockSpec(memory_space=pltpu.SMEM)] + [inside] * 4,
        out_specs=inside,
        compiler_params=pltpu.CompilerParams(vmem_limit_bytes=32 << 20),
        cost_estimate=pl.CostEstimate(
            flops=0, bytes_accessed=8 * chips * rows * width, transcendentals=0
        ),
        name="assemble",
    )(owners, main, tail, main_sib, tail_sib)


def swap_tensor(x):
    return lax.ppermute(x, "tensor", [(0, 1), (1, 0)])


def whole_rows(own, other, rank):
    return jnp.where(
        rank == 0, jnp.concatenate([own, other], axis=0), jnp.concatenate([other, own], axis=0)
    )


def sum_everywhere(x):
    x = x + swap_tensor(x)
    step = 1
    while step < lax.axis_size("dp"):
        x = x + lax.ppermute(x, "dp", [(i, i ^ step) for i in range(lax.axis_size("dp"))])
        step *= 2
    return x


def rms_scale(rows):
    return lax.rsqrt(jnp.mean(rows * rows, axis=-1, keepdims=True) + EPS)


def norm_back(grad, normed, scale, gain):
    weighted = grad * gain
    return scale * (weighted - normed * jnp.mean(weighted * normed, axis=-1, keepdims=True))


def dot32(a, b, dims):
    return lax.dot_general(a, b, (dims, ((), ())), preferred_element_type=F32)


NN = ((1,), (0,))
NT = ((1,), (1,))
TN = ((0,), (0,))


VMEM_BYTES = 48 << 20


def attention_forward(x, gain, weights, by_offset, seq_col, seq_row):
    count, d = x.shape
    head_cols = weights.shape[1] // 4
    heads = head_cols // HEAD_DIM
    scale = HEAD_DIM ** (-0.5)
    lanes = by_offset.shape[1]

    def kernel(x_ref, gain_ref, w_ref, off_ref, col_ref, row_ref, *outs):
        normed_ref, scale_ref, proj_ref, p_ref, context_ref, part_ref = outs
        rows = x_ref[...].astype(F32)
        r = lax.rsqrt(jnp.mean(rows * rows, axis=-1, keepdims=True) + EPS)
        scale_ref[...] = r
        normed = (rows * r * gain_ref[...]).astype(BF)
        normed_ref[...] = normed
        for s in range(3):
            at = pl.ds(s * head_cols, head_cols)
            proj_ref[:, at] = dot32(normed, w_ref[:, at], NN).astype(BF)
        same = col_ref[...] == row_ref[...]
        for h in range(heads):
            q = proj_ref[:, pl.ds(h * HEAD_DIM, HEAD_DIM)]
            k = proj_ref[:, pl.ds(head_cols + h * HEAD_DIM, HEAD_DIM)]
            v = proj_ref[:, pl.ds(2 * head_cols + h * HEAD_DIM, HEAD_DIM)]
            line = jnp.broadcast_to(off_ref[pl.ds(h, 1), :], (count, lanes))
            bias = pltpu.roll(line, lanes - (count - 1), 1, stride=1, stride_axis=0)[:, :count]
            scores = jnp.where(same, dot32(q, k, NT) * scale + bias, NEG)
            expo = jnp.exp(scores - jnp.max(scores, axis=-1, keepdims=True))
            p = expo / jnp.sum(expo, axis=-1, keepdims=True)
            p_ref[h] = p
            context_ref[:, pl.ds(h * HEAD_DIM, HEAD_DIM)] = dot32(p.astype(BF), v, NN).astype(BF)
        out_w = w_ref[:, pl.ds(3 * head_cols, head_cols)]
        part_ref[...] = dot32(context_ref[...], out_w, NT).astype(BF)

    inside = pl.BlockSpec(memory_space=pltpu.VMEM)
    return pl.pallas_call(
        kernel,
        out_shape=(
            jax.ShapeDtypeStruct((count, d), BF),
            jax.ShapeDtypeStruct((count, 1), F32),
            jax.ShapeDtypeStruct((count, 3 * head_cols), BF),
            jax.ShapeDtypeStruct((heads, count, count), F32),
            jax.ShapeDtypeStruct((count, head_cols), BF),
            jax.ShapeDtypeStruct((count, d), BF),
        ),
        in_specs=[inside] * 6,
        out_specs=(inside,) * 6,
        compiler_params=pltpu.CompilerParams(vmem_limit_bytes=VMEM_BYTES),
        cost_estimate=pl.CostEstimate(
            flops=8 * count * d * head_cols + 4 * heads * count * count * HEAD_DIM,
            bytes_accessed=2 * d * 4 * head_cols + 4 * heads * count * count + 8 * count * d,
            transcendentals=heads * count * count,
        ),
        name="attention_forward",
    )(x, gain, weights, by_offset, seq_col, seq_row)


def attention_backward(grad, weights, proj, p_full, context, lanes):
    count, d = grad.shape
    head_cols = weights.shape[1] // 4
    heads = head_cols // HEAD_DIM
    scale = HEAD_DIM ** (-0.5)

    def kernel(grad_ref, w_ref, proj_ref, p_ref, out_ref, sums_ref, gc_ref):
        out_w = w_ref[:, pl.ds(3 * head_cols, head_cols)]
        gc_ref[...] = dot32(grad_ref[...], out_w, NN).astype(BF)
        down = lax.broadcasted_iota(jnp.int32, (count, count), 0)
        across = lax.broadcasted_iota(jnp.int32, (count, count), 1)
        flip = (down + across == count - 1).astype(F32).astype(BF)
        for h in range(heads):
            at = [pl.ds(s * head_cols + h * HEAD_DIM, HEAD_DIM) for s in range(3)]
            q, k, v = proj_ref[:, at[0]], proj_ref[:, at[1]], proj_ref[:, at[2]]
            p = p_ref[h]
            gc = gc_ref[:, at[0]]
            dp = dot32(gc, v, NT)
            ds = (p * (dp - jnp.sum(p * dp, axis=-1, keepdims=True))).astype(BF)
            out_ref[:, at[0]] = (dot32(ds, k, NN) * scale).astype(BF)
            out_ref[:, at[1]] = (dot32(ds, q, TN) * scale).astype(BF)
            out_ref[:, at[2]] = dot32(p.astype(BF), gc, TN).astype(BF)
            turned = dot32(ds, flip, TN)
            wide = jnp.concatenate([turned, jnp.zeros((count, lanes - count), F32)], axis=1)
            rolled = pltpu.roll(wide, 0, 1, stride=1, stride_axis=0)
            sums_ref[pl.ds(h, 1), :] = jnp.sum(rolled, axis=0, keepdims=True)

    inside = pl.BlockSpec(memory_space=pltpu.VMEM)
    return pl.pallas_call(
        kernel,
        out_shape=(
            jax.ShapeDtypeStruct((count, 3 * head_cols), BF),
            jax.ShapeDtypeStruct((heads, lanes), F32),
        ),
        in_specs=[inside] * 4,
        out_specs=(inside,) * 2,
        scratch_shapes=[pltpu.VMEM((count, head_cols), BF)],
        compiler_params=pltpu.CompilerParams(vmem_limit_bytes=VMEM_BYTES),
        cost_estimate=pl.CostEstimate(
            flops=2 * count * d * head_cols + 12 * heads * count * count * HEAD_DIM,
            bytes_accessed=4 * heads * count * count + 8 * count * d,
            transcendentals=0,
        ),
        name="attention_backward",
    )(grad, weights, proj, p_full)


def body(
    block_in,
    attn_gain,
    w_qkv,
    w_out,
    rel_bias,
    moe_gain,
    w_router,
    w_in,
    w_down,
    seq_lengths,
    expert_ids,
    rel_table,
    out_grad,
):
    rows_local, width = block_in.shape
    rank = lax.axis_index("tensor")
    ring = Ring()
    shard = w_out.shape[0]
    head_cols = w_out.shape[1]
    units = w_in.shape[2]
    heads_local = head_cols // HEAD_DIM
    count = 2 * rows_local

    attn_shard = jnp.concatenate([w_qkv.reshape(shard, 3 * head_cols), w_out], axis=1)
    x_low = whole_rows(block_in, swap_tensor(block_in), rank)
    x_all = x_low.astype(F32)
    attn_all = ring.gather(attn_shard)
    in_all = ring.gather(w_in.reshape(shard, EXPERTS * units))
    down_all = ring.gather(w_down.reshape(shard, EXPERTS * units))
    grad_out = whole_rows(out_grad, swap_tensor(out_grad), rank).astype(F32)

    places = jnp.arange(count, dtype=jnp.int32)
    ends = jnp.cumsum(seq_lengths[0])
    seq_ids = jnp.sum((places[:, None] >= ends[None, :]).astype(jnp.int32), axis=1)
    bias_local = lax.dynamic_slice_in_dim(rel_bias, rank * heads_local, heads_local, 1)
    bucket_hits = (
        rel_table[:, None] == jnp.arange(rel_bias.shape[0], dtype=jnp.int32)[None, :]
    ).astype(F32)
    by_offset = jnp.dot(bucket_hits, bias_local, precision=HIGH)
    lanes = 2 * count
    by_offset = jnp.pad(by_offset.T, ((0, 0), (0, lanes - by_offset.shape[0])))
    normed_one, scale_one, projected, p_full, context, attn_part = attention_forward(
        x_low, attn_gain[None, :], attn_all, by_offset, seq_ids[:, None], seq_ids[None, :]
    )
    n_one = x_all * scale_one
    hidden = x_all + (attn_part.astype(F32) + swap_tensor(attn_part).astype(F32))

    scale_two = rms_scale(hidden)
    n_two = hidden * scale_two
    mixed = n_two * moe_gain
    logits = jnp.stack([jnp.sum(mixed * w_router[:, e], axis=1) for e in range(EXPERTS)], axis=1)
    router_probs = jax.nn.softmax(logits, axis=-1)
    expert_col = expert_ids[:, 0]
    hits = expert_col[:, None] == jnp.arange(EXPERTS, dtype=jnp.int32)[None, :]
    hits_f = hits.astype(F32)
    gate = jnp.sum(router_probs * hits_f, axis=1, keepdims=True)
    hits_i = hits.astype(jnp.int32)
    slot = jnp.sum(jnp.cumsum(hits_i, axis=0) * hits_i, axis=1) - 1
    flat = expert_col * CAP + slot
    dispatch = (flat[:, None] == jnp.arange(EXPERTS * CAP, dtype=jnp.int32)[None, :]).astype(BF)
    grad_routed = (gate * grad_out).astype(BF)
    blocks = dot32(dispatch, mixed.astype(BF), TN).astype(BF)
    grad_blocks = dot32(dispatch, grad_routed, TN).astype(BF)

    def part(x, e):
        return x[e * CAP : (e + 1) * CAP]

    def cols(x, e):
        return x[:, e * units : (e + 1) * units]

    pre = [dot32(part(blocks, e), cols(in_all, e), NN) for e in range(EXPERTS)]
    active = [jax.nn.gelu(v, approximate=True).astype(BF) for v in pre]
    grad_w_down = jnp.concatenate(
        [dot32(part(grad_blocks, e), active[e], TN).astype(BF) for e in range(EXPERTS)], axis=1
    )
    returned = jnp.concatenate(
        [dot32(active[e], cols(down_all, e), NT).astype(BF) for e in range(EXPERTS)], axis=0
    )
    grad_pre = []
    for e in range(EXPERTS):
        grad_active = dot32(part(grad_blocks, e), cols(down_all, e), NN)
        _, pull = jax.vjp(lambda v: jax.nn.gelu(v, approximate=True), pre[e])
        grad_pre.append(pull(grad_active)[0].astype(BF))
    grad_sent = jnp.concatenate(
        [dot32(grad_pre[e], cols(in_all, e), NT).astype(BF) for e in range(EXPERTS)], axis=0
    )
    grad_w_in = jnp.concatenate(
        [dot32(part(blocks, e), grad_pre[e], TN).astype(BF) for e in range(EXPERTS)], axis=1
    )
    routed_part = dot32(dispatch, returned, NN)
    sent_part = dot32(dispatch, grad_sent, NN)
    gate_part = jnp.sum(grad_out * routed_part, axis=1, keepdims=True)
    logits_part = gate_part * gate * (hits_f - router_probs)
    mixed_part = sent_part + sum(
        logits_part[:, e : e + 1] * w_router[:, e] for e in range(EXPERTS)
    )
    mixed_low = mixed_part.astype(BF)
    grad_mixed = mixed_low.astype(F32) + swap_tensor(mixed_low).astype(F32)
    moe_gain_part = jnp.sum(mixed_part * n_two, axis=0)
    router_part = [jnp.sum(mixed * logits_part[:, e : e + 1], axis=0) for e in range(EXPERTS)]

    def own_rows(x):
        return lax.dynamic_slice_in_dim(x, rank * rows_local, rows_local, 0)

    def other_rows(x):
        return lax.dynamic_slice_in_dim(x, (1 - rank) * rows_local, rows_local, 0)

    routed_low = routed_part.astype(BF)
    routed = own_rows(routed_low).astype(F32) + swap_tensor(other_rows(routed_low)).astype(F32)
    result = own_rows(hidden) + own_rows(gate) * routed

    grad_w_down_mine = ring.scatter(grad_w_down, shard)
    grad_w_in_mine = ring.scatter(grad_w_in, shard)

    grad_hidden = grad_out + norm_back(grad_mixed, n_two, scale_two, moe_gain)
    grad_attended = grad_hidden.astype(BF)
    grad_projected, offset_sums = attention_backward(
        grad_attended, attn_all, projected, p_full, context, lanes
    )
    grad_w_out = dot32(grad_attended, context, TN).astype(BF)
    grad_w_qkv = dot32(normed_one, grad_projected, TN).astype(BF)
    attn_mine = ring.scatter(jnp.concatenate([grad_w_qkv, grad_w_out], axis=1), shard)
    normed_part = dot32(grad_projected, attn_all[:, : 3 * head_cols], NT)
    attn_gain_part = jnp.sum(normed_part * n_one, axis=0)
    normed_low = normed_part.astype(BF)
    grad_normed = own_rows(normed_low).astype(F32) + swap_tensor(other_rows(normed_low)).astype(F32)
    grad_block = own_rows(grad_hidden) + norm_back(
        grad_normed, own_rows(n_one), own_rows(scale_one), attn_gain
    )
    grad_bias_heads = jnp.dot(offset_sums[:, : rel_table.shape[0]], bucket_hits, precision=HIGH)
    grad_rel = lax.dynamic_update_slice_in_dim(
        jnp.zeros(rel_bias.shape, F32), grad_bias_heads.T, rank * heads_local, 1
    )
    small = [attn_gain_part, moe_gain_part] + router_part + [grad_rel.reshape(-1)]
    line = jnp.concatenate(small)
    summed = sum_everywhere(line.reshape(-1, 128)).reshape(-1)
    return (
        result.astype(BF),
        grad_block,
        summed[:width],
        attn_mine[:, : 3 * head_cols].reshape(w_qkv.shape),
        attn_mine[:, 3 * head_cols :],
        summed[4 * width :].reshape(rel_bias.shape),
        summed[width : 2 * width],
        jnp.stack([summed[2 * width : 3 * width], summed[3 * width : 4 * width]], axis=1),
        grad_w_in_mine.reshape(w_in.shape),
        grad_w_down_mine.reshape(w_down.shape),
    )


def solution(mesh):
    placed = (
        P(("dp", "tensor"), None),
        P(),
        P("dp", None, "tensor"),
        P("dp", "tensor"),
        P(),
        P(),
        P(),
        P("dp", None, "tensor"),
        P("dp", None, "tensor"),
        P("dp", None),
        P("dp", None),
        P(),
        P(("dp", "tensor"), None),
    )
    return jax.shard_map(
        body,
        mesh=mesh,
        in_specs=placed,
        out_specs=(
            P(("dp", "tensor"), None),
            P(("dp", "tensor"), None),
            P(),
            P("dp", None, "tensor"),
            P("dp", "tensor"),
            P(),
            P(),
            P(),
            P("dp", None, "tensor"),
            P("dp", None, "tensor"),
        ),
        check_vma=False,
    )
```

```python
import jax
import jax.numpy as jnp
from jax import lax
from jax.experimental import pallas as pl
from jax.experimental.pallas import tpu as pltpu
from jax.sharding import PartitionSpec as P

HEAD_DIM = 64
EXPERTS = 2
CAP = 176

LONGEST = 16

EPS = 1e-06
NEG = -1e30
VMEM_BYTES = 48 << 20
HIGH = lax.Precision.HIGHEST
BF = jnp.bfloat16
F32 = jnp.float32


def ring_chip(place, chips):
    place = place % chips
    return jnp.where(place < chips // 2, 2 * place, 2 * (chips - 1 - place) + 1)


def ring_place(chip, chips):
    return jnp.where(chip % 2 == 0, chip // 2, chips - 1 - chip // 2)


class Ring:
    def __init__(self):
        self.n = lax.axis_size("dp")
        self.chips = self.n // 2
        order = [2 * i for i in range(self.chips // 2)]
        order = order + [c + 1 for c in reversed(order)]
        pairs = [
            (order[i] * 2 + k, order[(i + 1) % self.chips] * 2 + k)
            for i in range(self.chips)
            for k in (0, 1)
        ]
        self.right = pairs
        self.left = [(b, a) for a, b in pairs]
        self.swap = [(i, i ^ 1) for i in range(self.n)]
        index = lax.axis_index("dp")
        self.core = index % 2
        self.long = self.chips > LONGEST
        self.place = ring_place(index // 2, self.chips)
        reach = self.chips // 2
        self.distances = [0] + [d for s in range(1, reach) for d in (-s, s)] + [reach]

    def other_core(self, x):
        return lax.ppermute(x, "dp", self.swap)

    def by_core(self, own, other, axis):
        return jnp.where(
            self.core == 0,
            jnp.concatenate([own, other], axis=axis),
            jnp.concatenate([other, own], axis=axis),
        )

    def chip_at(self, distance):
        return ring_chip(self.place + distance + self.chips, self.chips)


class Gather:
    def __init__(self, ring, shard, far):
        self.ring, self.shard, self.far = ring, shard, far
        self.reach = ring.chips // 2
        self.pieces = [shard]
        self.sent = (shard, shard)
        self.steps = 0

    def step(self, *deps):
        ring = self.ring
        if ring.long or self.steps == self.reach:
            return ()
        self.steps += 1
        r, l = after(self.sent, deps)
        if self.steps < self.reach:
            self.sent = (lax.ppermute(r, "dp", ring.right), lax.ppermute(l, "dp", ring.left))
        elif self.far == "right":
            self.sent = (lax.ppermute(r, "dp", ring.right),)
        else:
            self.sent = (lax.ppermute(l, "dp", ring.left),)
        self.pieces += self.sent
        return self.sent

    def whole(self):
        return assemble(self.pieces, jnp.stack([self.ring.chip_at(d) for d in self.ring.distances]))


class Scatter:
    def __init__(self, ring, pairs, rows, far, both_cores):
        self.ring, self.rows, self.far = ring, rows, far
        self.reach = ring.chips // 2
        self.steps = 0
        if ring.long:
            terms = [dot32(lhs, rhs, TN).astype(BF) for lhs, rhs in pairs]
            self.grads = jnp.concatenate(terms, axis=1)
            return
        near = [d for s in range(self.reach - 1, 0, -1) for d in (s, -s)]
        self.slots = [self.reach] + near + [0]
        chips = jnp.stack([ring.chip_at(d) for d in self.slots])
        if both_cores:
            self.cuts = []
            (self.mine,) = outer(pairs, chips, rows, [ring.chips])
        else:
            self.cuts = [3, ring.chips] if ring.chips > 4 else [ring.chips]
            owners = jnp.concatenate([chips * 2 + ring.core, chips * 2 + 1 - ring.core])
            sizes = [y - x for x, y in zip([0] + self.cuts[:-1], self.cuts)]
            self.mine, *sib = outer(pairs, owners, rows, [ring.chips] + sizes)
            self.got = [lax.ppermute(part, "dp", ring.swap) for part in sib]

    def local(self, distance):
        slot = self.slots.index(distance)
        term = self.mine[slot * self.rows : (slot + 1) * self.rows].astype(F32)
        if self.cuts:
            part = next(i for i, cut in enumerate(self.cuts) if slot < cut)
            begin = slot - (self.cuts[part - 1] if part else 0)
            got = self.got[part][begin * self.rows : (begin + 1) * self.rows]
            term = term + got.astype(F32)
        return term

    def step(self, *deps):
        ring = self.ring
        if ring.long or self.steps == self.reach:
            return ()
        distance = self.reach - self.steps
        self.steps += 1
        if distance == self.reach:
            (far,) = after((self.local(distance).astype(BF),), deps)
            way = ring.right if self.far == "right" else ring.left
            self.sent = (lax.ppermute(far, "dp", way),)
            return self.sent
        r, l = self.local(distance), self.local(-distance)
        if distance < self.reach - 1:
            r, l = r + self.sent[0].astype(F32), l + self.sent[1].astype(F32)
        elif self.far == "right":
            r = r + self.sent[0].astype(F32)
        else:
            l = l + self.sent[0].astype(F32)
        r, l = after((r.astype(BF), l.astype(BF)), deps)
        self.sent = (lax.ppermute(r, "dp", ring.right), lax.ppermute(l, "dp", ring.left))
        return self.sent

    def total(self):
        r, l = self.sent
        return self.local(0) + r.astype(F32) + l.astype(F32)


def outer(pairs, owners, rows, counts):
    height = pairs[0][0].shape[1]
    widths = [rhs.shape[1] for _, rhs in pairs]
    width = sum(widths)
    tile = 768

    def kernel(owners_ref, *refs):
        ins, outs, held_ref = refs[: 2 * len(pairs)], refs[2 * len(pairs) : -1], refs[-1]
        at = 0
        for i, wide in enumerate(widths):
            lhs = ins[2 * i][...]
            for start in range(0, wide, tile):
                size = min(tile, wide - start)
                held_ref[:, pl.ds(at, size)] = dot32(
                    lhs, ins[2 * i + 1][:, pl.ds(start, size)], TN
                ).astype(BF)
                at += size
        slot = 0
        for ref, number in zip(outs, counts):
            for to in range(number):
                source = pl.multiple_of(owners_ref[slot] * rows, 16)
                ref[pl.ds(to * rows, rows), :] = held_ref[pl.ds(source, rows), :]
                slot += 1

    inside = pl.BlockSpec(memory_space=pltpu.VMEM)
    return pl.pallas_call(
        kernel,
        out_shape=[jax.ShapeDtypeStruct((number * rows, width), BF) for number in counts],
        in_specs=[pl.BlockSpec(memory_space=pltpu.SMEM)] + [inside] * (2 * len(pairs)),
        out_specs=[inside] * len(counts),
        scratch_shapes=[pltpu.VMEM((height, width), BF)],
        compiler_params=pltpu.CompilerParams(vmem_limit_bytes=VMEM_BYTES),
        cost_estimate=pl.CostEstimate(
            flops=sum(2 * lhs.shape[0] * height * rhs.shape[1] for lhs, rhs in pairs),
            bytes_accessed=4 * height * width,
            transcendentals=0,
        ),
        name="outer",
    )(owners, *[x for pair in pairs for x in pair])


def after(values, deps):
    if not deps:
        return values
    return lax.optimization_barrier((tuple(values), deps))[0]


def assemble(pieces, owners):
    rows, width = pieces[0].shape
    number = len(pieces)

    def kernel(owners_ref, *refs):
        ins, out_ref, sems = refs[:number], refs[number], refs[number + 1]
        copies = []
        for i in range(number):
            target = out_ref.at[pl.ds(pl.multiple_of(owners_ref[i] * rows, 16), rows)]
            copies.append(pltpu.make_async_copy(ins[i], target, sems.at[i]))
        for copy in copies:
            copy.start()
        for copy in copies:
            copy.wait()

    return pl.pallas_call(
        kernel,
        out_shape=jax.ShapeDtypeStruct((number * rows, width), BF),
        in_specs=[pl.BlockSpec(memory_space=pltpu.SMEM)]
        + [pl.BlockSpec(memory_space=pl.ANY)] * number,
        out_specs=pl.BlockSpec(memory_space=pltpu.VMEM),
        scratch_shapes=[pltpu.SemaphoreType.DMA((number,))],
        compiler_params=pltpu.CompilerParams(vmem_limit_bytes=VMEM_BYTES),
        cost_estimate=pl.CostEstimate(
            flops=0, bytes_accessed=4 * number * rows * width, transcendentals=0
        ),
        name="assemble",
    )(owners, *pieces)


def interleave(own, other, core, rows):
    chips, width = own.shape[0] // rows, own.shape[1]

    def kernel(core_ref, own_ref, other_ref, out_ref):
        for k, ref in enumerate((own_ref, other_ref)):
            first = (1 - core_ref[0]) if k else core_ref[0]
            for chip in range(chips):
                target = pl.multiple_of((2 * chip + first) * rows, 16)
                out_ref[pl.ds(target, rows), :] = ref[pl.ds(chip * rows, rows), :]

    inside = pl.BlockSpec(memory_space=pltpu.VMEM)
    return pl.pallas_call(
        kernel,
        out_shape=jax.ShapeDtypeStruct((2 * chips * rows, width), BF),
        in_specs=[pl.BlockSpec(memory_space=pltpu.SMEM), inside, inside],
        out_specs=inside,
        compiler_params=pltpu.CompilerParams(vmem_limit_bytes=VMEM_BYTES),
        cost_estimate=pl.CostEstimate(
            flops=0, bytes_accessed=8 * chips * rows * width, transcendentals=0
        ),
        name="interleave",
    )(core[None], own, other)


def swap_tensor(x):
    return lax.ppermute(x, "tensor", [(0, 1), (1, 0)])


def whole_rows(own, other, rank):
    return jnp.where(
        rank == 0, jnp.concatenate([own, other], axis=0), jnp.concatenate([other, own], axis=0)
    )


def sum_everywhere(x):
    x = x + swap_tensor(x)
    step = 1
    while step < lax.axis_size("dp"):
        x = x + lax.ppermute(x, "dp", [(i, i ^ step) for i in range(lax.axis_size("dp"))])
        step *= 2
    return x


def rms_scale(rows):
    return lax.rsqrt(jnp.mean(rows * rows, axis=-1, keepdims=True) + EPS)


def norm_back(grad, normed, scale, gain):
    weighted = grad * gain
    return scale * (weighted - normed * jnp.mean(weighted * normed, axis=-1, keepdims=True))


def dot32(a, b, dims):
    return lax.dot_general(a, b, (dims, ((), ())), preferred_element_type=F32)


NN = ((1,), (0,))
NT = ((1,), (1,))
TN = ((0,), (0,))


def attention_forward(x, gain, weights, by_offset, seq_col, seq_row):
    count, d = x.shape
    head_cols = weights.shape[1] // 4
    heads = head_cols // HEAD_DIM
    scale = HEAD_DIM ** (-0.5)
    lanes = by_offset.shape[1]

    def kernel(x_ref, gain_ref, w_ref, off_ref, col_ref, row_ref, *outs):
        normed_ref, scale_ref, proj_ref, p_ref, context_ref, part_ref = outs
        rows = x_ref[...].astype(F32)
        r = lax.rsqrt(jnp.mean(rows * rows, axis=-1, keepdims=True) + EPS)
        scale_ref[...] = r
        normed = (rows * r * gain_ref[...]).astype(BF)
        normed_ref[...] = normed
        for s in range(3):
            at = pl.ds(s * head_cols, head_cols)
            proj_ref[:, at] = dot32(normed, w_ref[:, at], NN).astype(BF)
        same = col_ref[...] == row_ref[...]
        for h in range(heads):
            q = proj_ref[:, pl.ds(h * HEAD_DIM, HEAD_DIM)]
            k = proj_ref[:, pl.ds(head_cols + h * HEAD_DIM, HEAD_DIM)]
            v = proj_ref[:, pl.ds(2 * head_cols + h * HEAD_DIM, HEAD_DIM)]
            line = jnp.broadcast_to(off_ref[pl.ds(h, 1), :], (count, lanes))
            bias = pltpu.roll(line, lanes - (count - 1), 1, stride=1, stride_axis=0)[:, :count]
            scores = jnp.where(same, dot32(q, k, NT) * scale + bias, NEG)
            expo = jnp.exp(scores - jnp.max(scores, axis=-1, keepdims=True))
            p = expo / jnp.sum(expo, axis=-1, keepdims=True)
            p_ref[h] = p
            context_ref[:, pl.ds(h * HEAD_DIM, HEAD_DIM)] = dot32(p.astype(BF), v, NN).astype(BF)
        out_w = w_ref[:, pl.ds(3 * head_cols, head_cols)]
        part_ref[...] = dot32(context_ref[...], out_w, NT).astype(BF)

    inside = pl.BlockSpec(memory_space=pltpu.VMEM)
    return pl.pallas_call(
        kernel,
        out_shape=(
            jax.ShapeDtypeStruct((count, d), BF),
            jax.ShapeDtypeStruct((count, 1), F32),
            jax.ShapeDtypeStruct((count, 3 * head_cols), BF),
            jax.ShapeDtypeStruct((heads, count, count), F32),
            jax.ShapeDtypeStruct((count, head_cols), BF),
            jax.ShapeDtypeStruct((count, d), BF),
        ),
        in_specs=[inside] * 6,
        out_specs=(inside,) * 6,
        compiler_params=pltpu.CompilerParams(vmem_limit_bytes=VMEM_BYTES),
        cost_estimate=pl.CostEstimate(
            flops=8 * count * d * head_cols + 4 * heads * count * count * HEAD_DIM,
            bytes_accessed=2 * d * 4 * head_cols + 4 * heads * count * count + 8 * count * d,
            transcendentals=heads * count * count,
        ),
        name="attention_forward",
    )(x, gain, weights, by_offset, seq_col, seq_row)


def attention_backward(grad, weights, proj, p_full, context, lanes):
    count, d = grad.shape
    head_cols = weights.shape[1] // 4
    heads = head_cols // HEAD_DIM
    scale = HEAD_DIM ** (-0.5)

    def kernel(grad_ref, w_ref, proj_ref, p_ref, out_ref, sums_ref, gc_ref):
        out_w = w_ref[:, pl.ds(3 * head_cols, head_cols)]
        gc_ref[...] = dot32(grad_ref[...], out_w, NN).astype(BF)
        down = lax.broadcasted_iota(jnp.int32, (count, count), 0)
        across = lax.broadcasted_iota(jnp.int32, (count, count), 1)
        flip = (down + across == count - 1).astype(F32).astype(BF)
        for h in range(heads):
            at = [pl.ds(s * head_cols + h * HEAD_DIM, HEAD_DIM) for s in range(3)]
            q, k, v = proj_ref[:, at[0]], proj_ref[:, at[1]], proj_ref[:, at[2]]
            p = p_ref[h]
            gc = gc_ref[:, at[0]]
            dp = dot32(gc, v, NT)
            ds = (p * (dp - jnp.sum(p * dp, axis=-1, keepdims=True))).astype(BF)
            out_ref[:, at[0]] = (dot32(ds, k, NN) * scale).astype(BF)
            out_ref[:, at[1]] = (dot32(ds, q, TN) * scale).astype(BF)
            out_ref[:, at[2]] = dot32(p.astype(BF), gc, TN).astype(BF)
            turned = dot32(ds, flip, TN)
            wide = jnp.concatenate([turned, jnp.zeros((count, lanes - count), F32)], axis=1)
            rolled = pltpu.roll(wide, 0, 1, stride=1, stride_axis=0)
            sums_ref[pl.ds(h, 1), :] = jnp.sum(rolled, axis=0, keepdims=True)

    inside = pl.BlockSpec(memory_space=pltpu.VMEM)
    return pl.pallas_call(
        kernel,
        out_shape=(
            jax.ShapeDtypeStruct((count, 3 * head_cols), BF),
            jax.ShapeDtypeStruct((heads, lanes), F32),
        ),
        in_specs=[inside] * 4,
        out_specs=(inside,) * 2,
        scratch_shapes=[pltpu.VMEM((count, head_cols), BF)],
        compiler_params=pltpu.CompilerParams(vmem_limit_bytes=VMEM_BYTES),
        cost_estimate=pl.CostEstimate(
            flops=2 * count * d * head_cols + 12 * heads * count * count * HEAD_DIM,
            bytes_accessed=4 * heads * count * count + 8 * count * d,
            transcendentals=0,
        ),
        name="attention_backward",
    )(grad, weights, proj, p_full)


def body(
    block_in,
    attn_gain,
    w_qkv,
    w_out,
    rel_bias,
    moe_gain,
    w_router,
    w_in,
    w_down,
    seq_lengths,
    expert_ids,
    rel_table,
    out_grad,
):
    rows_local, width = block_in.shape
    rank = lax.axis_index("tensor")
    ring = Ring()
    shard = w_out.shape[0]
    head_cols = w_out.shape[1]
    units = w_in.shape[2]
    heads_local = head_cols // HEAD_DIM
    count = 2 * rows_local

    attn_shard = jnp.concatenate([w_qkv.reshape(shard, 3 * head_cols), w_out], axis=1)
    x_other = swap_tensor(block_in)
    split = units // 2

    def unit_half(w, core):
        return lax.dynamic_slice_in_dim(w, core * split, split, axis=2)

    def unit_shard(w, got):
        own = unit_half(w, ring.core).reshape(shard, EXPERTS * split)
        return ring.by_core(own, got.reshape(shard, EXPERTS * split), 0)

    ring_a = Gather(ring, attn_shard, "right")
    ring_a.step()
    if not ring.long:
        other_half = 1 - ring.core
        got_in = ring.other_core(unit_half(w_in, other_half))
        got_down = ring.other_core(unit_half(w_down, other_half))
        ring_in = Gather(ring, unit_shard(w_in, got_in), "right")
        ring_down = Gather(ring, unit_shard(w_down, got_down), "left")
        ring_a.step()
        a3 = ring_a.step()
        ring_a.step()
        ring_in.step(*a3)
        ring_down.step(*a3)
        own_a = ring_a.whole()
        attn_all = interleave(own_a, ring.other_core(own_a), ring.core, shard)
    else:
        attn_all = lax.all_gather(attn_shard, "dp", axis=0, tiled=True)
        in_all, down_all = (
            unit_half(lax.all_gather(w, "dp", axis=0, tiled=True), ring.core).reshape(
                -1, EXPERTS * split
            )
            for w in (w_in, w_down)
        )
    x_low = whole_rows(block_in, x_other, rank)
    x_all = x_low.astype(F32)
    grad_other = swap_tensor(out_grad)
    grad_out = whole_rows(out_grad, grad_other, rank).astype(F32)

    places = jnp.arange(count, dtype=jnp.int32)
    ends = jnp.cumsum(seq_lengths[0])
    seq_ids = jnp.sum((places[:, None] >= ends[None, :]).astype(jnp.int32), axis=1)
    bias_local = lax.dynamic_slice_in_dim(rel_bias, rank * heads_local, heads_local, 1)
    bucket_hits = (
        rel_table[:, None] == jnp.arange(rel_bias.shape[0], dtype=jnp.int32)[None, :]
    ).astype(F32)
    by_offset = jnp.dot(bucket_hits, bias_local, precision=HIGH)
    lanes = 2 * count
    by_offset = jnp.pad(by_offset.T, ((0, 0), (0, lanes - by_offset.shape[0])))
    normed_one, scale_one, projected, p_full, context, attn_part = attention_forward(
        x_low, attn_gain[None, :], attn_all, by_offset, seq_ids[:, None], seq_ids[None, :]
    )
    n_one = x_all * scale_one
    if not ring.long:
        ring_in.step(attn_part)
        ring_down.step(attn_part)
    hidden = x_all + (attn_part.astype(F32) + swap_tensor(attn_part).astype(F32))

    scale_two = rms_scale(hidden)
    n_two = hidden * scale_two
    mixed = n_two * moe_gain
    logits = jnp.stack([jnp.sum(mixed * w_router[:, e], axis=1) for e in range(EXPERTS)], axis=1)
    router_probs = jax.nn.softmax(logits, axis=-1)
    expert_col = expert_ids[:, 0]
    hits = expert_col[:, None] == jnp.arange(EXPERTS, dtype=jnp.int32)[None, :]
    hits_f = hits.astype(F32)
    gate = jnp.sum(router_probs * hits_f, axis=1, keepdims=True)
    hits_i = hits.astype(jnp.int32)
    slot = jnp.sum(jnp.cumsum(hits_i, axis=0) * hits_i, axis=1) - 1
    flat = expert_col * CAP + slot
    dispatch = (flat[:, None] == jnp.arange(EXPERTS * CAP, dtype=jnp.int32)[None, :]).astype(BF)
    grad_routed = (gate * grad_out).astype(BF)
    blocks = dot32(dispatch, mixed.astype(BF), TN).astype(BF)
    grad_blocks = dot32(dispatch, grad_routed, TN).astype(BF)


    def shared_slots(x):
        got = ring.other_core(x)
        return [
            jnp.concatenate([y[e * CAP : (e + 1) * CAP] for y in (x, got)], axis=0)
            for e in range(EXPERTS)
        ]

    blocks = shared_slots(blocks)
    grad_blocks = shared_slots(grad_blocks)
    if not ring.long:
        ring_in.step(*blocks, *grad_blocks)
        ring_down.step(*blocks, *grad_blocks)
        ring_in.step()
        ring_down.step()
        in_all = ring_in.whole()
        down_all = ring_down.whole()

    def cols(x, e):
        return x[:, e * split : (e + 1) * split]

    def own_sum(parts):
        away = jnp.concatenate([x[CAP:] for x in parts], axis=0)
        mine = jnp.concatenate([x[:CAP] for x in parts], axis=0)
        return (mine.astype(F32) + ring.other_core(away).astype(F32)).astype(BF)

    experts = range(EXPERTS)
    pre = [dot32(blocks[e], cols(in_all, e), NN) for e in experts]
    active = [jax.nn.gelu(v, approximate=True).astype(BF) for v in pre]
    send_down = Scatter(
        ring, [(grad_blocks[e], active[e]) for e in experts], 2 * shard, "right", True
    )
    send_down.step()
    returned = own_sum([dot32(active[e], cols(down_all, e), NT).astype(BF) for e in experts])
    grad_pre = []
    for e in experts:
        grad_active = dot32(grad_blocks[e], cols(down_all, e), NN)
        _, pull = jax.vjp(lambda v: jax.nn.gelu(v, approximate=True), pre[e])
        grad_pre.append(pull(grad_active)[0].astype(BF))
    grad_sent = own_sum([dot32(grad_pre[e], cols(in_all, e), NT).astype(BF) for e in experts])
    send_in = Scatter(ring, [(blocks[e], grad_pre[e]) for e in experts], 2 * shard, "left", True)
    routed_part = dot32(dispatch, returned, NN)
    sent_part = dot32(dispatch, grad_sent, NN)
    gate_part = jnp.sum(grad_out * routed_part, axis=1, keepdims=True)
    logits_part = gate_part * gate * (hits_f - router_probs)
    mixed_part = sent_part + sum(
        logits_part[:, e : e + 1] * w_router[:, e] for e in range(EXPERTS)
    )
    mixed_low = mixed_part.astype(BF)
    mixed_other = swap_tensor(mixed_low)
    in1 = send_in.step(mixed_low)
    send_down.step(mixed_low)
    (mixed_other,) = after((mixed_other,), in1)
    grad_mixed = mixed_low.astype(F32) + mixed_other.astype(F32)
    moe_gain_part = jnp.sum(mixed_part * n_two, axis=0)
    router_part = [jnp.sum(mixed * logits_part[:, e : e + 1], axis=0) for e in range(EXPERTS)]

    def own_rows(x):
        return lax.dynamic_slice_in_dim(x, rank * rows_local, rows_local, 0)

    def other_rows(x):
        return lax.dynamic_slice_in_dim(x, (1 - rank) * rows_local, rows_local, 0)

    routed_low = routed_part.astype(BF)
    routed = own_rows(routed_low).astype(F32) + swap_tensor(other_rows(routed_low)).astype(F32)
    result = own_rows(hidden) + own_rows(gate) * routed

    grad_hidden = grad_out + norm_back(grad_mixed, n_two, scale_two, moe_gain)
    grad_attended = grad_hidden.astype(BF)
    in2 = send_in.step()
    send_down.step()
    (grad_attended,) = after((grad_attended,), in2)
    grad_projected, offset_sums = attention_backward(
        grad_attended, attn_all, projected, p_full, context, lanes
    )
    send_a = Scatter(ring, [(normed_one, grad_projected), (grad_attended, context)], shard, "right", False)
    send_in.step(grad_projected)
    send_down.step(grad_projected)
    normed_part = dot32(grad_projected, attn_all[:, : 3 * head_cols], NT)
    attn_gain_part = jnp.sum(normed_part * n_one, axis=0)
    normed_low = normed_part.astype(BF)
    grad_normed = own_rows(normed_low).astype(F32) + swap_tensor(other_rows(normed_low)).astype(F32)
    grad_block = own_rows(grad_hidden) + norm_back(
        grad_normed, own_rows(n_one), own_rows(scale_one), attn_gain
    )
    grad_bias_heads = jnp.dot(offset_sums[:, : rel_table.shape[0]], bucket_hits, precision=HIGH)
    grad_rel = lax.dynamic_update_slice_in_dim(
        jnp.zeros(rel_bias.shape, F32), grad_bias_heads.T, rank * heads_local, 1
    )
    small = [attn_gain_part, moe_gain_part] + router_part + [grad_rel.reshape(-1)]
    line = jnp.concatenate(small)
    for _ in range(ring.chips // 2):
        send_a.step()
        send_in.step()
        send_down.step()

    def unit_total(send):
        if ring.long:
            zeros = jnp.zeros(send.grads.shape[:1] + (EXPERTS, units), BF)
            terms = send.grads.reshape(-1, EXPERTS, split)
            terms = lax.dynamic_update_slice_in_dim(zeros, terms, ring.core * split, 2)
            return lax.psum_scatter(terms, "dp", scatter_dimension=0, tiled=True).astype(F32)
        sums = send.total().reshape(2, shard, EXPERTS, split)
        away = lax.dynamic_index_in_dim(sums, 1 - ring.core, 0, keepdims=False)
        mine = lax.dynamic_index_in_dim(sums, ring.core, 0, keepdims=False)
        return ring.by_core(mine, ring.other_core(away), 2)

    grad_w_down_mine = unit_total(send_down)
    grad_w_in_mine = unit_total(send_in)
    if ring.long:
        attn_mine = lax.psum_scatter(send_a.grads, "dp", scatter_dimension=0, tiled=True)
        attn_mine = attn_mine.astype(F32)
    else:
        attn_mine = send_a.total()
    summed = sum_everywhere(line.reshape(-1, 128)).reshape(-1)
    return (
        result.astype(BF),
        grad_block,
        summed[:width],
        attn_mine[:, : 3 * head_cols].reshape(w_qkv.shape),
        attn_mine[:, 3 * head_cols :],
        summed[4 * width :].reshape(rel_bias.shape),
        summed[width : 2 * width],
        jnp.stack([summed[2 * width : 3 * width], summed[3 * width : 4 * width]], axis=1),
        grad_w_in_mine,
        grad_w_down_mine,
    )


def solution(mesh):
    placed = (
        P(("dp", "tensor"), None),
        P(),
        P("dp", None, "tensor"),
        P("dp", "tensor"),
        P(),
        P(),
        P(),
        P("dp", None, "tensor"),
        P("dp", None, "tensor"),
        P("dp", None),
        P("dp", None),
        P(),
        P(("dp", "tensor"), None),
    )
    return jax.shard_map(
        body,
        mesh=mesh,
        in_specs=placed,
        out_specs=(
            P(("dp", "tensor"), None),
            P(("dp", "tensor"), None),
            P(),
            P("dp", None, "tensor"),
            P("dp", "tensor"),
            P(),
            P(),
            P(),
            P("dp", None, "tensor"),
            P("dp", None, "tensor"),
        ),
        check_vma=False,
    )
```

```python
import jax
import jax.numpy as jnp
from jax import lax
from jax.experimental import pallas as pl
from jax.experimental.pallas import tpu as pltpu
from jax.sharding import PartitionSpec as P

HEAD_DIM = 64
EXPERTS = 2
CAP = 176

LONGEST = 16

EPS = 1e-06
NEG = -1e30
VMEM_BYTES = 12 << 20
EXPERT_VMEM_BYTES = 24 << 20
SMALL = pl.CostEstimate(flops=1, bytes_accessed=1, transcendentals=0)
HIGH = lax.Precision.HIGHEST
BF = jnp.bfloat16
F32 = jnp.float32


def ring_chip(place, chips):
    place = place % chips
    return jnp.where(place < chips // 2, 2 * place, 2 * (chips - 1 - place) + 1)


def ring_place(chip, chips):
    return jnp.where(chip % 2 == 0, chip // 2, chips - 1 - chip // 2)


class Ring:
    def __init__(self):
        self.n = lax.axis_size("dp")
        self.chips = self.n // 2
        order = [2 * i for i in range(self.chips // 2)]
        order = order + [c + 1 for c in reversed(order)]
        pairs = [
            (order[i] * 2 + k, order[(i + 1) % self.chips] * 2 + k)
            for i in range(self.chips)
            for k in (0, 1)
        ]
        self.right = pairs
        self.left = [(b, a) for a, b in pairs]
        self.swap = [(i, i ^ 1) for i in range(self.n)]
        index = lax.axis_index("dp")
        self.core = index % 2
        self.long = self.chips > LONGEST
        self.place = ring_place(index // 2, self.chips)
        reach = self.chips // 2
        self.distances = [0] + [d for s in range(1, reach) for d in (-s, s)] + [reach]
        self.slots = [reach] + [d for s in range(reach - 1, 0, -1) for d in (s, -s)] + [0]

    def other_core(self, x):
        return lax.ppermute(x, "dp", self.swap)

    def by_core(self, own, other, axis):
        return jnp.where(
            self.core == 0,
            jnp.concatenate([own, other], axis=axis),
            jnp.concatenate([other, own], axis=axis),
        )

    def slot_chips(self):
        return jnp.stack([self.chip_at(d) for d in self.slots])

    def chip_at(self, distance):
        return ring_chip(self.place + distance + self.chips, self.chips)


class Gather:
    def __init__(self, ring, shard, halves):
        self.ring, self.shard, self.halves = ring, shard, halves
        self.reach = ring.chips // 2
        self.pieces = [shard]
        self.sent = (shard, shard)
        self.steps = 0

    def step(self, *deps):
        ring, half = self.ring, self.shard.shape[1] // 2
        self.steps += 1
        r, l = after(self.sent, deps)
        if self.steps < self.reach:
            self.sent = (lax.ppermute(r, "dp", ring.right), lax.ppermute(l, "dp", ring.left))
        elif self.halves:
            self.sent = (
                lax.ppermute(r[:, :half], "dp", ring.right),
                lax.ppermute(l[:, half:], "dp", ring.left),
            )
        else:
            self.sent = (lax.ppermute(r, "dp", ring.right),)
        self.pieces += self.sent
        return self.sent

    def owners(self):
        chips = [self.ring.chip_at(d) for d in self.ring.distances]
        return jnp.stack(chips + chips[-1:] if self.halves else chips)


class Scatter:
    def __init__(self, ring, terms, rows):
        self.ring, self.rows = ring, rows
        self.reach = ring.chips // 2
        self.steps = 0
        self.slots = ring.slots
        self.terms = terms
        self.each = len(self.terms) > 2
        self.got = None if self.each else ring.other_core(self.terms[1])

    def blocks(self, distance):
        at = self.slots.index(distance)
        return [(self.terms[at], 0)] if self.each else [(self.terms[0], at), (self.got, at)]

    def step(self, *deps):
        ring = self.ring
        distance = self.reach - self.steps
        self.steps += 1
        if distance == self.reach:
            r, l = ring_far(self.blocks(distance), self.rows)
        else:
            sent = after(self.sent, deps)
            r, l = ring_add(self.blocks(distance), self.blocks(-distance), sent, self.rows)
        self.sent = (lax.ppermute(r, "dp", ring.right), lax.ppermute(l, "dp", ring.left))
        return self.sent

    def total(self):
        r, l = self.sent
        terms = [
            x[at * self.rows : (at + 1) * self.rows].astype(F32) for x, at in self.blocks(0)
        ]
        return sum(terms) + r.astype(F32) + l.astype(F32)


def row_block(rows, width, at):
    return pl.BlockSpec((rows, width), lambda i: (at, 0))


def ring_far(blocks, rows):
    width = blocks[0][0].shape[1]
    half = width // 2

    def kernel(*refs):
        ins, (r_ref, l_ref) = refs[:-2], refs[-2:]
        total = sum(ref[...].astype(F32) for ref in ins).astype(BF)
        r_ref[...] = total[:, :half]
        l_ref[...] = total[:, half:]

    return pl.pallas_call(
        kernel,
        out_shape=[jax.ShapeDtypeStruct((rows, half), BF)] * 2,
        in_specs=[row_block(rows, width, at) for _, at in blocks],
        out_specs=[row_block(rows, half, 0)] * 2,
        compiler_params=pltpu.CompilerParams(vmem_limit_bytes=VMEM_BYTES),
        cost_estimate=SMALL,
        grid=(1,),
        name="ring_far",
    )(*[x for x, _ in blocks])


def ring_add(right, left, sent, rows):
    width = right[0][0].shape[1]
    arrived = sent[0].shape[1]
    number = len(right)
    tiles = 2 if arrived < width else max(1, width // 768)
    tile = width // tiles

    def kernel(*refs):
        ins, outs = refs[:-2], refs[-2:]
        for k, out_ref in enumerate(outs):
            own = ins[k * (number + 1) : (k + 1) * (number + 1) - 1]
            got = ins[(k + 1) * (number + 1) - 1]
            total = sum(ref[...].astype(F32) for ref in own)
            more = got[...].astype(F32)
            if arrived < width:
                more = jnp.where(pl.program_id(0) == k, more, 0.0)
            out_ref[...] = (total + more).astype(BF)

    def block(at):
        return pl.BlockSpec((rows, tile), lambda i: (at, i))

    got_block = block(0) if arrived == width else row_block(rows, tile, 0)
    specs, args = [], []
    for blocks, got in ((right, sent[0]), (left, sent[1])):
        specs += [block(at) for _, at in blocks] + [got_block]
        args += [x for x, _ in blocks] + [got]
    return pl.pallas_call(
        kernel,
        out_shape=[jax.ShapeDtypeStruct((rows, width), BF)] * 2,
        in_specs=specs,
        out_specs=[block(0)] * 2,
        compiler_params=pltpu.CompilerParams(vmem_limit_bytes=VMEM_BYTES),
        cost_estimate=SMALL,
        grid=(tiles,),
        name="ring_add",
    )(*args)


def outer(pairs, owners, rows, counts):
    height = pairs[0][0].shape[1]
    widths = [rhs.shape[1] for _, rhs in pairs]
    width = sum(widths)
    tile = 768

    def kernel(owners_ref, *refs):
        ins, outs, held_ref = refs[: 2 * len(pairs)], refs[2 * len(pairs) : -1], refs[-1]
        at = 0
        for i, wide in enumerate(widths):
            lhs = ins[2 * i][...]
            for start in range(0, wide, tile):
                size = min(tile, wide - start)
                held_ref[:, pl.ds(at, size)] = dot32(
                    lhs, ins[2 * i + 1][:, pl.ds(start, size)], TN
                ).astype(BF)
                at += size
        slot = 0
        for ref, number in zip(outs, counts):
            for to in range(number):
                source = pl.multiple_of(owners_ref[slot] * rows, 16)
                ref[pl.ds(to * rows, rows), :] = held_ref[pl.ds(source, rows), :]
                slot += 1

    inside = pl.BlockSpec(memory_space=pltpu.VMEM)
    return pl.pallas_call(
        kernel,
        out_shape=[jax.ShapeDtypeStruct((number * rows, width), BF) for number in counts],
        in_specs=[pl.BlockSpec(memory_space=pltpu.SMEM)] + [inside] * (2 * len(pairs)),
        out_specs=[inside] * len(counts),
        scratch_shapes=[pltpu.VMEM((height, width), BF)],
        compiler_params=pltpu.CompilerParams(vmem_limit_bytes=VMEM_BYTES),
        cost_estimate=SMALL,
        name="outer",
    )(owners, *[x for pair in pairs for x in pair])


def after(values, deps):
    if not deps:
        return values
    return lax.optimization_barrier((tuple(values), deps))[0]


def ring_total(block, sent, core):
    x, at = block
    rows, width = sent[0].shape
    tile, half = 768, rows // 2

    def kernel(core_ref, own_ref, r_ref, l_ref, mine_ref, away_ref, total_ref):
        total_ref[...] = (
            own_ref[...].astype(F32) + r_ref[...].astype(F32) + l_ref[...].astype(F32)
        )
        begin = pl.multiple_of(core_ref[0] * half, 8)
        mine_ref[...] = total_ref[pl.ds(begin, half), :]
        away_ref[...] = total_ref[pl.ds(half - begin, half), :]

    def block_of(number, at):
        return pl.BlockSpec((number, tile), lambda i: (at, i))

    return pl.pallas_call(
        kernel,
        out_shape=[jax.ShapeDtypeStruct((half, width), F32)] * 2,
        in_specs=[pl.BlockSpec(memory_space=pltpu.SMEM), block_of(rows, at)]
        + [block_of(rows, 0)] * 2,
        out_specs=[block_of(half, 0)] * 2,
        scratch_shapes=[pltpu.VMEM((rows, tile), F32)],
        compiler_params=pltpu.CompilerParams(vmem_limit_bytes=VMEM_BYTES),
        cost_estimate=SMALL,
        grid=(width // tile,),
        name="ring_total",
    )(core[None], x, *sent)


def combine(mine, got, core):
    rows, width = mine.shape
    split = width // 2 // EXPERTS

    def kernel(core_ref, mine_ref, got_ref, *outs):
        for k, ref in enumerate((mine_ref, got_ref)):
            first = (1 - core_ref[0]) if k else core_ref[0]
            at = pl.ds(pl.multiple_of(first * split, 128), split)
            for i, out_ref in enumerate(outs):
                for e in range(EXPERTS):
                    out_ref[:, e, at] = ref[:, pl.ds((i * EXPERTS + e) * split, split)]

    inside = pl.BlockSpec(memory_space=pltpu.VMEM)
    return pl.pallas_call(
        kernel,
        out_shape=[jax.ShapeDtypeStruct((rows, EXPERTS, 2 * split), F32)] * 2,
        in_specs=[pl.BlockSpec(memory_space=pltpu.SMEM)] + [inside] * 2,
        out_specs=[inside] * 2,
        compiler_params=pltpu.CompilerParams(vmem_limit_bytes=VMEM_BYTES),
        cost_estimate=SMALL,
        name="combine",
    )(core[None], mine, got)


def place_pieces(ins, owners_ref, outs, sems, rows):
    copies = []
    wide = outs[0].shape[1]
    for i, ref in enumerate(ins):
        target = pl.ds(pl.multiple_of(owners_ref[i] * rows, 16), rows)
        shift = wide if i > 0 and ref.shape[1] < ins[0].shape[1] and i == len(ins) - 1 else 0
        for begin in range(0, ref.shape[1], wide):
            to = outs[(begin + shift) // wide].at[target]
            source = ref if ref.shape[1] == wide else ref.at[:, pl.ds(begin, wide)]
            copies.append(pltpu.make_async_copy(source, to, sems.at[len(copies)]))
    return copies


def assemble(pieces, owners):
    rows, width = pieces[0].shape
    number = len(pieces)

    def kernel(owners_ref, *refs):
        copies = place_pieces(
            refs[:number], owners_ref, refs[number : number + 1], refs[number + 1], rows
        )
        for copy in copies:
            copy.start()
        for copy in copies:
            copy.wait()

    return pl.pallas_call(
        kernel,
        out_shape=jax.ShapeDtypeStruct((number * rows, width), BF),
        in_specs=[pl.BlockSpec(memory_space=pltpu.SMEM)]
        + [pl.BlockSpec(memory_space=pl.ANY)] * number,
        out_specs=pl.BlockSpec(memory_space=pltpu.VMEM),
        scratch_shapes=[pltpu.SemaphoreType.DMA((number,))],
        compiler_params=pltpu.CompilerParams(vmem_limit_bytes=VMEM_BYTES),
        cost_estimate=SMALL,
        name="assemble",
    )(owners, *pieces)


def gelu_and_slope(v):
    c = 0.7978845608028654
    t = jnp.tanh(c * (v + 0.044715 * (v * v * v)))
    slope = 0.5 * (1.0 + t) + 0.5 * v * (1.0 - t * t) * c * (1.0 + 3 * 0.044715 * (v * v))
    return 0.5 * v * (1.0 + t), slope


def expert_rows(own_ref, got_ref, e, begin, width):
    at = (pl.ds(e * CAP, CAP), pl.ds(begin, width))
    return jnp.concatenate([own_ref[at], got_ref[at]], axis=0)


def expert_layers(own, got, pieces, owners, slots, rows_out):
    filled, d = own.shape[0], own.shape[1] // 2
    rows, width = pieces[0].shape
    count = len(pieces)
    number = count - (pieces[-1].shape[1] < width)
    units = width // 2 // EXPERTS
    chips = slots.shape[0]

    def kernel(owners_ref, slots_ref, own_ref, got_ref, *refs):
        ins, mine_ref, away_ref = refs[:count], refs[count], refs[count + 1]
        outs = refs[count + 2 : count + 2 + chips]
        in_ref, down_ref, held_ref, sems, out_sems = refs[count + 2 + chips :]
        copies = place_pieces(ins, owners_ref, (in_ref, down_ref), sems, rows)
        for copy in copies:
            copy.start()
        for copy in copies:
            copy.wait()
        for e in range(EXPERTS):
            cols = pl.ds(e * units, units)
            w_i, w_d = in_ref[:, cols], down_ref[:, cols]
            x, g = (expert_rows(own_ref, got_ref, e, k * d, d) for k in range(2))
            active, slope = gelu_and_slope(dot32(x, w_i, NN))
            active = active.astype(BF)
            grad_pre = (dot32(g, w_d, NN) * slope).astype(BF)
            back = dot32(active, w_d, NT).astype(BF)
            sent = dot32(grad_pre, w_i, NT).astype(BF)
            for k, ref in enumerate((mine_ref, away_ref)):
                ref[pl.ds(e * CAP, CAP), pl.ds(0, d)] = back[k * CAP : (k + 1) * CAP]
                ref[pl.ds(e * CAP, CAP), pl.ds(d, d)] = sent[k * CAP : (k + 1) * CAP]
            held_ref[:, pl.ds(e * units, units)] = dot32(x, grad_pre, TN).astype(BF)
            held_ref[:, pl.ds((EXPERTS + e) * units, units)] = dot32(g, active, TN).astype(BF)
        copies = []
        for slot in range(chips):
            begin = pl.multiple_of(slots_ref[slot] * rows_out, 16)
            source = held_ref.at[pl.ds(begin, rows_out)]
            copies.append(pltpu.make_async_copy(source, outs[slot], out_sems.at[slot]))
        for copy in copies:
            copy.start()
        for copy in copies:
            copy.wait()

    inside = pl.BlockSpec(memory_space=pltpu.VMEM)
    anywhere = pl.BlockSpec(memory_space=pl.ANY)
    scalars = pl.BlockSpec(memory_space=pltpu.SMEM)
    mine, away, *terms = pl.pallas_call(
        kernel,
        out_shape=[jax.ShapeDtypeStruct((filled, 2 * d), BF)] * 2
        + [jax.ShapeDtypeStruct((rows_out, width), BF)] * chips,
        in_specs=[scalars, scalars, inside, inside] + [anywhere] * count,
        out_specs=[inside, inside] + [anywhere] * chips,
        scratch_shapes=[pltpu.VMEM((number * rows, width // 2), BF)] * 2
        + [
            pltpu.VMEM((d, width), BF),
            pltpu.SemaphoreType.DMA((2 * number,)),
            pltpu.SemaphoreType.DMA((chips,)),
        ],
        compiler_params=pltpu.CompilerParams(vmem_limit_bytes=EXPERT_VMEM_BYTES),
        cost_estimate=SMALL,
        name="expert_layers",
    )(owners, slots, own, got, *pieces)
    return mine, away, terms


def interleave(own, other, core, rows):
    chips, width = own.shape[0] // rows, own.shape[1]

    def kernel(core_ref, own_ref, other_ref, out_ref):
        for k, ref in enumerate((own_ref, other_ref)):
            first = (1 - core_ref[0]) if k else core_ref[0]
            for chip in range(chips):
                target = pl.multiple_of((2 * chip + first) * rows, 16)
                out_ref[pl.ds(target, rows), :] = ref[pl.ds(chip * rows, rows), :]

    inside = pl.BlockSpec(memory_space=pltpu.VMEM)
    return pl.pallas_call(
        kernel,
        out_shape=jax.ShapeDtypeStruct((2 * chips * rows, width), BF),
        in_specs=[pl.BlockSpec(memory_space=pltpu.SMEM), inside, inside],
        out_specs=inside,
        compiler_params=pltpu.CompilerParams(vmem_limit_bytes=VMEM_BYTES),
        cost_estimate=SMALL,
        name="interleave",
    )(core[None], own, other)


def swap_tensor(x):
    return lax.ppermute(x, "tensor", [(0, 1), (1, 0)])


def whole_rows(own, other, rank):
    return jnp.where(
        rank == 0, jnp.concatenate([own, other], axis=0), jnp.concatenate([other, own], axis=0)
    )


def sum_chips(x):
    step = 2
    while step < lax.axis_size("dp"):
        x = x + lax.ppermute(x, "dp", [(i, i ^ step) for i in range(lax.axis_size("dp"))])
        step *= 2
    return x


def rms_scale(rows):
    return lax.rsqrt(jnp.mean(rows * rows, axis=-1, keepdims=True) + EPS)


def norm_back(grad, normed, scale, gain):
    weighted = grad * gain
    return scale * (weighted - normed * jnp.mean(weighted * normed, axis=-1, keepdims=True))


def dot32(a, b, dims):
    return lax.dot_general(a, b, (dims, ((), ())), preferred_element_type=F32)


NN = ((1,), (0,))
NT = ((1,), (1,))
TN = ((0,), (0,))


def attention_forward(x, gain, weights, by_offset, seq_col, seq_row):
    count, d = x.shape
    head_cols = weights.shape[1] // 4
    heads = head_cols // HEAD_DIM
    scale = HEAD_DIM ** (-0.5)
    lanes = by_offset.shape[1]

    def kernel(x_ref, gain_ref, w_ref, off_ref, col_ref, row_ref, *outs):
        normed_ref, scale_ref, proj_ref, p_ref, context_ref, part_ref = outs
        rows = x_ref[...].astype(F32)
        r = lax.rsqrt(jnp.mean(rows * rows, axis=-1, keepdims=True) + EPS)
        scale_ref[...] = r
        normed = (rows * r * gain_ref[...]).astype(BF)
        normed_ref[...] = normed
        for s in range(3):
            at = pl.ds(s * head_cols, head_cols)
            proj_ref[:, at] = dot32(normed, w_ref[:, at], NN).astype(BF)
        same = col_ref[...] == row_ref[...]
        for h in range(heads):
            q = proj_ref[:, pl.ds(h * HEAD_DIM, HEAD_DIM)]
            k = proj_ref[:, pl.ds(head_cols + h * HEAD_DIM, HEAD_DIM)]
            v = proj_ref[:, pl.ds(2 * head_cols + h * HEAD_DIM, HEAD_DIM)]
            line = jnp.broadcast_to(off_ref[pl.ds(h, 1), :], (count, lanes))
            bias = pltpu.roll(line, lanes - (count - 1), 1, stride=1, stride_axis=0)[:, :count]
            scores = jnp.where(same, dot32(q, k, NT) * scale + bias, NEG)
            expo = jnp.exp(scores - jnp.max(scores, axis=-1, keepdims=True))
            p = expo / jnp.sum(expo, axis=-1, keepdims=True)
            p_ref[h] = p
            context_ref[:, pl.ds(h * HEAD_DIM, HEAD_DIM)] = dot32(p.astype(BF), v, NN).astype(BF)
        out_w = w_ref[:, pl.ds(3 * head_cols, head_cols)]
        part_ref[...] = dot32(context_ref[...], out_w, NT).astype(BF)

    inside = pl.BlockSpec(memory_space=pltpu.VMEM)
    return pl.pallas_call(
        kernel,
        out_shape=(
            jax.ShapeDtypeStruct((count, d), BF),
            jax.ShapeDtypeStruct((count, 1), F32),
            jax.ShapeDtypeStruct((count, 3 * head_cols), BF),
            jax.ShapeDtypeStruct((heads, count, count), F32),
            jax.ShapeDtypeStruct((count, head_cols), BF),
            jax.ShapeDtypeStruct((count, d), BF),
        ),
        in_specs=[inside] * 6,
        out_specs=(inside,) * 6,
        compiler_params=pltpu.CompilerParams(vmem_limit_bytes=VMEM_BYTES),
        cost_estimate=SMALL,
        name="attention_forward",
    )(x, gain, weights, by_offset, seq_col, seq_row)


def attention_backward(low, other, hidden, scales, gain, out_grad, weights, proj, p_full, lanes):
    count, d = low.shape
    head_cols = weights.shape[1] // 4
    heads = head_cols // HEAD_DIM
    scale = HEAD_DIM ** (-0.5)

    def kernel(low_ref, other_ref, hidden_ref, scales_ref, gain_ref, g_ref, w_ref, proj_ref, p_ref,
               hidden_grad_ref, grad_ref, out_ref, sums_ref, gc_ref):
        r2 = scales_ref[:, 3:4]
        n = hidden_ref[...] * r2
        u = (low_ref[...].astype(F32) + other_ref[...].astype(F32)) * gain_ref[...]
        total = g_ref[...].astype(F32) + r2 * (u - n * jnp.mean(u * n, axis=-1, keepdims=True))
        hidden_grad_ref[...] = total
        grad_ref[...] = total.astype(BF)
        out_w = w_ref[:, pl.ds(3 * head_cols, head_cols)]
        gc_ref[...] = dot32(grad_ref[...], out_w, NN).astype(BF)
        down = lax.broadcasted_iota(jnp.int32, (count, count), 0)
        across = lax.broadcasted_iota(jnp.int32, (count, count), 1)
        flip = (down + across == count - 1).astype(F32).astype(BF)
        for h in range(heads):
            at = [pl.ds(s * head_cols + h * HEAD_DIM, HEAD_DIM) for s in range(3)]
            q, k, v = proj_ref[:, at[0]], proj_ref[:, at[1]], proj_ref[:, at[2]]
            p = p_ref[h]
            gc = gc_ref[:, at[0]]
            dp = dot32(gc, v, NT)
            ds = (p * (dp - jnp.sum(p * dp, axis=-1, keepdims=True))).astype(BF)
            out_ref[:, at[0]] = (dot32(ds, k, NN) * scale).astype(BF)
            out_ref[:, at[1]] = (dot32(ds, q, TN) * scale).astype(BF)
            out_ref[:, at[2]] = dot32(p.astype(BF), gc, TN).astype(BF)
            turned = dot32(ds, flip, TN)
            wide = jnp.concatenate([turned, jnp.zeros((count, lanes - count), F32)], axis=1)
            rolled = pltpu.roll(wide, 0, 1, stride=1, stride_axis=0)
            sums_ref[pl.ds(h, 1), :] = jnp.sum(rolled, axis=0, keepdims=True)

    inside = pl.BlockSpec(memory_space=pltpu.VMEM)
    return pl.pallas_call(
        kernel,
        out_shape=(
            jax.ShapeDtypeStruct((count, d), F32),
            jax.ShapeDtypeStruct((count, d), BF),
            jax.ShapeDtypeStruct((count, 3 * head_cols), BF),
            jax.ShapeDtypeStruct((heads, lanes), F32),
        ),
        in_specs=[inside] * 9,
        out_specs=(inside,) * 4,
        scratch_shapes=[pltpu.VMEM((count, head_cols), BF)],
        compiler_params=pltpu.CompilerParams(vmem_limit_bytes=VMEM_BYTES),
        cost_estimate=SMALL,
        name="attention_backward",
    )(low, other, hidden, scales, gain, out_grad, weights, proj, p_full)


def route(x, part, other, gain, w_router, expert_col, flat, out_grad):
    count, d = x.shape

    def kernel(x_ref, part_ref, other_ref, gain_ref, w_ref, expert_ref, flat_ref, g_ref,
               hidden_ref, blocks_ref, scales_ref):
        hidden = x_ref[...].astype(F32) + (part_ref[...].astype(F32) + other_ref[...].astype(F32))
        hidden_ref[...] = hidden
        r2 = lax.rsqrt(jnp.mean(hidden * hidden, axis=-1, keepdims=True) + EPS)
        mixed = hidden * r2 * gain_ref[...]
        logits = [
            jnp.sum(mixed * w_ref[e : e + 1, :], axis=-1, keepdims=True) for e in range(EXPERTS)
        ]
        top = jnp.maximum(logits[0], logits[1])
        expo = [jnp.exp(v - top) for v in logits]
        probs = [v / (expo[0] + expo[1]) for v in expo]
        hits = [(expert_ref[...] == e).astype(F32) for e in range(EXPERTS)]
        gate = probs[0] * hits[0] + probs[1] * hits[1]
        lane = lax.broadcasted_iota(jnp.int32, (count, 128), 1)
        columns = [gate] + [gate * (h - p) for h, p in zip(hits, probs)] + [r2]
        scales_ref[...] = sum(jnp.where(lane == i, v, 0.0) for i, v in enumerate(columns))
        slots = lax.broadcasted_iota(jnp.int32, (EXPERTS * CAP, count), 0)
        chosen = (slots == flat_ref[...]).astype(F32).astype(BF)
        blocks_ref[:, pl.ds(0, d)] = dot32(chosen, mixed.astype(BF), NN).astype(BF)
        grad_routed = (gate * g_ref[...].astype(F32)).astype(BF)
        blocks_ref[:, pl.ds(d, d)] = dot32(chosen, grad_routed, NN).astype(BF)

    inside = pl.BlockSpec(memory_space=pltpu.VMEM)
    return pl.pallas_call(
        kernel,
        out_shape=(
            jax.ShapeDtypeStruct((count, d), F32),
            jax.ShapeDtypeStruct((EXPERTS * CAP, 2 * d), BF),
            jax.ShapeDtypeStruct((count, 128), F32),
        ),
        in_specs=[inside] * 8,
        out_specs=(inside,) * 3,
        compiler_params=pltpu.CompilerParams(vmem_limit_bytes=VMEM_BYTES),
        cost_estimate=SMALL,
        name="route",
    )(x, part, other, gain, w_router, expert_col, flat, out_grad)


def rows_back(mine, got, hidden, scales, gain, w_router, flat, out_grad):
    count, d = hidden.shape

    def kernel(mine_ref, got_ref, hidden_ref, scales_ref, gain_ref, w_ref, flat_ref, g_ref,
               mixed_ref, routed_ref, gains_ref):
        sums = (mine_ref[...].astype(F32) + got_ref[...].astype(F32)).astype(BF)
        slots = lax.broadcasted_iota(jnp.int32, (count, EXPERTS * CAP), 1)
        chosen = (slots == flat_ref[...]).astype(F32).astype(BF)
        routed = dot32(chosen, sums[:, :d], NN)
        gate, r2 = scales_ref[:, 0:1], scales_ref[:, 3:4]
        routed_ref[...] = (gate * routed).astype(BF)
        gate_part = jnp.sum(g_ref[...].astype(F32) * routed, axis=-1, keepdims=True)
        grad_logits = [gate_part * scales_ref[:, 1 + e : 2 + e] for e in range(EXPERTS)]
        part = dot32(chosen, sums[:, d:], NN)
        part = part + sum(grad_logits[e] * w_ref[e : e + 1, :] for e in range(EXPERTS))
        mixed_ref[...] = part.astype(BF)
        n = hidden_ref[...] * r2
        gains_ref[0:1, :] = jnp.sum(part * n, axis=0, keepdims=True)
        mixed = n * gain_ref[...]
        for e in range(EXPERTS):
            gains_ref[1 + e : 2 + e, :] = jnp.sum(mixed * grad_logits[e], axis=0, keepdims=True)
        gains_ref[1 + EXPERTS :, :] = jnp.zeros((7 - EXPERTS, d), F32)

    inside = pl.BlockSpec(memory_space=pltpu.VMEM)
    return pl.pallas_call(
        kernel,
        out_shape=(
            jax.ShapeDtypeStruct((count, d), BF),
            jax.ShapeDtypeStruct((count, d), BF),
            jax.ShapeDtypeStruct((8, d), F32),
        ),
        in_specs=[inside] * 8,
        out_specs=(inside,) * 3,
        compiler_params=pltpu.CompilerParams(vmem_limit_bytes=VMEM_BYTES),
        cost_estimate=SMALL,
        name="rows_back",
    )(mine, got, hidden, scales, gain, w_router, flat, out_grad)


def input_back(grad, weights, x, sums, bucket_hits, gains, rank):
    count, d = x.shape
    heads, lanes = sums.shape
    buckets = bucket_hits.shape[1]
    each = d // 128

    def kernel(rank_ref, grad_ref, w_ref, x_ref, sums_ref, hits_ref, gains_ref, low_ref, line_ref):
        part = dot32(grad_ref[...], w_ref[:, pl.ds(0, grad_ref.shape[1])], NT)
        low_ref[...] = part.astype(BF)
        rows = x_ref[...].astype(F32)
        n = rows * lax.rsqrt(jnp.mean(rows * rows, axis=-1, keepdims=True) + EPS)
        vectors = [jnp.sum(part * n, axis=0, keepdims=True)]
        vectors += [gains_ref[k : k + 1, :] for k in range(1 + EXPERTS)]
        for k, vector in enumerate(vectors):
            for j in range(each):
                line_ref[pl.ds(16 + k * each + j, 1), :] = vector[:, j * 128 : (j + 1) * 128]
        rel = jnp.dot(sums_ref[...], hits_ref[...], precision=HIGH, preferred_element_type=F32)
        rel = jnp.concatenate([rel, jnp.zeros((heads, 128 - buckets), F32)], axis=1)
        line_ref[0:16, :] = jnp.zeros((16, 128), F32)
        for k in range(2):
            line_ref[pl.ds(k * heads, heads), :] = jnp.where(rank_ref[0] == k, rel, 0.0)

    inside = pl.BlockSpec(memory_space=pltpu.VMEM)
    return pl.pallas_call(
        kernel,
        out_shape=(
            jax.ShapeDtypeStruct((count, d), BF),
            jax.ShapeDtypeStruct((16 + (2 + EXPERTS) * each, 128), F32),
        ),
        in_specs=[pl.BlockSpec(memory_space=pltpu.SMEM)] + [inside] * 6,
        out_specs=(inside,) * 2,
        compiler_params=pltpu.CompilerParams(vmem_limit_bytes=VMEM_BYTES),
        cost_estimate=SMALL,
        name="input_back",
    )(rank[None], grad, weights, x, sums, bucket_hits, gains)


def body(
    block_in,
    attn_gain,
    w_qkv,
    w_out,
    rel_bias,
    moe_gain,
    w_router,
    w_in,
    w_down,
    seq_lengths,
    expert_ids,
    rel_table,
    out_grad,
):
    rows_local, width = block_in.shape
    rank = lax.axis_index("tensor")
    ring = Ring()
    shard = w_out.shape[0]
    head_cols = w_out.shape[1]
    units = w_in.shape[2]
    heads_local = head_cols // HEAD_DIM
    count = 2 * rows_local

    attn_shard = jnp.concatenate([w_qkv.reshape(shard, 3 * head_cols), w_out], axis=1)
    x_other, g_other = swap_tensor(block_in), swap_tensor(out_grad)
    split = units // 2

    def unit_half(w, core):
        return lax.dynamic_slice_in_dim(w, core * split, split, axis=2)

    if not ring.long:
        ring_a = Gather(ring, attn_shard, False)
        a1 = ring_a.step()
        own_half, other_half = (
            jnp.concatenate(
                [unit_half(w, core).reshape(shard, EXPERTS * split) for w in (w_in, w_down)],
                axis=1,
            )
            for core in (ring.core, 1 - ring.core)
        )
        got_half = ring.other_core(other_half)
        a2 = ring_a.step()
        ring_b = Gather(ring, ring.by_core(own_half, got_half, 0), True)
        a3 = ring_a.step()
        a4 = ring_a.step()
        ring_b.step(*a3, x_other, g_other)
        own_a = assemble(ring_a.pieces, ring_a.owners())
        other_a = ring.other_core(own_a)
        attn_all = interleave(own_a, other_a, ring.core, shard)
    else:
        attn_all = lax.all_gather(attn_shard, "dp", axis=0, tiled=True)
        in_all, down_all = (
            unit_half(lax.all_gather(w, "dp", axis=0, tiled=True), ring.core).reshape(
                -1, EXPERTS * split
            )
            for w in (w_in, w_down)
        )
    x_low = whole_rows(block_in, x_other, rank)
    g_low = whole_rows(out_grad, g_other, rank)

    places = jnp.arange(count, dtype=jnp.int32)
    ends = jnp.cumsum(seq_lengths[0])
    seq_ids = jnp.sum((places[:, None] >= ends[None, :]).astype(jnp.int32), axis=1)
    bias_local = lax.dynamic_slice_in_dim(rel_bias, rank * heads_local, heads_local, 1)
    bucket_hits = (
        rel_table[:, None] == jnp.arange(rel_bias.shape[0], dtype=jnp.int32)[None, :]
    ).astype(F32)
    by_offset = jnp.dot(bucket_hits, bias_local, precision=HIGH)
    lanes = 2 * count
    by_offset = jnp.pad(by_offset.T, ((0, 0), (0, lanes - by_offset.shape[0])))
    normed_one, _, projected, p_full, context, attn_part = attention_forward(
        x_low, attn_gain[None, :], attn_all, by_offset, seq_ids[:, None], seq_ids[None, :]
    )
    if not ring.long:
        ring_b.step(other_a)
        ring_b.step(attn_part)
    attn_other = swap_tensor(attn_part)
    expert_col = expert_ids[:, 0]
    hits = (
        expert_col[:, None] == jnp.arange(EXPERTS, dtype=jnp.int32)[None, :]
    ).astype(jnp.int32)
    flat = expert_col * CAP + jnp.sum(jnp.cumsum(hits, axis=0) * hits, axis=1) - 1
    gain_row, router_rows = moe_gain[None, :], w_router.T
    hidden, own_blocks, scales = route(
        x_low, attn_part, attn_other, gain_row, router_rows, expert_ids, flat[None, :], g_low
    )
    if not ring.long:
        got_blocks = ring.other_core(own_blocks)
        ring_b.step(got_blocks)
        mine, away, terms = expert_layers(
            own_blocks, got_blocks, ring_b.pieces, ring_b.owners(), ring.slot_chips(), 2 * shard
        )
        send = Scatter(ring, terms, 2 * shard)
        c1 = send.step()
    else:
        whole = jnp.concatenate([in_all, down_all], axis=1)
        first = jnp.zeros((1,), jnp.int32)
        mine, away, terms = expert_layers(
            own_blocks, ring.other_core(own_blocks), [whole], first, first, width
        )
    got_sums = ring.other_core(away)
    mixed_low, routed_low, gains = rows_back(
        mine, got_sums, hidden, scales, gain_row, router_rows, flat[:, None], g_low
    )
    if not ring.long:
        c2 = send.step(mixed_low)
    mixed_other = swap_tensor(mixed_low)
    if not ring.long:
        (mixed_other,) = after((mixed_other,), c1)

    def own_rows(x):
        return lax.dynamic_slice_in_dim(x, rank * rows_local, rows_local, 0)

    def other_rows(x):
        return lax.dynamic_slice_in_dim(x, (1 - rank) * rows_local, rows_local, 0)

    routed_other = swap_tensor(other_rows(routed_low))
    result = own_rows(hidden) + (
        own_rows(routed_low).astype(F32) + routed_other.astype(F32)
    )
    grad_hidden, grad_attended, grad_projected, offset_sums = attention_backward(
        mixed_low, mixed_other, hidden, scales, gain_row, g_low, attn_all, projected, p_full, lanes
    )

    attn_pairs = [(normed_one, grad_projected), (grad_attended, context)]
    if not ring.long:
        attn_pairs[0] = (normed_one, after((grad_projected,), c2)[0])
        chips = ring.slot_chips()
        owners = jnp.concatenate([chips * 2 + ring.core, chips * 2 + 1 - ring.core])
        send_a = Scatter(ring, outer(attn_pairs, owners, shard, [ring.chips] * 2), shard)
        c3 = send.step()
        a1 = send_a.step()
    hits_wide = jnp.pad(bucket_hits, ((0, lanes - bucket_hits.shape[0]), (0, 0)))
    normed_low, line = input_back(
        grad_projected, attn_all, x_low, offset_sums, hits_wide, gains, rank
    )
    normed_other = swap_tensor(other_rows(normed_low))
    line = line + swap_tensor(line)
    line = line + ring.other_core(line)
    if not ring.long:
        c4 = send.step(line, *a1)
        a2 = send_a.step(*c3)
        (line,) = after((line,), c4 + a2)
        send_a.step(*c4)
        send_a.step()
    summed = sum_chips(line)
    grad_normed = own_rows(normed_low).astype(F32) + normed_other.astype(F32)
    x_own = block_in.astype(F32)
    scale_own = rms_scale(x_own)
    grad_block = own_rows(grad_hidden) + norm_back(
        grad_normed, x_own * scale_own, scale_own, attn_gain
    )
    if ring.long:
        zeros = jnp.zeros((width, 2 * EXPERTS, units), BF)
        terms = terms[0].reshape(width, 2 * EXPERTS, split)
        terms = lax.dynamic_update_slice_in_dim(zeros, terms, ring.core * split, 2)
        sums = lax.psum_scatter(terms, "dp", scatter_dimension=0, tiled=True).astype(F32)
        grad_w_in_mine, grad_w_down_mine = sums[:, :EXPERTS], sums[:, EXPERTS:]
        terms = jnp.concatenate([dot32(x, y, TN).astype(BF) for x, y in attn_pairs], axis=1)
        attn_mine = lax.psum_scatter(terms, "dp", scatter_dimension=0, tiled=True)
        attn_mine = attn_mine.astype(F32)
    else:
        mine, away = ring_total(send.blocks(0)[0], send.sent, ring.core)
        grad_w_in_mine, grad_w_down_mine = combine(mine, ring.other_core(away), ring.core)
        attn_mine = send_a.total()
    summed_rel = summed[: rel_bias.shape[1], : rel_bias.shape[0]].T
    summed = summed[16:].reshape(2 + EXPERTS, width)
    return (
        result.astype(BF),
        grad_block,
        summed[0],
        attn_mine[:, : 3 * head_cols].reshape(w_qkv.shape),
        attn_mine[:, 3 * head_cols :],
        summed_rel,
        summed[1],
        summed[2:].T,
        grad_w_in_mine,
        grad_w_down_mine,
    )


def solution(mesh):
    placed = (
        P(("dp", "tensor"), None),
        P(),
        P("dp", None, "tensor"),
        P("dp", "tensor"),
        P(),
        P(),
        P(),
        P("dp", None, "tensor"),
        P("dp", None, "tensor"),
        P("dp", None),
        P("dp", None),
        P(),
        P(("dp", "tensor"), None),
    )
    return jax.shard_map(
        body,
        mesh=mesh,
        in_specs=placed,
        out_specs=(
            P(("dp", "tensor"), None),
            P(("dp", "tensor"), None),
            P(),
            P("dp", None, "tensor"),
            P("dp", "tensor"),
            P(),
            P(),
            P(),
            P("dp", None, "tensor"),
            P("dp", None, "tensor"),
        ),
        check_vma=False,
    )
```

```python
import jax
import jax.numpy as jnp
from jax import lax
from jax.experimental import pallas as pl
from jax.experimental.pallas import tpu as pltpu
from jax.sharding import PartitionSpec as P

HEAD_DIM = 64
EXPERTS = 2
CAP = 176

LONGEST = 16

EPS = 1e-06
NEG = -1e30
VMEM_BYTES = 12 << 20
RING_VMEM_BYTES = 6 << 20
EXPERT_VMEM_BYTES = 24 << 20
SMALL = pl.CostEstimate(flops=1, bytes_accessed=1, transcendentals=0)
HIGH = lax.Precision.HIGHEST
BF = jnp.bfloat16
F32 = jnp.float32


def ring_chip(place, chips):
    place = place % chips
    return jnp.where(place < chips // 2, 2 * place, 2 * (chips - 1 - place) + 1)


def ring_place(chip, chips):
    return jnp.where(chip % 2 == 0, chip // 2, chips - 1 - chip // 2)


class Ring:
    def __init__(self):
        self.n = lax.axis_size("dp")
        self.chips = self.n // 2
        order = [2 * i for i in range(self.chips // 2)]
        order = order + [c + 1 for c in reversed(order)]
        pairs = [
            (order[i] * 2 + k, order[(i + 1) % self.chips] * 2 + k)
            for i in range(self.chips)
            for k in (0, 1)
        ]
        self.right = pairs
        self.left = [(b, a) for a, b in pairs]
        self.swap = [(i, i ^ 1) for i in range(self.n)]
        index = lax.axis_index("dp")
        self.core = index % 2
        self.long = self.chips > LONGEST
        self.place = ring_place(index // 2, self.chips)
        reach = self.chips // 2
        self.distances = [0] + [d for s in range(1, reach) for d in (-s, s)] + [reach]
        self.slots = [reach] + [d for s in range(reach - 1, 0, -1) for d in (s, -s)] + [0]

    def other_core(self, x):
        return lax.ppermute(x, "dp", self.swap)

    def by_core(self, own, other, axis):
        return jnp.where(
            self.core == 0,
            jnp.concatenate([own, other], axis=axis),
            jnp.concatenate([other, own], axis=axis),
        )

    def slot_chips(self):
        return jnp.stack([self.chip_at(d) for d in self.slots])

    def chip_at(self, distance):
        return ring_chip(self.place + distance + self.chips, self.chips)


class Gather:
    def __init__(self, ring, shard, halves):
        self.ring, self.shard, self.halves = ring, shard, halves
        self.reach = ring.chips // 2
        self.pieces = [shard]
        self.sent = (shard, shard)
        self.steps = 0

    def step(self, *deps):
        ring, half = self.ring, self.shard.shape[1] // 2
        self.steps += 1
        r, l = after(self.sent, deps)
        if self.steps < self.reach:
            self.sent = (lax.ppermute(r, "dp", ring.right), lax.ppermute(l, "dp", ring.left))
        elif self.halves:
            self.sent = (
                lax.ppermute(r[:, :half], "dp", ring.right),
                lax.ppermute(l[:, half:], "dp", ring.left),
            )
        else:
            self.sent = (lax.ppermute(r, "dp", ring.right),)
        self.pieces += self.sent
        return self.sent

    def owners(self, begin=0, end=None):
        return jnp.stack([self.ring.chip_at(d) for d in self.ring.distances[begin:end]])


class Scatter:
    def __init__(self, ring, terms, rows):
        self.ring, self.rows = ring, rows
        self.reach = ring.chips // 2
        self.steps = 0
        self.slots = ring.slots
        self.terms = terms
        self.each = len(self.terms) > 2
        self.got = None if self.each else ring.other_core(self.terms[1])

    def blocks(self, distance):
        at = self.slots.index(distance)
        return [(self.terms[at], 0)] if self.each else [(self.terms[0], at), (self.got, at)]

    def step(self, *deps):
        ring = self.ring
        distance = self.reach - self.steps
        self.steps += 1
        if distance == self.reach:
            r, l = ring_far(self.blocks(distance), self.rows, self.each)
        else:
            sent = after(self.sent, deps)
            r, l = ring_add(
                self.blocks(distance), self.blocks(-distance), sent, self.rows, self.each
            )
        self.sent = (lax.ppermute(r, "dp", ring.right), lax.ppermute(l, "dp", ring.left))
        return self.sent

    def total(self):
        r, l = self.sent
        terms = [
            x[at * self.rows : (at + 1) * self.rows].astype(F32) for x, at in self.blocks(0)
        ]
        return sum(terms) + r.astype(F32) + l.astype(F32)


def outer(pairs, owners, rows, counts):
    height = pairs[0][0].shape[1]
    widths = [rhs.shape[1] for _, rhs in pairs]
    width = sum(widths)
    tile = 768

    def kernel(owners_ref, *refs):
        ins, outs, held_ref = refs[: 2 * len(pairs)], refs[2 * len(pairs) : -1], refs[-1]
        at = 0
        for i, wide in enumerate(widths):
            lhs = ins[2 * i][...]
            for start in range(0, wide, tile):
                size = min(tile, wide - start)
                held_ref[:, pl.ds(at, size)] = dot32(
                    lhs, ins[2 * i + 1][:, pl.ds(start, size)], TN
                ).astype(BF)
                at += size
        slot = 0
        for ref, number in zip(outs, counts):
            for to in range(number):
                source = pl.multiple_of(owners_ref[slot] * rows, 16)
                ref[pl.ds(to * rows, rows), :] = held_ref[pl.ds(source, rows), :]
                slot += 1

    inside = pl.BlockSpec(memory_space=pltpu.VMEM)
    return pl.pallas_call(
        kernel,
        out_shape=[jax.ShapeDtypeStruct((number * rows, width), BF) for number in counts],
        in_specs=[pl.BlockSpec(memory_space=pltpu.SMEM)] + [inside] * (2 * len(pairs)),
        out_specs=[inside] * len(counts),
        scratch_shapes=[pltpu.VMEM((height, width), BF)],
        compiler_params=pltpu.CompilerParams(vmem_limit_bytes=VMEM_BYTES),
        cost_estimate=SMALL,
        name="outer",
    )(owners, *[x for pair in pairs for x in pair])


def after(values, deps):
    if not deps:
        return values
    return lax.optimization_barrier((tuple(values), deps))[0]


def fetch(refs, places, rows, held_ref, sems):
    copies = [
        pltpu.make_async_copy(ref.at[pl.ds(at * rows, rows)], held_ref.at[i], sems.at[i])
        for i, (ref, at) in enumerate(zip(refs, places))
    ]
    for copy in copies:
        copy.start()
    for copy in copies:
        copy.wait()


def terms_spec(each):
    return pl.BlockSpec(memory_space=pltpu.HBM if each else pl.ANY)


def ring_far(blocks, rows, each):
    width = blocks[0][0].shape[1]
    half = width // 2
    number = len(blocks)

    def kernel(*refs):
        ins, (r_ref, l_ref, held_ref, sems) = refs[:number], refs[number:]
        fetch(ins, [at for _, at in blocks], rows, held_ref, sems)
        for k, ref in enumerate((r_ref, l_ref)):
            cols = pl.ds(k * half, half)
            ref[...] = sum(held_ref[i, :, cols].astype(F32) for i in range(number)).astype(BF)

    inside = pl.BlockSpec(memory_space=pltpu.VMEM)
    return pl.pallas_call(
        kernel,
        out_shape=[jax.ShapeDtypeStruct((rows, half), BF)] * 2,
        in_specs=[terms_spec(each)] * number,
        out_specs=[inside] * 2,
        scratch_shapes=[
            pltpu.VMEM((number, rows, width), BF), pltpu.SemaphoreType.DMA((number,))
        ],
        compiler_params=pltpu.CompilerParams(vmem_limit_bytes=RING_VMEM_BYTES),
        cost_estimate=SMALL,
        name="ring_far",
    )(*[x for x, _ in blocks])


def ring_add(right, left, sent, rows, each):
    width = right[0][0].shape[1]
    arrived = sent[0].shape[1]
    number = len(right)
    blocks = right + left

    def kernel(*refs):
        ins, got = refs[: 2 * number], refs[2 * number : 2 * number + 2]
        outs, (held_ref, sems) = refs[2 * number + 2 : 2 * number + 4], refs[2 * number + 4 :]
        fetch(ins, [at for _, at in blocks], rows, held_ref, sems)
        for k, out_ref in enumerate(outs):
            for part in range(width // arrived):
                cols = pl.ds(part * arrived, arrived)
                total = sum(
                    held_ref[k * number + i, :, cols].astype(F32) for i in range(number)
                )
                if arrived == width or part == k:
                    total = total + got[k][...].astype(F32)
                out_ref[:, cols] = total.astype(BF)

    inside = pl.BlockSpec(memory_space=pltpu.VMEM)
    return pl.pallas_call(
        kernel,
        out_shape=[jax.ShapeDtypeStruct((rows, width), BF)] * 2,
        in_specs=[terms_spec(each)] * (2 * number) + [inside] * 2,
        out_specs=[inside] * 2,
        scratch_shapes=[
            pltpu.VMEM((2 * number, rows, width), BF), pltpu.SemaphoreType.DMA((2 * number,))
        ],
        compiler_params=pltpu.CompilerParams(vmem_limit_bytes=RING_VMEM_BYTES),
        cost_estimate=SMALL,
        name="ring_add",
    )(*[x for x, _ in blocks], *sent)


def ring_total(block, sent, core):
    rows, width = sent[0].shape
    half = rows // 2

    def kernel(core_ref, own_ref, r_ref, l_ref, mine_ref, away_ref, held_ref, sems):
        fetch([own_ref], [block[1]], rows, held_ref, sems)
        begin = pl.multiple_of(core_ref[0] * half, 16)
        for at, out_ref in ((begin, mine_ref), (pl.multiple_of(half - begin, 16), away_ref)):
            here = pl.ds(at, half)
            out_ref[...] = (
                held_ref[0, here, :].astype(F32)
                + r_ref[here, :].astype(F32)
                + l_ref[here, :].astype(F32)
            )

    inside = pl.BlockSpec(memory_space=pltpu.VMEM)
    return pl.pallas_call(
        kernel,
        out_shape=[jax.ShapeDtypeStruct((half, width), F32)] * 2,
        in_specs=[pl.BlockSpec(memory_space=pltpu.SMEM), terms_spec(True), inside, inside],
        out_specs=[inside] * 2,
        scratch_shapes=[pltpu.VMEM((1, rows, width), BF), pltpu.SemaphoreType.DMA((1,))],
        compiler_params=pltpu.CompilerParams(vmem_limit_bytes=RING_VMEM_BYTES),
        cost_estimate=SMALL,
        name="ring_total",
    )(core[None], block[0], *sent)


def combine(mine, got, core):
    rows, width = mine.shape
    split = width // 2 // EXPERTS

    def kernel(core_ref, mine_ref, got_ref, *outs):
        for k, ref in enumerate((mine_ref, got_ref)):
            first = (1 - core_ref[0]) if k else core_ref[0]
            at = pl.ds(pl.multiple_of(first * split, 128), split)
            for i, out_ref in enumerate(outs):
                for e in range(EXPERTS):
                    out_ref[:, e, at] = ref[:, pl.ds((i * EXPERTS + e) * split, split)]

    inside = pl.BlockSpec(memory_space=pltpu.VMEM)
    return pl.pallas_call(
        kernel,
        out_shape=[jax.ShapeDtypeStruct((rows, EXPERTS, 2 * split), F32)] * 2,
        in_specs=[pl.BlockSpec(memory_space=pltpu.SMEM)] + [inside] * 2,
        out_specs=[inside] * 2,
        compiler_params=pltpu.CompilerParams(vmem_limit_bytes=VMEM_BYTES),
        cost_estimate=SMALL,
        name="combine",
    )(core[None], mine, got)


def place(pieces, owners, chips):
    rows, width = pieces[0].shape
    half = width // 2
    number = len(pieces)

    def kernel(owners_ref, *refs):
        ins, outs, sems = refs[:number], refs[number:-1], refs[-1]
        copies = []
        for i, ref in enumerate(ins):
            target = pl.ds(pl.multiple_of(owners_ref[i] * rows, 16), rows)
            for k, out_ref in enumerate(outs):
                source = ref.at[:, pl.ds(k * half, half)]
                copies.append(
                    pltpu.make_async_copy(source, out_ref.at[target], sems.at[len(copies)])
                )
        for copy in copies:
            copy.start()
        for copy in copies:
            copy.wait()

    return pl.pallas_call(
        kernel,
        out_shape=[jax.ShapeDtypeStruct((chips * rows, half), BF)] * 2,
        in_specs=[pl.BlockSpec(memory_space=pltpu.SMEM)]
        + [pl.BlockSpec(memory_space=pl.ANY)] * number,
        out_specs=[pl.BlockSpec(memory_space=pltpu.VMEM)] * 2,
        scratch_shapes=[pltpu.SemaphoreType.DMA((2 * number,))],
        compiler_params=pltpu.CompilerParams(vmem_limit_bytes=RING_VMEM_BYTES),
        cost_estimate=SMALL,
        name="place",
    )(owners, *pieces)


def assemble(pieces, owners):
    rows, width = pieces[0].shape
    number = len(pieces)

    def kernel(owners_ref, *refs):
        out_ref, sems = refs[number:]
        copies = []
        for i in range(number):
            target = out_ref.at[pl.ds(pl.multiple_of(owners_ref[i] * rows, 16), rows)]
            copies.append(pltpu.make_async_copy(refs[i], target, sems.at[i]))
        for copy in copies:
            copy.start()
        for copy in copies:
            copy.wait()

    return pl.pallas_call(
        kernel,
        out_shape=jax.ShapeDtypeStruct((number * rows, width), BF),
        in_specs=[pl.BlockSpec(memory_space=pltpu.SMEM)]
        + [pl.BlockSpec(memory_space=pl.ANY)] * number,
        out_specs=pl.BlockSpec(memory_space=pltpu.VMEM),
        scratch_shapes=[pltpu.SemaphoreType.DMA((number,))],
        compiler_params=pltpu.CompilerParams(vmem_limit_bytes=VMEM_BYTES),
        cost_estimate=SMALL,
        name="assemble",
    )(owners, *pieces)


def gelu_and_slope(v):
    c = 0.7978845608028654
    t = jnp.tanh(c * (v + 0.044715 * (v * v * v)))
    slope = 0.5 * (1.0 + t) + 0.5 * v * (1.0 - t * t) * c * (1.0 + 3 * 0.044715 * (v * v))
    return 0.5 * v * (1.0 + t), slope


def expert_rows(own_ref, got_ref, e, begin, width):
    at = (pl.ds(e * CAP, CAP), pl.ds(begin, width))
    return jnp.concatenate([own_ref[at], got_ref[at]], axis=0)


def expert_layers(own, got, state, last, last_owner, slots, rows_out):
    filled, d = own.shape[0], own.shape[1] // 2
    width = 2 * state[0].shape[1]
    units = width // 2 // EXPERTS
    chips = slots.shape[0]
    number = len(last)

    def kernel(last_ref, slots_ref, own_hbm, got_hbm, *refs):
        ins, refs = refs[2 : 2 + number], refs[2 + number :]
        mine_ref, away_ref, outs, refs = refs[0], refs[1], refs[2 : 2 + chips], refs[2 + chips :]
        in_ref, down_ref, own_ref, got_ref, held_ref, sems, out_sems = refs
        weights = (in_ref, down_ref)
        pairs = ((own_hbm, own_ref), (got_hbm, got_ref))
        copies = [pltpu.make_async_copy(*pair, sems.at[i]) for i, pair in enumerate(pairs)]
        for copy in copies:
            copy.start()
        for copy in copies:
            copy.wait()
        for ref, weight in zip(ins, weights):
            rows = ref.shape[0]
            weight[pl.ds(pl.multiple_of(last_ref[0] * rows, 16), rows), :] = ref[...]
        for e in range(EXPERTS):
            cols = pl.ds(e * units, units)
            w_i, w_d = in_ref[:, cols], down_ref[:, cols]
            x, g = (expert_rows(own_ref, got_ref, e, k * d, d) for k in range(2))
            active, slope = gelu_and_slope(dot32(x, w_i, NN))
            active = active.astype(BF)
            grad_pre = (dot32(g, w_d, NN) * slope).astype(BF)
            back = dot32(active, w_d, NT).astype(BF)
            sent = dot32(grad_pre, w_i, NT).astype(BF)
            for k, ref in enumerate((mine_ref, away_ref)):
                ref[pl.ds(e * CAP, CAP), pl.ds(0, d)] = back[k * CAP : (k + 1) * CAP]
                ref[pl.ds(e * CAP, CAP), pl.ds(d, d)] = sent[k * CAP : (k + 1) * CAP]
            held_ref[:, pl.ds(e * units, units)] = dot32(x, grad_pre, TN).astype(BF)
            held_ref[:, pl.ds((EXPERTS + e) * units, units)] = dot32(g, active, TN).astype(BF)
        copies = []
        for slot in range(chips):
            begin = pl.multiple_of(slots_ref[slot] * rows_out, 16)
            source = held_ref.at[pl.ds(begin, rows_out)]
            copies.append(pltpu.make_async_copy(source, outs[slot], out_sems.at[slot]))
        for copy in copies:
            copy.start()
        for copy in copies:
            copy.wait()

    inside = pl.BlockSpec(memory_space=pltpu.VMEM)
    outside = pl.BlockSpec(memory_space=pltpu.HBM)
    scalars = pl.BlockSpec(memory_space=pltpu.SMEM)
    mine, away, *terms, _, _ = pl.pallas_call(
        kernel,
        out_shape=[jax.ShapeDtypeStruct((filled, 2 * d), BF)] * 2
        + [jax.ShapeDtypeStruct((rows_out, width), BF)] * chips
        + [jax.ShapeDtypeStruct((d, width // 2), BF)] * 2,
        in_specs=[scalars] * 2 + [outside] * 2 + [inside] * (2 + number),
        out_specs=[inside] * 2 + [outside] * chips + [inside] * 2,
        input_output_aliases={4: 2 + chips, 5: 3 + chips},
        scratch_shapes=[pltpu.VMEM((filled, 2 * d), BF)] * 2
        + [
            pltpu.VMEM((d, width), BF),
            pltpu.SemaphoreType.DMA((2,)),
            pltpu.SemaphoreType.DMA((chips,)),
        ],
        compiler_params=pltpu.CompilerParams(vmem_limit_bytes=EXPERT_VMEM_BYTES),
        cost_estimate=SMALL,
        name="expert_layers",
    )(last_owner[None], slots, own, got, *state, *last)
    return mine, away, terms


def interleave(own, other, core, rows):
    chips, width = own.shape[0] // rows, own.shape[1]

    def kernel(core_ref, own_ref, other_ref, out_ref):
        for k, ref in enumerate((own_ref, other_ref)):
            first = (1 - core_ref[0]) if k else core_ref[0]
            for chip in range(chips):
                target = pl.multiple_of((2 * chip + first) * rows, 16)
                out_ref[pl.ds(target, rows), :] = ref[pl.ds(chip * rows, rows), :]

    inside = pl.BlockSpec(memory_space=pltpu.VMEM)
    return pl.pallas_call(
        kernel,
        out_shape=jax.ShapeDtypeStruct((2 * chips * rows, width), BF),
        in_specs=[pl.BlockSpec(memory_space=pltpu.SMEM), inside, inside],
        out_specs=inside,
        compiler_params=pltpu.CompilerParams(vmem_limit_bytes=VMEM_BYTES),
        cost_estimate=SMALL,
        name="interleave",
    )(core[None], own, other)


def swap_tensor(x):
    return lax.ppermute(x, "tensor", [(0, 1), (1, 0)])


def whole_rows(own, other, rank):
    return jnp.where(
        rank == 0, jnp.concatenate([own, other], axis=0), jnp.concatenate([other, own], axis=0)
    )


def sum_pairs(x, step):
    pairs = [(i, i ^ step) for i in range(lax.axis_size("dp"))]
    return x + lax.ppermute(x, "dp", pairs)


def rms_scale(rows):
    return lax.rsqrt(jnp.mean(rows * rows, axis=-1, keepdims=True) + EPS)


def norm_back(grad, normed, scale, gain):
    weighted = grad * gain
    return scale * (weighted - normed * jnp.mean(weighted * normed, axis=-1, keepdims=True))


def dot32(a, b, dims):
    return lax.dot_general(a, b, (dims, ((), ())), preferred_element_type=F32)


NN = ((1,), (0,))
NT = ((1,), (1,))
TN = ((0,), (0,))


def attention_forward(x, gain, weights, by_offset, seq_col, seq_row):
    count, d = x.shape
    head_cols = weights.shape[1] // 4
    heads = head_cols // HEAD_DIM
    scale = HEAD_DIM ** (-0.5)
    lanes = by_offset.shape[1]

    def kernel(x_ref, gain_ref, w_ref, off_ref, col_ref, row_ref, *outs):
        normed_ref, scale_ref, proj_ref, p_ref, context_ref, part_ref = outs
        rows = x_ref[...].astype(F32)
        r = lax.rsqrt(jnp.mean(rows * rows, axis=-1, keepdims=True) + EPS)
        scale_ref[...] = r
        normed = (rows * r * gain_ref[...]).astype(BF)
        normed_ref[...] = normed
        for s in range(3):
            at = pl.ds(s * head_cols, head_cols)
            proj_ref[:, at] = dot32(normed, w_ref[:, at], NN).astype(BF)
        same = col_ref[...] == row_ref[...]
        for h in range(heads):
            q = proj_ref[:, pl.ds(h * HEAD_DIM, HEAD_DIM)]
            k = proj_ref[:, pl.ds(head_cols + h * HEAD_DIM, HEAD_DIM)]
            v = proj_ref[:, pl.ds(2 * head_cols + h * HEAD_DIM, HEAD_DIM)]
            line = jnp.broadcast_to(off_ref[pl.ds(h, 1), :], (count, lanes))
            bias = pltpu.roll(line, lanes - (count - 1), 1, stride=1, stride_axis=0)[:, :count]
            scores = jnp.where(same, dot32(q, k, NT) * scale + bias, NEG)
            expo = jnp.exp(scores - jnp.max(scores, axis=-1, keepdims=True))
            p = expo / jnp.sum(expo, axis=-1, keepdims=True)
            p_ref[h] = p
            context_ref[:, pl.ds(h * HEAD_DIM, HEAD_DIM)] = dot32(p.astype(BF), v, NN).astype(BF)
        out_w = w_ref[:, pl.ds(3 * head_cols, head_cols)]
        part_ref[...] = dot32(context_ref[...], out_w, NT).astype(BF)

    inside = pl.BlockSpec(memory_space=pltpu.VMEM)
    return pl.pallas_call(
        kernel,
        out_shape=(
            jax.ShapeDtypeStruct((count, d), BF),
            jax.ShapeDtypeStruct((count, 1), F32),
            jax.ShapeDtypeStruct((count, 3 * head_cols), BF),
            jax.ShapeDtypeStruct((heads, count, count), F32),
            jax.ShapeDtypeStruct((count, head_cols), BF),
            jax.ShapeDtypeStruct((count, d), BF),
        ),
        in_specs=[inside] * 6,
        out_specs=(inside,) * 6,
        compiler_params=pltpu.CompilerParams(vmem_limit_bytes=VMEM_BYTES),
        cost_estimate=SMALL,
        name="attention_forward",
    )(x, gain, weights, by_offset, seq_col, seq_row)


def attention_backward(low, other, hidden, scales, gain, out_grad, weights, proj, p_full, lanes):
    count, d = low.shape
    head_cols = weights.shape[1] // 4
    heads = head_cols // HEAD_DIM
    scale = HEAD_DIM ** (-0.5)

    def kernel(low_ref, other_ref, hidden_ref, scales_ref, gain_ref, g_ref, w_ref, proj_ref, p_ref,
               hidden_grad_ref, grad_ref, out_ref, sums_ref, gc_ref):
        r2 = scales_ref[:, 3:4]
        n = hidden_ref[...] * r2
        u = (low_ref[...].astype(F32) + other_ref[...].astype(F32)) * gain_ref[...]
        total = g_ref[...].astype(F32) + r2 * (u - n * jnp.mean(u * n, axis=-1, keepdims=True))
        hidden_grad_ref[...] = total
        grad_ref[...] = total.astype(BF)
        out_w = w_ref[:, pl.ds(3 * head_cols, head_cols)]
        gc_ref[...] = dot32(grad_ref[...], out_w, NN).astype(BF)
        down = lax.broadcasted_iota(jnp.int32, (count, count), 0)
        across = lax.broadcasted_iota(jnp.int32, (count, count), 1)
        flip = (down + across == count - 1).astype(F32).astype(BF)
        for h in range(heads):
            at = [pl.ds(s * head_cols + h * HEAD_DIM, HEAD_DIM) for s in range(3)]
            q, k, v = proj_ref[:, at[0]], proj_ref[:, at[1]], proj_ref[:, at[2]]
            p = p_ref[h]
            gc = gc_ref[:, at[0]]
            dp = dot32(gc, v, NT)
            ds = (p * (dp - jnp.sum(p * dp, axis=-1, keepdims=True))).astype(BF)
            out_ref[:, at[0]] = (dot32(ds, k, NN) * scale).astype(BF)
            out_ref[:, at[1]] = (dot32(ds, q, TN) * scale).astype(BF)
            out_ref[:, at[2]] = dot32(p.astype(BF), gc, TN).astype(BF)
            turned = dot32(ds, flip, TN)
            wide = jnp.concatenate([turned, jnp.zeros((count, lanes - count), F32)], axis=1)
            rolled = pltpu.roll(wide, 0, 1, stride=1, stride_axis=0)
            sums_ref[pl.ds(h, 1), :] = jnp.sum(rolled, axis=0, keepdims=True)

    inside = pl.BlockSpec(memory_space=pltpu.VMEM)
    return pl.pallas_call(
        kernel,
        out_shape=(
            jax.ShapeDtypeStruct((count, d), F32),
            jax.ShapeDtypeStruct((count, d), BF),
            jax.ShapeDtypeStruct((count, 3 * head_cols), BF),
            jax.ShapeDtypeStruct((heads, lanes), F32),
        ),
        in_specs=[inside] * 9,
        out_specs=(inside,) * 4,
        scratch_shapes=[pltpu.VMEM((count, head_cols), BF)],
        compiler_params=pltpu.CompilerParams(vmem_limit_bytes=VMEM_BYTES),
        cost_estimate=SMALL,
        name="attention_backward",
    )(low, other, hidden, scales, gain, out_grad, weights, proj, p_full)


def route(x, part, other, gain, w_router, expert_col, flat, out_grad):
    count, d = x.shape

    def kernel(x_ref, part_ref, other_ref, gain_ref, w_ref, expert_ref, flat_ref, g_ref,
               hidden_ref, out_ref, scales_ref, blocks_ref, sem):
        hidden = x_ref[...].astype(F32) + (part_ref[...].astype(F32) + other_ref[...].astype(F32))
        hidden_ref[...] = hidden
        r2 = lax.rsqrt(jnp.mean(hidden * hidden, axis=-1, keepdims=True) + EPS)
        mixed = hidden * r2 * gain_ref[...]
        logits = [
            jnp.sum(mixed * w_ref[e : e + 1, :], axis=-1, keepdims=True) for e in range(EXPERTS)
        ]
        top = jnp.maximum(logits[0], logits[1])
        expo = [jnp.exp(v - top) for v in logits]
        probs = [v / (expo[0] + expo[1]) for v in expo]
        hits = [(expert_ref[...] == e).astype(F32) for e in range(EXPERTS)]
        gate = probs[0] * hits[0] + probs[1] * hits[1]
        lane = lax.broadcasted_iota(jnp.int32, (count, 128), 1)
        columns = [gate] + [gate * (h - p) for h, p in zip(hits, probs)] + [r2]
        scales_ref[...] = sum(jnp.where(lane == i, v, 0.0) for i, v in enumerate(columns))
        slots = lax.broadcasted_iota(jnp.int32, (EXPERTS * CAP, count), 0)
        chosen = (slots == flat_ref[...]).astype(F32).astype(BF)
        blocks_ref[:, pl.ds(0, d)] = dot32(chosen, mixed.astype(BF), NN).astype(BF)
        grad_routed = (gate * g_ref[...].astype(F32)).astype(BF)
        blocks_ref[:, pl.ds(d, d)] = dot32(chosen, grad_routed, NN).astype(BF)
        copy = pltpu.make_async_copy(blocks_ref, out_ref, sem)
        copy.start()
        copy.wait()

    inside = pl.BlockSpec(memory_space=pltpu.VMEM)
    return pl.pallas_call(
        kernel,
        out_shape=(
            jax.ShapeDtypeStruct((count, d), F32),
            jax.ShapeDtypeStruct((EXPERTS * CAP, 2 * d), BF),
            jax.ShapeDtypeStruct((count, 128), F32),
        ),
        in_specs=[inside] * 8,
        out_specs=(inside, pl.BlockSpec(memory_space=pltpu.HBM), inside),
        scratch_shapes=[pltpu.VMEM((EXPERTS * CAP, 2 * d), BF), pltpu.SemaphoreType.DMA],
        compiler_params=pltpu.CompilerParams(vmem_limit_bytes=VMEM_BYTES),
        cost_estimate=SMALL,
        name="route",
    )(x, part, other, gain, w_router, expert_col, flat, out_grad)


def rows_back(mine, got, hidden, scales, gain, w_router, flat, out_grad):
    count, d = hidden.shape

    def kernel(mine_ref, got_ref, hidden_ref, scales_ref, gain_ref, w_ref, flat_ref, g_ref,
               mixed_ref, routed_ref, gains_ref):
        sums = (mine_ref[...].astype(F32) + got_ref[...].astype(F32)).astype(BF)
        slots = lax.broadcasted_iota(jnp.int32, (count, EXPERTS * CAP), 1)
        chosen = (slots == flat_ref[...]).astype(F32).astype(BF)
        routed = dot32(chosen, sums[:, :d], NN)
        gate, r2 = scales_ref[:, 0:1], scales_ref[:, 3:4]
        routed_ref[...] = (gate * routed).astype(BF)
        gate_part = jnp.sum(g_ref[...].astype(F32) * routed, axis=-1, keepdims=True)
        grad_logits = [gate_part * scales_ref[:, 1 + e : 2 + e] for e in range(EXPERTS)]
        part = dot32(chosen, sums[:, d:], NN)
        part = part + sum(grad_logits[e] * w_ref[e : e + 1, :] for e in range(EXPERTS))
        mixed_ref[...] = part.astype(BF)
        n = hidden_ref[...] * r2
        gains_ref[0:1, :] = jnp.sum(part * n, axis=0, keepdims=True)
        mixed = n * gain_ref[...]
        for e in range(EXPERTS):
            gains_ref[1 + e : 2 + e, :] = jnp.sum(mixed * grad_logits[e], axis=0, keepdims=True)
        gains_ref[1 + EXPERTS :, :] = jnp.zeros((7 - EXPERTS, d), F32)

    inside = pl.BlockSpec(memory_space=pltpu.VMEM)
    return pl.pallas_call(
        kernel,
        out_shape=(
            jax.ShapeDtypeStruct((count, d), BF),
            jax.ShapeDtypeStruct((count, d), BF),
            jax.ShapeDtypeStruct((8, d), F32),
        ),
        in_specs=[inside] * 8,
        out_specs=(inside,) * 3,
        compiler_params=pltpu.CompilerParams(vmem_limit_bytes=VMEM_BYTES),
        cost_estimate=SMALL,
        name="rows_back",
    )(mine, got, hidden, scales, gain, w_router, flat, out_grad)


def input_back(grad, weights, x, sums, bucket_hits, gains, rank):
    count, d = x.shape
    heads, lanes = sums.shape
    buckets = bucket_hits.shape[1]
    each = d // 128

    def kernel(rank_ref, grad_ref, w_ref, x_ref, sums_ref, hits_ref, gains_ref, low_ref, line_ref):
        part = dot32(grad_ref[...], w_ref[:, pl.ds(0, grad_ref.shape[1])], NT)
        low_ref[...] = part.astype(BF)
        rows = x_ref[...].astype(F32)
        n = rows * lax.rsqrt(jnp.mean(rows * rows, axis=-1, keepdims=True) + EPS)
        vectors = [jnp.sum(part * n, axis=0, keepdims=True)]
        vectors += [gains_ref[k : k + 1, :] for k in range(1 + EXPERTS)]
        for k, vector in enumerate(vectors):
            for j in range(each):
                line_ref[pl.ds(16 + k * each + j, 1), :] = vector[:, j * 128 : (j + 1) * 128]
        rel = jnp.dot(sums_ref[...], hits_ref[...], precision=HIGH, preferred_element_type=F32)
        rel = jnp.concatenate([rel, jnp.zeros((heads, 128 - buckets), F32)], axis=1)
        line_ref[0:16, :] = jnp.zeros((16, 128), F32)
        for k in range(2):
            line_ref[pl.ds(k * heads, heads), :] = jnp.where(rank_ref[0] == k, rel, 0.0)

    inside = pl.BlockSpec(memory_space=pltpu.VMEM)
    return pl.pallas_call(
        kernel,
        out_shape=(
            jax.ShapeDtypeStruct((count, d), BF),
            jax.ShapeDtypeStruct((16 + (2 + EXPERTS) * each, 128), F32),
        ),
        in_specs=[pl.BlockSpec(memory_space=pltpu.SMEM)] + [inside] * 6,
        out_specs=(inside,) * 2,
        compiler_params=pltpu.CompilerParams(vmem_limit_bytes=VMEM_BYTES),
        cost_estimate=SMALL,
        name="input_back",
    )(rank[None], grad, weights, x, sums, bucket_hits, gains)


def body(
    block_in,
    attn_gain,
    w_qkv,
    w_out,
    rel_bias,
    moe_gain,
    w_router,
    w_in,
    w_down,
    seq_lengths,
    expert_ids,
    rel_table,
    out_grad,
):
    rows_local, width = block_in.shape
    rank = lax.axis_index("tensor")
    ring = Ring()
    shard = w_out.shape[0]
    head_cols = w_out.shape[1]
    units = w_in.shape[2]
    heads_local = head_cols // HEAD_DIM
    count = 2 * rows_local

    attn_shard = jnp.concatenate([w_qkv.reshape(shard, 3 * head_cols), w_out], axis=1)
    x_other, g_other = swap_tensor(block_in), swap_tensor(out_grad)
    split = units // 2

    def unit_half(w, core):
        return lax.dynamic_slice_in_dim(w, core * split, split, axis=2)

    if not ring.long:
        ring_a = Gather(ring, attn_shard, False)
        a1 = ring_a.step()
        own_half, other_half = (
            jnp.concatenate(
                [unit_half(w, core).reshape(shard, EXPERTS * split) for w in (w_in, w_down)],
                axis=1,
            )
            for core in (ring.core, 1 - ring.core)
        )
        got_half = ring.other_core(other_half)
        a2 = ring_a.step()
        ring_b = Gather(ring, ring.by_core(own_half, got_half, 0), True)
        a3 = ring_a.step()
        a4 = ring_a.step()
        ring_b.step(*a3, x_other, g_other)
        own_a = assemble(ring_a.pieces, ring_a.owners())
        other_a = ring.other_core(own_a)
        attn_all = interleave(own_a, other_a, ring.core, shard)
    else:
        attn_all = lax.all_gather(attn_shard, "dp", axis=0, tiled=True)
        in_all, down_all = (
            unit_half(lax.all_gather(w, "dp", axis=0, tiled=True), ring.core).reshape(
                -1, EXPERTS * split
            )
            for w in (w_in, w_down)
        )
    x_low = whole_rows(block_in, x_other, rank)
    g_low = whole_rows(out_grad, g_other, rank)

    places = jnp.arange(count, dtype=jnp.int32)
    ends = jnp.cumsum(seq_lengths[0])
    seq_ids = jnp.sum((places[:, None] >= ends[None, :]).astype(jnp.int32), axis=1)
    bias_local = lax.dynamic_slice_in_dim(rel_bias, rank * heads_local, heads_local, 1)
    bucket_hits = (
        rel_table[:, None] == jnp.arange(rel_bias.shape[0], dtype=jnp.int32)[None, :]
    ).astype(F32)
    by_offset = jnp.dot(bucket_hits, bias_local, precision=HIGH)
    lanes = 2 * count
    by_offset = jnp.pad(by_offset.T, ((0, 0), (0, lanes - by_offset.shape[0])))
    normed_one, _, projected, p_full, context, attn_part = attention_forward(
        x_low, attn_gain[None, :], attn_all, by_offset, seq_ids[:, None], seq_ids[None, :]
    )
    if not ring.long:
        ring_b.step()
        ring_b.step(attn_part)
    attn_other = swap_tensor(attn_part)
    expert_col = expert_ids[:, 0]
    hits = (
        expert_col[:, None] == jnp.arange(EXPERTS, dtype=jnp.int32)[None, :]
    ).astype(jnp.int32)
    flat = expert_col * CAP + jnp.sum(jnp.cumsum(hits, axis=0) * hits, axis=1) - 1
    gain_row, router_rows = moe_gain[None, :], w_router.T
    hidden, own_blocks, scales = route(
        x_low, attn_part, attn_other, gain_row, router_rows, expert_ids, flat[None, :], g_low
    )
    if not ring.long:
        got_blocks = ring.other_core(own_blocks)
        state = place(ring_b.pieces, ring_b.owners(0, ring.chips - 1), ring.chips)
        last = ring_b.step(got_blocks)
        mine, away, terms = expert_layers(
            own_blocks,
            got_blocks,
            state,
            last,
            ring.chip_at(ring.chips // 2),
            ring.slot_chips(),
            2 * shard,
        )
        send = Scatter(ring, terms, 2 * shard)
        c1 = send.step()
    else:
        first = jnp.zeros((1,), jnp.int32)
        mine, away, terms = expert_layers(
            own_blocks,
            ring.other_core(own_blocks),
            (in_all, down_all),
            (),
            first[0],
            first,
            width,
        )
    got_sums = ring.other_core(away)
    mixed_low, routed_low, gains = rows_back(
        mine, got_sums, hidden, scales, gain_row, router_rows, flat[:, None], g_low
    )
    if not ring.long:
        c2 = send.step(mixed_low)
    mixed_other = swap_tensor(mixed_low)
    if not ring.long:
        (mixed_other,) = after((mixed_other,), c1)

    def own_rows(x):
        return lax.dynamic_slice_in_dim(x, rank * rows_local, rows_local, 0)

    def other_rows(x):
        return lax.dynamic_slice_in_dim(x, (1 - rank) * rows_local, rows_local, 0)

    routed_other = swap_tensor(other_rows(routed_low))
    result = own_rows(hidden) + (
        own_rows(routed_low).astype(F32) + routed_other.astype(F32)
    )
    grad_hidden, grad_attended, grad_projected, offset_sums = attention_backward(
        mixed_low, mixed_other, hidden, scales, gain_row, g_low, attn_all, projected, p_full, lanes
    )

    attn_pairs = [(normed_one, grad_projected), (grad_attended, context)]
    if not ring.long:
        attn_pairs[0] = (normed_one, after((grad_projected,), c2)[0])
        chips = ring.slot_chips()
        owners = jnp.concatenate([chips * 2 + ring.core, chips * 2 + 1 - ring.core])
        send_a = Scatter(ring, outer(attn_pairs, owners, shard, [ring.chips] * 2), shard)
        c3 = send.step()
        a1 = send_a.step()
    hits_wide = jnp.pad(bucket_hits, ((0, lanes - bucket_hits.shape[0]), (0, 0)))
    normed_low, line = input_back(
        grad_projected, attn_all, x_low, offset_sums, hits_wide, gains, rank
    )
    normed_other = swap_tensor(other_rows(normed_low))
    line = line + swap_tensor(line)
    line = line + ring.other_core(line)
    if not ring.long:
        c4 = send.step(*a1)
        a2 = send_a.step(*c3)
        a3 = send_a.step(*c4)
        (line,) = after((line,), c4)
        line = sum_pairs(line, 2)
        mine, away = ring_total(send.blocks(0)[0], send.sent, ring.core)
        line = sum_pairs(line, 4)
        (line,) = after((line,), a3)
    else:
        line = sum_pairs(sum_pairs(line, 2), 4)
    step = 8
    while step < ring.n:
        line = sum_pairs(line, step)
        step *= 2
    summed = line
    grad_normed = own_rows(normed_low).astype(F32) + normed_other.astype(F32)
    x_own = block_in.astype(F32)
    scale_own = rms_scale(x_own)
    grad_block = own_rows(grad_hidden) + norm_back(
        grad_normed, x_own * scale_own, scale_own, attn_gain
    )
    if ring.long:
        zeros = jnp.zeros((width, 2 * EXPERTS, units), BF)
        terms = terms[0].reshape(width, 2 * EXPERTS, split)
        terms = lax.dynamic_update_slice_in_dim(zeros, terms, ring.core * split, 2)
        sums = lax.psum_scatter(terms, "dp", scatter_dimension=0, tiled=True).astype(F32)
        grad_w_in_mine, grad_w_down_mine = sums[:, :EXPERTS], sums[:, EXPERTS:]
        terms = jnp.concatenate([dot32(x, y, TN).astype(BF) for x, y in attn_pairs], axis=1)
        attn_mine = lax.psum_scatter(terms, "dp", scatter_dimension=0, tiled=True)
        attn_mine = attn_mine.astype(F32)
    else:
        send_a.step(mine, grad_block)
        grad_w_in_mine, grad_w_down_mine = combine(mine, ring.other_core(away), ring.core)
        attn_mine = send_a.total()
    summed_rel = summed[: rel_bias.shape[1], : rel_bias.shape[0]].T
    summed = summed[16:].reshape(2 + EXPERTS, width)
    return (
        result.astype(BF),
        grad_block,
        summed[0],
        attn_mine[:, : 3 * head_cols].reshape(w_qkv.shape),
        attn_mine[:, 3 * head_cols :],
        summed_rel,
        summed[1],
        summed[2:].T,
        grad_w_in_mine,
        grad_w_down_mine,
    )


def solution(mesh):
    placed = (
        P(("dp", "tensor"), None),
        P(),
        P("dp", None, "tensor"),
        P("dp", "tensor"),
        P(),
        P(),
        P(),
        P("dp", None, "tensor"),
        P("dp", None, "tensor"),
        P("dp", None),
        P("dp", None),
        P(),
        P(("dp", "tensor"), None),
    )
    return jax.shard_map(
        body,
        mesh=mesh,
        in_specs=placed,
        out_specs=(
            P(("dp", "tensor"), None),
            P(("dp", "tensor"), None),
            P(),
            P("dp", None, "tensor"),
            P("dp", "tensor"),
            P(),
            P(),
            P(),
            P("dp", None, "tensor"),
            P("dp", None, "tensor"),
        ),
        check_vma=False,
    )
```

```python
import jax
import jax.numpy as jnp
from jax import lax
from jax.experimental import pallas as pl
from jax.experimental.pallas import tpu as pltpu
from jax.sharding import PartitionSpec as P

HEAD_DIM = 64
EXPERTS = 2
CAP = 176

LONGEST = 16

EPS = 1e-06
NEG = -1e30
VMEM_BYTES = 12 << 20
RING_VMEM_BYTES = 6 << 20
EXPERT_VMEM_BYTES = 24 << 20
SMALL = pl.CostEstimate(flops=1, bytes_accessed=1, transcendentals=0)
HIGH = lax.Precision.HIGHEST
BF = jnp.bfloat16
F32 = jnp.float32


def ring_chip(place, chips):
    place = place % chips
    return jnp.where(place < chips // 2, 2 * place, 2 * (chips - 1 - place) + 1)


def ring_place(chip, chips):
    return jnp.where(chip % 2 == 0, chip // 2, chips - 1 - chip // 2)


class Ring:
    def __init__(self):
        self.n = lax.axis_size("dp")
        self.chips = self.n // 2
        order = [2 * i for i in range(self.chips // 2)]
        order = order + [c + 1 for c in reversed(order)]
        pairs = [
            (order[i] * 2 + k, order[(i + 1) % self.chips] * 2 + k)
            for i in range(self.chips)
            for k in (0, 1)
        ]
        self.right = pairs
        self.left = [(b, a) for a, b in pairs]
        self.swap = [(i, i ^ 1) for i in range(self.n)]
        index = lax.axis_index("dp")
        self.core = index % 2
        self.long = self.chips > LONGEST
        self.place = ring_place(index // 2, self.chips)
        reach = self.chips // 2
        self.distances = [0] + [d for s in range(1, reach) for d in (-s, s)] + [reach]
        self.slots = [reach] + [d for s in range(reach - 1, 0, -1) for d in (s, -s)] + [0]

    def other_core(self, x):
        return lax.ppermute(x, "dp", self.swap)

    def by_core(self, own, other, axis):
        return jnp.where(
            self.core == 0,
            jnp.concatenate([own, other], axis=axis),
            jnp.concatenate([other, own], axis=axis),
        )

    def slot_chips(self):
        return jnp.stack([self.chip_at(d) for d in self.slots])

    def chip_at(self, distance):
        return ring_chip(self.place + distance + self.chips, self.chips)


class Gather:
    def __init__(self, ring, shard, halves):
        self.ring, self.shard, self.halves = ring, shard, halves
        self.reach = ring.chips // 2
        self.pieces = [shard]
        self.sent = (shard, shard)
        self.steps = 0

    def step(self, *deps):
        ring, half = self.ring, self.shard.shape[1] // 2
        self.steps += 1
        r, l = after(self.sent, deps)
        if self.steps < self.reach:
            self.sent = (lax.ppermute(r, "dp", ring.right), lax.ppermute(l, "dp", ring.left))
        elif self.halves:
            self.sent = (
                lax.ppermute(r[:, :half], "dp", ring.right),
                lax.ppermute(l[:, half:], "dp", ring.left),
            )
        else:
            self.sent = (lax.ppermute(r, "dp", ring.right),)
        self.pieces += self.sent
        return self.sent

    def owners(self, begin=0, end=None):
        return jnp.stack([self.ring.chip_at(d) for d in self.ring.distances[begin:end]])


class Scatter:
    def __init__(self, ring, terms, rows):
        self.ring, self.rows = ring, rows
        self.reach = ring.chips // 2
        self.steps = 0
        self.slots = ring.slots
        self.terms = terms
        self.each = len(self.terms) > 2
        self.got = None if self.each else ring.other_core(self.terms[1])

    def blocks(self, distance):
        at = self.slots.index(distance)
        return [(self.terms[at], 0)] if self.each else [(self.terms[0], at), (self.got, at)]

    def step(self, *deps):
        ring = self.ring
        distance = self.reach - self.steps
        self.steps += 1
        if distance == self.reach:
            r, l = ring_far(self.blocks(distance), self.rows, self.each)
        else:
            sent = after(self.sent, deps)
            r, l = ring_add(
                self.blocks(distance), self.blocks(-distance), sent, self.rows, self.each
            )
        self.going = (r, l)
        self.sent = (lax.ppermute(r, "dp", ring.right), lax.ppermute(l, "dp", ring.left))
        return self.sent

    def total(self):
        r, l = self.sent
        terms = [
            x[at * self.rows : (at + 1) * self.rows].astype(F32) for x, at in self.blocks(0)
        ]
        return sum(terms) + r.astype(F32) + l.astype(F32)


def outer(pairs, owners, rows, counts):
    height = pairs[0][0].shape[1]
    widths = [rhs.shape[1] for _, rhs in pairs]
    width = sum(widths)
    tile = 768

    def kernel(owners_ref, *refs):
        ins, outs, held_ref = refs[: 2 * len(pairs)], refs[2 * len(pairs) : -1], refs[-1]
        at = 0
        for i, wide in enumerate(widths):
            lhs = ins[2 * i][...]
            for start in range(0, wide, tile):
                size = min(tile, wide - start)
                held_ref[:, pl.ds(at, size)] = dot32(
                    lhs, ins[2 * i + 1][:, pl.ds(start, size)], TN
                ).astype(BF)
                at += size
        slot = 0
        for ref, number in zip(outs, counts):
            for to in range(number):
                source = pl.multiple_of(owners_ref[slot] * rows, 16)
                ref[pl.ds(to * rows, rows), :] = held_ref[pl.ds(source, rows), :]
                slot += 1

    inside = pl.BlockSpec(memory_space=pltpu.VMEM)
    return pl.pallas_call(
        kernel,
        out_shape=[jax.ShapeDtypeStruct((number * rows, width), BF) for number in counts],
        in_specs=[pl.BlockSpec(memory_space=pltpu.SMEM)] + [inside] * (2 * len(pairs)),
        out_specs=[inside] * len(counts),
        scratch_shapes=[pltpu.VMEM((height, width), BF)],
        compiler_params=pltpu.CompilerParams(vmem_limit_bytes=VMEM_BYTES),
        cost_estimate=SMALL,
        name="outer",
    )(owners, *[x for pair in pairs for x in pair])


def after(values, deps):
    if not deps:
        return values
    return lax.optimization_barrier((tuple(values), deps))[0]


def fetch(refs, places, rows, held_ref, sems):
    copies = [
        pltpu.make_async_copy(ref.at[pl.ds(at * rows, rows)], held_ref.at[i], sems.at[i])
        for i, (ref, at) in enumerate(zip(refs, places))
    ]
    for copy in copies:
        copy.start()
    for copy in copies:
        copy.wait()


def terms_spec(each):
    return pl.BlockSpec(memory_space=pltpu.HBM if each else pl.ANY)


def ring_far(blocks, rows, each):
    width = blocks[0][0].shape[1]
    half = width // 2
    number = len(blocks)

    def kernel(*refs):
        ins, (r_ref, l_ref, held_ref, sems) = refs[:number], refs[number:]
        fetch(ins, [at for _, at in blocks], rows, held_ref, sems)
        for k, ref in enumerate((r_ref, l_ref)):
            cols = pl.ds(k * half, half)
            ref[...] = sum(held_ref[i, :, cols].astype(F32) for i in range(number)).astype(BF)

    inside = pl.BlockSpec(memory_space=pltpu.VMEM)
    return pl.pallas_call(
        kernel,
        out_shape=[jax.ShapeDtypeStruct((rows, half), BF)] * 2,
        in_specs=[terms_spec(each)] * number,
        out_specs=[inside] * 2,
        scratch_shapes=[
            pltpu.VMEM((number, rows, width), BF), pltpu.SemaphoreType.DMA((number,))
        ],
        compiler_params=pltpu.CompilerParams(vmem_limit_bytes=RING_VMEM_BYTES),
        cost_estimate=SMALL,
        name="ring_far",
    )(*[x for x, _ in blocks])


def ring_add(right, left, sent, rows, each):
    width = right[0][0].shape[1]
    arrived = sent[0].shape[1]
    number = len(right)
    blocks = right + left

    def kernel(*refs):
        ins, got = refs[: 2 * number], refs[2 * number : 2 * number + 2]
        outs, (held_ref, sems) = refs[2 * number + 2 : 2 * number + 4], refs[2 * number + 4 :]
        fetch(ins, [at for _, at in blocks], rows, held_ref, sems)
        for k, out_ref in enumerate(outs):
            for part in range(width // arrived):
                cols = pl.ds(part * arrived, arrived)
                total = sum(
                    held_ref[k * number + i, :, cols].astype(F32) for i in range(number)
                )
                if arrived == width or part == k:
                    total = total + got[k][...].astype(F32)
                out_ref[:, cols] = total.astype(BF)

    inside = pl.BlockSpec(memory_space=pltpu.VMEM)
    return pl.pallas_call(
        kernel,
        out_shape=[jax.ShapeDtypeStruct((rows, width), BF)] * 2,
        in_specs=[terms_spec(each)] * (2 * number) + [inside] * 2,
        out_specs=[inside] * 2,
        scratch_shapes=[
            pltpu.VMEM((2 * number, rows, width), BF), pltpu.SemaphoreType.DMA((2 * number,))
        ],
        compiler_params=pltpu.CompilerParams(vmem_limit_bytes=RING_VMEM_BYTES),
        cost_estimate=SMALL,
        name="ring_add",
    )(*[x for x, _ in blocks], *sent)


def ring_total(block, sent, core):
    rows, width = sent[0].shape
    half = rows // 2

    def kernel(core_ref, own_ref, r_ref, l_ref, mine_ref, away_ref, held_ref, sems):
        fetch([own_ref], [block[1]], rows, held_ref, sems)
        begin = pl.multiple_of(core_ref[0] * half, 16)
        for at, out_ref in ((begin, mine_ref), (pl.multiple_of(half - begin, 16), away_ref)):
            here = pl.ds(at, half)
            out_ref[...] = (
                held_ref[0, here, :].astype(F32)
                + r_ref[here, :].astype(F32)
                + l_ref[here, :].astype(F32)
            )

    inside = pl.BlockSpec(memory_space=pltpu.VMEM)
    return pl.pallas_call(
        kernel,
        out_shape=[jax.ShapeDtypeStruct((half, width), F32)] * 2,
        in_specs=[pl.BlockSpec(memory_space=pltpu.SMEM), terms_spec(True), inside, inside],
        out_specs=[inside] * 2,
        scratch_shapes=[pltpu.VMEM((1, rows, width), BF), pltpu.SemaphoreType.DMA((1,))],
        compiler_params=pltpu.CompilerParams(vmem_limit_bytes=RING_VMEM_BYTES),
        cost_estimate=SMALL,
        name="ring_total",
    )(core[None], block[0], *sent)


def combine(mine, got, core):
    rows, width = mine.shape
    split = width // 2 // EXPERTS

    def kernel(core_ref, mine_ref, got_ref, *outs):
        for k, ref in enumerate((mine_ref, got_ref)):
            first = (1 - core_ref[0]) if k else core_ref[0]
            at = pl.ds(pl.multiple_of(first * split, 128), split)
            for i, out_ref in enumerate(outs):
                for e in range(EXPERTS):
                    out_ref[:, e, at] = ref[:, pl.ds((i * EXPERTS + e) * split, split)]

    inside = pl.BlockSpec(memory_space=pltpu.VMEM)
    return pl.pallas_call(
        kernel,
        out_shape=[jax.ShapeDtypeStruct((rows, EXPERTS, 2 * split), F32)] * 2,
        in_specs=[pl.BlockSpec(memory_space=pltpu.SMEM)] + [inside] * 2,
        out_specs=[inside] * 2,
        compiler_params=pltpu.CompilerParams(vmem_limit_bytes=VMEM_BYTES),
        cost_estimate=SMALL,
        name="combine",
    )(core[None], mine, got)


def place(pieces, owners, chips):
    rows, width = pieces[0].shape
    half = width // 2
    number = len(pieces)

    def kernel(owners_ref, *refs):
        ins, outs, sems = refs[:number], refs[number:-1], refs[-1]
        copies = []
        for i, ref in enumerate(ins):
            target = pl.ds(pl.multiple_of(owners_ref[i] * rows, 16), rows)
            for k, out_ref in enumerate(outs):
                source = ref.at[:, pl.ds(k * half, half)]
                copies.append(
                    pltpu.make_async_copy(source, out_ref.at[target], sems.at[len(copies)])
                )
        for copy in copies:
            copy.start()
        for copy in copies:
            copy.wait()

    return pl.pallas_call(
        kernel,
        out_shape=[jax.ShapeDtypeStruct((chips * rows, half), BF)] * 2,
        in_specs=[pl.BlockSpec(memory_space=pltpu.SMEM)]
        + [pl.BlockSpec(memory_space=pl.ANY)] * number,
        out_specs=[pl.BlockSpec(memory_space=pltpu.VMEM)] * 2,
        scratch_shapes=[pltpu.SemaphoreType.DMA((2 * number,))],
        compiler_params=pltpu.CompilerParams(vmem_limit_bytes=RING_VMEM_BYTES),
        cost_estimate=SMALL,
        name="place",
    )(owners, *pieces)


def assemble(pieces, owners):
    rows, width = pieces[0].shape
    number = len(pieces)

    def kernel(owners_ref, *refs):
        out_ref, sems = refs[number:]
        copies = []
        for i in range(number):
            target = out_ref.at[pl.ds(pl.multiple_of(owners_ref[i] * rows, 16), rows)]
            copies.append(pltpu.make_async_copy(refs[i], target, sems.at[i]))
        for copy in copies:
            copy.start()
        for copy in copies:
            copy.wait()

    return pl.pallas_call(
        kernel,
        out_shape=jax.ShapeDtypeStruct((number * rows, width), BF),
        in_specs=[pl.BlockSpec(memory_space=pltpu.SMEM)]
        + [pl.BlockSpec(memory_space=pl.ANY)] * number,
        out_specs=pl.BlockSpec(memory_space=pltpu.VMEM),
        scratch_shapes=[pltpu.SemaphoreType.DMA((number,))],
        compiler_params=pltpu.CompilerParams(vmem_limit_bytes=VMEM_BYTES),
        cost_estimate=SMALL,
        name="assemble",
    )(owners, *pieces)


def gelu_and_slope(v):
    c = 0.7978845608028654
    t = jnp.tanh(c * (v + 0.044715 * (v * v * v)))
    slope = 0.5 * (1.0 + t) + 0.5 * v * (1.0 - t * t) * c * (1.0 + 3 * 0.044715 * (v * v))
    return 0.5 * v * (1.0 + t), slope


def expert_rows(own_ref, got_ref, e, begin, width):
    at = (pl.ds(e * CAP, CAP), pl.ds(begin, width))
    return jnp.concatenate([own_ref[at], got_ref[at]], axis=0)


def expert_layers(own, got, state, last, last_owner, slots, rows_out):
    filled, d = own.shape[0], own.shape[1] // 2
    width = 2 * state[0].shape[1]
    units = width // 2 // EXPERTS
    chips = slots.shape[0]
    number = len(last)

    def kernel(last_ref, slots_ref, own_hbm, got_hbm, *refs):
        ins, refs = refs[2 : 2 + number], refs[2 + number :]
        mine_ref, away_ref, outs, refs = refs[0], refs[1], refs[2 : 2 + chips], refs[2 + chips :]
        in_ref, down_ref, own_ref, got_ref, held_ref, sems, out_sems = refs
        weights = (in_ref, down_ref)
        pairs = ((own_hbm, own_ref), (got_hbm, got_ref))
        copies = [pltpu.make_async_copy(*pair, sems.at[i]) for i, pair in enumerate(pairs)]
        for copy in copies:
            copy.start()
        for copy in copies:
            copy.wait()
        for ref, weight in zip(ins, weights):
            rows = ref.shape[0]
            weight[pl.ds(pl.multiple_of(last_ref[0] * rows, 16), rows), :] = ref[...]
        for e in range(EXPERTS):
            cols = pl.ds(e * units, units)
            w_i, w_d = in_ref[:, cols], down_ref[:, cols]
            x, g = (expert_rows(own_ref, got_ref, e, k * d, d) for k in range(2))
            active, slope = gelu_and_slope(dot32(x, w_i, NN))
            active = active.astype(BF)
            grad_pre = (dot32(g, w_d, NN) * slope).astype(BF)
            back = dot32(active, w_d, NT).astype(BF)
            sent = dot32(grad_pre, w_i, NT).astype(BF)
            for k, ref in enumerate((mine_ref, away_ref)):
                ref[pl.ds(e * CAP, CAP), pl.ds(0, d)] = back[k * CAP : (k + 1) * CAP]
                ref[pl.ds(e * CAP, CAP), pl.ds(d, d)] = sent[k * CAP : (k + 1) * CAP]
            held_ref[:, pl.ds(e * units, units)] = dot32(x, grad_pre, TN).astype(BF)
            held_ref[:, pl.ds((EXPERTS + e) * units, units)] = dot32(g, active, TN).astype(BF)
        copies = []
        for slot in range(chips):
            begin = pl.multiple_of(slots_ref[slot] * rows_out, 16)
            source = held_ref.at[pl.ds(begin, rows_out)]
            copies.append(pltpu.make_async_copy(source, outs[slot], out_sems.at[slot]))
        for copy in copies:
            copy.start()
        for copy in copies:
            copy.wait()

    inside = pl.BlockSpec(memory_space=pltpu.VMEM)
    outside = pl.BlockSpec(memory_space=pltpu.HBM)
    scalars = pl.BlockSpec(memory_space=pltpu.SMEM)
    mine, away, *terms, _, _ = pl.pallas_call(
        kernel,
        out_shape=[jax.ShapeDtypeStruct((filled, 2 * d), BF)] * 2
        + [jax.ShapeDtypeStruct((rows_out, width), BF)] * chips
        + [jax.ShapeDtypeStruct((d, width // 2), BF)] * 2,
        in_specs=[scalars] * 2 + [outside] * 2 + [inside] * (2 + number),
        out_specs=[inside] * 2 + [outside] * chips + [inside] * 2,
        input_output_aliases={4: 2 + chips, 5: 3 + chips},
        scratch_shapes=[pltpu.VMEM((filled, 2 * d), BF)] * 2
        + [
            pltpu.VMEM((d, width), BF),
            pltpu.SemaphoreType.DMA((2,)),
            pltpu.SemaphoreType.DMA((chips,)),
        ],
        compiler_params=pltpu.CompilerParams(vmem_limit_bytes=EXPERT_VMEM_BYTES),
        cost_estimate=SMALL,
        name="expert_layers",
    )(last_owner[None], slots, own, got, *state, *last)
    return mine, away, terms


def interleave(own, other, core, rows):
    chips, width = own.shape[0] // rows, own.shape[1]

    def kernel(core_ref, own_ref, other_ref, out_ref):
        for k, ref in enumerate((own_ref, other_ref)):
            first = (1 - core_ref[0]) if k else core_ref[0]
            for chip in range(chips):
                target = pl.multiple_of((2 * chip + first) * rows, 16)
                out_ref[pl.ds(target, rows), :] = ref[pl.ds(chip * rows, rows), :]

    inside = pl.BlockSpec(memory_space=pltpu.VMEM)
    return pl.pallas_call(
        kernel,
        out_shape=jax.ShapeDtypeStruct((2 * chips * rows, width), BF),
        in_specs=[pl.BlockSpec(memory_space=pltpu.SMEM), inside, inside],
        out_specs=inside,
        compiler_params=pltpu.CompilerParams(vmem_limit_bytes=VMEM_BYTES),
        cost_estimate=SMALL,
        name="interleave",
    )(core[None], own, other)


def swap_tensor(x):
    return lax.ppermute(x, "tensor", [(0, 1), (1, 0)])


def whole_rows(own, other, rank):
    return jnp.where(
        rank == 0, jnp.concatenate([own, other], axis=0), jnp.concatenate([other, own], axis=0)
    )


def sum_pairs(x, step):
    pairs = [(i, i ^ step) for i in range(lax.axis_size("dp"))]
    return x + lax.ppermute(x, "dp", pairs)


def rms_scale(rows):
    return lax.rsqrt(jnp.mean(rows * rows, axis=-1, keepdims=True) + EPS)


def norm_back(grad, normed, scale, gain):
    weighted = grad * gain
    return scale * (weighted - normed * jnp.mean(weighted * normed, axis=-1, keepdims=True))


def dot32(a, b, dims):
    return lax.dot_general(a, b, (dims, ((), ())), preferred_element_type=F32)


NN = ((1,), (0,))
NT = ((1,), (1,))
TN = ((0,), (0,))


def attention_forward(x, gain, weights, by_offset, seq_col, seq_row):
    count, d = x.shape
    head_cols = weights.shape[1] // 4
    heads = head_cols // HEAD_DIM
    scale = HEAD_DIM ** (-0.5)
    lanes = by_offset.shape[1]

    def kernel(x_ref, gain_ref, w_ref, off_ref, col_ref, row_ref, *outs):
        normed_ref, scale_ref, proj_ref, p_ref, context_ref, part_ref = outs
        rows = x_ref[...].astype(F32)
        r = lax.rsqrt(jnp.mean(rows * rows, axis=-1, keepdims=True) + EPS)
        scale_ref[...] = r
        normed = (rows * r * gain_ref[...]).astype(BF)
        normed_ref[...] = normed
        for s in range(3):
            at = pl.ds(s * head_cols, head_cols)
            proj_ref[:, at] = dot32(normed, w_ref[:, at], NN).astype(BF)
        same = col_ref[...] == row_ref[...]
        for h in range(heads):
            q = proj_ref[:, pl.ds(h * HEAD_DIM, HEAD_DIM)]
            k = proj_ref[:, pl.ds(head_cols + h * HEAD_DIM, HEAD_DIM)]
            v = proj_ref[:, pl.ds(2 * head_cols + h * HEAD_DIM, HEAD_DIM)]
            line = jnp.broadcast_to(off_ref[pl.ds(h, 1), :], (count, lanes))
            bias = pltpu.roll(line, lanes - (count - 1), 1, stride=1, stride_axis=0)[:, :count]
            scores = jnp.where(same, dot32(q, k, NT) * scale + bias, NEG)
            expo = jnp.exp(scores - jnp.max(scores, axis=-1, keepdims=True))
            p = expo / jnp.sum(expo, axis=-1, keepdims=True)
            p_ref[h] = p
            context_ref[:, pl.ds(h * HEAD_DIM, HEAD_DIM)] = dot32(p.astype(BF), v, NN).astype(BF)
        out_w = w_ref[:, pl.ds(3 * head_cols, head_cols)]
        part_ref[...] = dot32(context_ref[...], out_w, NT).astype(BF)

    inside = pl.BlockSpec(memory_space=pltpu.VMEM)
    return pl.pallas_call(
        kernel,
        out_shape=(
            jax.ShapeDtypeStruct((count, d), BF),
            jax.ShapeDtypeStruct((count, 1), F32),
            jax.ShapeDtypeStruct((count, 3 * head_cols), BF),
            jax.ShapeDtypeStruct((heads, count, count), F32),
            jax.ShapeDtypeStruct((count, head_cols), BF),
            jax.ShapeDtypeStruct((count, d), BF),
        ),
        in_specs=[inside] * 6,
        out_specs=(inside,) * 6,
        compiler_params=pltpu.CompilerParams(vmem_limit_bytes=VMEM_BYTES),
        cost_estimate=SMALL,
        name="attention_forward",
    )(x, gain, weights, by_offset, seq_col, seq_row)


def attention_backward(low, other, hidden, scales, gain, out_grad, weights, proj, p_full, lanes):
    count, d = low.shape
    head_cols = weights.shape[1] // 4
    heads = head_cols // HEAD_DIM
    scale = HEAD_DIM ** (-0.5)

    def kernel(low_ref, other_ref, hidden_ref, scales_ref, gain_ref, g_ref, w_ref, proj_ref, p_ref,
               hidden_grad_ref, grad_ref, out_ref, sums_ref, gc_ref):
        r2 = scales_ref[:, 3:4]
        n = hidden_ref[...] * r2
        u = (low_ref[...].astype(F32) + other_ref[...].astype(F32)) * gain_ref[...]
        total = g_ref[...].astype(F32) + r2 * (u - n * jnp.mean(u * n, axis=-1, keepdims=True))
        hidden_grad_ref[...] = total
        grad_ref[...] = total.astype(BF)
        out_w = w_ref[:, pl.ds(3 * head_cols, head_cols)]
        gc_ref[...] = dot32(grad_ref[...], out_w, NN).astype(BF)
        down = lax.broadcasted_iota(jnp.int32, (count, count), 0)
        across = lax.broadcasted_iota(jnp.int32, (count, count), 1)
        flip = (down + across == count - 1).astype(F32).astype(BF)
        for h in range(heads):
            at = [pl.ds(s * head_cols + h * HEAD_DIM, HEAD_DIM) for s in range(3)]
            q, k, v = proj_ref[:, at[0]], proj_ref[:, at[1]], proj_ref[:, at[2]]
            p = p_ref[h]
            gc = gc_ref[:, at[0]]
            dp = dot32(gc, v, NT)
            ds = (p * (dp - jnp.sum(p * dp, axis=-1, keepdims=True))).astype(BF)
            out_ref[:, at[0]] = (dot32(ds, k, NN) * scale).astype(BF)
            out_ref[:, at[1]] = (dot32(ds, q, TN) * scale).astype(BF)
            out_ref[:, at[2]] = dot32(p.astype(BF), gc, TN).astype(BF)
            turned = dot32(ds, flip, TN)
            wide = jnp.concatenate([turned, jnp.zeros((count, lanes - count), F32)], axis=1)
            rolled = pltpu.roll(wide, 0, 1, stride=1, stride_axis=0)
            sums_ref[pl.ds(h, 1), :] = jnp.sum(rolled, axis=0, keepdims=True)

    inside = pl.BlockSpec(memory_space=pltpu.VMEM)
    return pl.pallas_call(
        kernel,
        out_shape=(
            jax.ShapeDtypeStruct((count, d), F32),
            jax.ShapeDtypeStruct((count, d), BF),
            jax.ShapeDtypeStruct((count, 3 * head_cols), BF),
            jax.ShapeDtypeStruct((heads, lanes), F32),
        ),
        in_specs=[inside] * 9,
        out_specs=(inside,) * 4,
        scratch_shapes=[pltpu.VMEM((count, head_cols), BF)],
        compiler_params=pltpu.CompilerParams(vmem_limit_bytes=VMEM_BYTES),
        cost_estimate=SMALL,
        name="attention_backward",
    )(low, other, hidden, scales, gain, out_grad, weights, proj, p_full)


def route(x, part, other, gain, w_router, expert_col, flat, out_grad):
    count, d = x.shape

    def kernel(x_ref, part_ref, other_ref, gain_ref, w_ref, expert_ref, flat_ref, g_ref,
               hidden_ref, out_ref, scales_ref, blocks_ref, sem):
        hidden = x_ref[...].astype(F32) + (part_ref[...].astype(F32) + other_ref[...].astype(F32))
        hidden_ref[...] = hidden
        r2 = lax.rsqrt(jnp.mean(hidden * hidden, axis=-1, keepdims=True) + EPS)
        mixed = hidden * r2 * gain_ref[...]
        logits = [
            jnp.sum(mixed * w_ref[e : e + 1, :], axis=-1, keepdims=True) for e in range(EXPERTS)
        ]
        top = jnp.maximum(logits[0], logits[1])
        expo = [jnp.exp(v - top) for v in logits]
        probs = [v / (expo[0] + expo[1]) for v in expo]
        hits = [(expert_ref[...] == e).astype(F32) for e in range(EXPERTS)]
        gate = probs[0] * hits[0] + probs[1] * hits[1]
        lane = lax.broadcasted_iota(jnp.int32, (count, 128), 1)
        columns = [gate] + [gate * (h - p) for h, p in zip(hits, probs)] + [r2]
        scales_ref[...] = sum(jnp.where(lane == i, v, 0.0) for i, v in enumerate(columns))
        slots = lax.broadcasted_iota(jnp.int32, (EXPERTS * CAP, count), 0)
        chosen = (slots == flat_ref[...]).astype(F32).astype(BF)
        blocks_ref[:, pl.ds(0, d)] = dot32(chosen, mixed.astype(BF), NN).astype(BF)
        grad_routed = (gate * g_ref[...].astype(F32)).astype(BF)
        blocks_ref[:, pl.ds(d, d)] = dot32(chosen, grad_routed, NN).astype(BF)
        copy = pltpu.make_async_copy(blocks_ref, out_ref, sem)
        copy.start()
        copy.wait()

    inside = pl.BlockSpec(memory_space=pltpu.VMEM)
    return pl.pallas_call(
        kernel,
        out_shape=(
            jax.ShapeDtypeStruct((count, d), F32),
            jax.ShapeDtypeStruct((EXPERTS * CAP, 2 * d), BF),
            jax.ShapeDtypeStruct((count, 128), F32),
        ),
        in_specs=[inside] * 8,
        out_specs=(inside, pl.BlockSpec(memory_space=pltpu.HBM), inside),
        scratch_shapes=[pltpu.VMEM((EXPERTS * CAP, 2 * d), BF), pltpu.SemaphoreType.DMA],
        compiler_params=pltpu.CompilerParams(vmem_limit_bytes=VMEM_BYTES),
        cost_estimate=SMALL,
        name="route",
    )(x, part, other, gain, w_router, expert_col, flat, out_grad)


def rows_back(mine, got, hidden, scales, gain, w_router, flat, out_grad):
    count, d = hidden.shape

    def kernel(mine_ref, got_ref, hidden_ref, scales_ref, gain_ref, w_ref, flat_ref, g_ref,
               mixed_ref, routed_ref, gains_ref):
        sums = (mine_ref[...].astype(F32) + got_ref[...].astype(F32)).astype(BF)
        slots = lax.broadcasted_iota(jnp.int32, (count, EXPERTS * CAP), 1)
        chosen = (slots == flat_ref[...]).astype(F32).astype(BF)
        routed = dot32(chosen, sums[:, :d], NN)
        gate, r2 = scales_ref[:, 0:1], scales_ref[:, 3:4]
        routed_ref[...] = (gate * routed).astype(BF)
        gate_part = jnp.sum(g_ref[...].astype(F32) * routed, axis=-1, keepdims=True)
        grad_logits = [gate_part * scales_ref[:, 1 + e : 2 + e] for e in range(EXPERTS)]
        part = dot32(chosen, sums[:, d:], NN)
        part = part + sum(grad_logits[e] * w_ref[e : e + 1, :] for e in range(EXPERTS))
        mixed_ref[...] = part.astype(BF)
        n = hidden_ref[...] * r2
        gains_ref[0:1, :] = jnp.sum(part * n, axis=0, keepdims=True)
        mixed = n * gain_ref[...]
        for e in range(EXPERTS):
            gains_ref[1 + e : 2 + e, :] = jnp.sum(mixed * grad_logits[e], axis=0, keepdims=True)
        gains_ref[1 + EXPERTS :, :] = jnp.zeros((7 - EXPERTS, d), F32)

    inside = pl.BlockSpec(memory_space=pltpu.VMEM)
    return pl.pallas_call(
        kernel,
        out_shape=(
            jax.ShapeDtypeStruct((count, d), BF),
            jax.ShapeDtypeStruct((count, d), BF),
            jax.ShapeDtypeStruct((8, d), F32),
        ),
        in_specs=[inside] * 8,
        out_specs=(inside,) * 3,
        compiler_params=pltpu.CompilerParams(vmem_limit_bytes=VMEM_BYTES),
        cost_estimate=SMALL,
        name="rows_back",
    )(mine, got, hidden, scales, gain, w_router, flat, out_grad)


def input_back(grad, weights, x, sums, bucket_hits, gains, rank):
    count, d = x.shape
    heads, lanes = sums.shape
    buckets = bucket_hits.shape[1]
    each = d // 128

    def kernel(rank_ref, grad_ref, w_ref, x_ref, sums_ref, hits_ref, gains_ref, low_ref, line_ref):
        part = dot32(grad_ref[...], w_ref[:, pl.ds(0, grad_ref.shape[1])], NT)
        low_ref[...] = part.astype(BF)
        rows = x_ref[...].astype(F32)
        n = rows * lax.rsqrt(jnp.mean(rows * rows, axis=-1, keepdims=True) + EPS)
        vectors = [jnp.sum(part * n, axis=0, keepdims=True)]
        vectors += [gains_ref[k : k + 1, :] for k in range(1 + EXPERTS)]
        for k, vector in enumerate(vectors):
            for j in range(each):
                line_ref[pl.ds(16 + k * each + j, 1), :] = vector[:, j * 128 : (j + 1) * 128]
        rel = jnp.dot(sums_ref[...], hits_ref[...], precision=HIGH, preferred_element_type=F32)
        rel = jnp.concatenate([rel, jnp.zeros((heads, 128 - buckets), F32)], axis=1)
        line_ref[0:16, :] = jnp.zeros((16, 128), F32)
        for k in range(2):
            line_ref[pl.ds(k * heads, heads), :] = jnp.where(rank_ref[0] == k, rel, 0.0)

    inside = pl.BlockSpec(memory_space=pltpu.VMEM)
    return pl.pallas_call(
        kernel,
        out_shape=(
            jax.ShapeDtypeStruct((count, d), BF),
            jax.ShapeDtypeStruct((16 + (2 + EXPERTS) * each, 128), F32),
        ),
        in_specs=[pl.BlockSpec(memory_space=pltpu.SMEM)] + [inside] * 6,
        out_specs=(inside,) * 2,
        compiler_params=pltpu.CompilerParams(vmem_limit_bytes=VMEM_BYTES),
        cost_estimate=SMALL,
        name="input_back",
    )(rank[None], grad, weights, x, sums, bucket_hits, gains)


def body(
    block_in,
    attn_gain,
    w_qkv,
    w_out,
    rel_bias,
    moe_gain,
    w_router,
    w_in,
    w_down,
    seq_lengths,
    expert_ids,
    rel_table,
    out_grad,
):
    rows_local, width = block_in.shape
    rank = lax.axis_index("tensor")
    ring = Ring()
    shard = w_out.shape[0]
    head_cols = w_out.shape[1]
    units = w_in.shape[2]
    heads_local = head_cols // HEAD_DIM
    count = 2 * rows_local

    attn_shard = jnp.concatenate([w_qkv.reshape(shard, 3 * head_cols), w_out], axis=1)
    x_other, g_other = swap_tensor(block_in), swap_tensor(out_grad)
    split = units // 2

    def unit_half(w, core):
        return lax.dynamic_slice_in_dim(w, core * split, split, axis=2)

    if not ring.long:
        ring_a = Gather(ring, attn_shard, False)
        a1 = ring_a.step()
        own_half, other_half = (
            jnp.concatenate(
                [unit_half(w, core).reshape(shard, EXPERTS * split) for w in (w_in, w_down)],
                axis=1,
            )
            for core in (ring.core, 1 - ring.core)
        )
        got_half = ring.other_core(other_half)
        a2 = ring_a.step()
        ring_b = Gather(ring, ring.by_core(own_half, got_half, 0), True)
        a3 = ring_a.step()
        a4 = ring_a.step()
        ring_b.step(*a3, x_other, g_other)
        own_a = assemble(ring_a.pieces, ring_a.owners())
        other_a = ring.other_core(own_a)
        attn_all = interleave(own_a, other_a, ring.core, shard)
    else:
        attn_all = lax.all_gather(attn_shard, "dp", axis=0, tiled=True)
        in_all, down_all = (
            unit_half(lax.all_gather(w, "dp", axis=0, tiled=True), ring.core).reshape(
                -1, EXPERTS * split
            )
            for w in (w_in, w_down)
        )
    x_low = whole_rows(block_in, x_other, rank)
    g_low = whole_rows(out_grad, g_other, rank)

    places = jnp.arange(count, dtype=jnp.int32)
    ends = jnp.cumsum(seq_lengths[0])
    seq_ids = jnp.sum((places[:, None] >= ends[None, :]).astype(jnp.int32), axis=1)
    bias_local = lax.dynamic_slice_in_dim(rel_bias, rank * heads_local, heads_local, 1)
    bucket_hits = (
        rel_table[:, None] == jnp.arange(rel_bias.shape[0], dtype=jnp.int32)[None, :]
    ).astype(F32)
    by_offset = jnp.dot(bucket_hits, bias_local, precision=HIGH)
    lanes = 2 * count
    by_offset = jnp.pad(by_offset.T, ((0, 0), (0, lanes - by_offset.shape[0])))
    normed_one, _, projected, p_full, context, attn_part = attention_forward(
        x_low, attn_gain[None, :], attn_all, by_offset, seq_ids[:, None], seq_ids[None, :]
    )
    if not ring.long:
        ring_b.step()
        ring_b.step(attn_part)
    attn_other = swap_tensor(attn_part)
    expert_col = expert_ids[:, 0]
    hits = (
        expert_col[:, None] == jnp.arange(EXPERTS, dtype=jnp.int32)[None, :]
    ).astype(jnp.int32)
    flat = expert_col * CAP + jnp.sum(jnp.cumsum(hits, axis=0) * hits, axis=1) - 1
    gain_row, router_rows = moe_gain[None, :], w_router.T
    hidden, own_blocks, scales = route(
        x_low, attn_part, attn_other, gain_row, router_rows, expert_ids, flat[None, :], g_low
    )
    if not ring.long:
        got_blocks = ring.other_core(own_blocks)
        state = place(ring_b.pieces, ring_b.owners(0, ring.chips - 1), ring.chips)
        last = ring_b.step(got_blocks)
        mine, away, terms = expert_layers(
            own_blocks,
            got_blocks,
            state,
            last,
            ring.chip_at(ring.chips // 2),
            ring.slot_chips(),
            2 * shard,
        )
        send = Scatter(ring, terms, 2 * shard)
        c1 = send.step()
    else:
        first = jnp.zeros((1,), jnp.int32)
        mine, away, terms = expert_layers(
            own_blocks,
            ring.other_core(own_blocks),
            (in_all, down_all),
            (),
            first[0],
            first,
            width,
        )
    got_sums = ring.other_core(away)
    mixed_low, routed_low, gains = rows_back(
        mine, got_sums, hidden, scales, gain_row, router_rows, flat[:, None], g_low
    )
    if not ring.long:
        c2 = send.step(mixed_low)
    mixed_other = swap_tensor(mixed_low)
    if not ring.long:
        (mixed_other,) = after((mixed_other,), c1)

    def own_rows(x):
        return lax.dynamic_slice_in_dim(x, rank * rows_local, rows_local, 0)

    def other_rows(x):
        return lax.dynamic_slice_in_dim(x, (1 - rank) * rows_local, rows_local, 0)

    routed_other = swap_tensor(other_rows(routed_low))
    result = own_rows(hidden) + (
        own_rows(routed_low).astype(F32) + routed_other.astype(F32)
    )
    grad_hidden, grad_attended, grad_projected, offset_sums = attention_backward(
        mixed_low, mixed_other, hidden, scales, gain_row, g_low, attn_all, projected, p_full, lanes
    )

    attn_pairs = [(normed_one, grad_projected), (grad_attended, context)]
    if not ring.long:
        attn_pairs[0] = (normed_one, after((grad_projected,), c2)[0])
        chips = ring.slot_chips()
        owners = jnp.concatenate([chips * 2 + ring.core, chips * 2 + 1 - ring.core])
        send_a = Scatter(ring, outer(attn_pairs, owners, shard, [ring.chips] * 2), shard)
        c3 = send.step()
        a1 = send_a.step()
    hits_wide = jnp.pad(bucket_hits, ((0, lanes - bucket_hits.shape[0]), (0, 0)))
    normed_low, line = input_back(
        grad_projected, attn_all, x_low, offset_sums, hits_wide, gains, rank
    )
    normed_other = swap_tensor(other_rows(normed_low))
    line = line + swap_tensor(line)
    line = line + ring.other_core(line)
    if not ring.long:
        c4 = send.step(*a1)
        a2 = send_a.step(*c3)
        a3 = send_a.step(*c4)
        (line,) = after((line,), c4)
        line = sum_pairs(line, 2)
        line = sum_pairs(line, 4)
        (line,) = after((line,), a3)
    else:
        line = sum_pairs(sum_pairs(line, 2), 4)
    step = 8
    while step < ring.n:
        line = sum_pairs(line, step)
        step *= 2
    summed = line
    grad_normed = own_rows(normed_low).astype(F32) + normed_other.astype(F32)
    x_own = block_in.astype(F32)
    scale_own = rms_scale(x_own)
    grad_block = own_rows(grad_hidden) + norm_back(
        grad_normed, x_own * scale_own, scale_own, attn_gain
    )
    if ring.long:
        zeros = jnp.zeros((width, 2 * EXPERTS, units), BF)
        terms = terms[0].reshape(width, 2 * EXPERTS, split)
        terms = lax.dynamic_update_slice_in_dim(zeros, terms, ring.core * split, 2)
        sums = lax.psum_scatter(terms, "dp", scatter_dimension=0, tiled=True).astype(F32)
        grad_w_in_mine, grad_w_down_mine = sums[:, :EXPERTS], sums[:, EXPERTS:]
        terms = jnp.concatenate([dot32(x, y, TN).astype(BF) for x, y in attn_pairs], axis=1)
        attn_mine = lax.psum_scatter(terms, "dp", scatter_dimension=0, tiled=True)
        attn_mine = attn_mine.astype(F32)
    else:
        send_a.step()
        sent = after(send.sent, send_a.going)
        mine, away = ring_total(send.blocks(0)[0], sent, ring.core)
        grad_w_in_mine, grad_w_down_mine = combine(mine, ring.other_core(away), ring.core)
        attn_mine = send_a.total()
    summed_rel = summed[: rel_bias.shape[1], : rel_bias.shape[0]].T
    summed = summed[16:].reshape(2 + EXPERTS, width)
    return (
        result.astype(BF),
        grad_block,
        summed[0],
        attn_mine[:, : 3 * head_cols].reshape(w_qkv.shape),
        attn_mine[:, 3 * head_cols :],
        summed_rel,
        summed[1],
        summed[2:].T,
        grad_w_in_mine,
        grad_w_down_mine,
    )


def solution(mesh):
    placed = (
        P(("dp", "tensor"), None),
        P(),
        P("dp", None, "tensor"),
        P("dp", "tensor"),
        P(),
        P(),
        P(),
        P("dp", None, "tensor"),
        P("dp", None, "tensor"),
        P("dp", None),
        P("dp", None),
        P(),
        P(("dp", "tensor"), None),
    )
    return jax.shard_map(
        body,
        mesh=mesh,
        in_specs=placed,
        out_specs=(
            P(("dp", "tensor"), None),
            P(("dp", "tensor"), None),
            P(),
            P("dp", None, "tensor"),
            P("dp", "tensor"),
            P(),
            P(),
            P(),
            P("dp", None, "tensor"),
            P("dp", None, "tensor"),
        ),
        check_vma=False,
    )
```

```python
import jax
import jax.numpy as jnp
from jax import lax
from jax.experimental import pallas as pl
from jax.experimental.pallas import tpu as pltpu
from jax.sharding import PartitionSpec as P

HEAD_DIM = 64
EXPERTS = 2
CAP = 176

LONGEST = 16

EPS = 1e-06
NEG = -1e30
VMEM_BYTES = 12 << 20
RING_VMEM_BYTES = 6 << 20
EXPERT_VMEM_BYTES = 24 << 20
SMALL = pl.CostEstimate(flops=1, bytes_accessed=1, transcendentals=0)
HIGH = lax.Precision.HIGHEST
BF = jnp.bfloat16
F32 = jnp.float32


def ring_chip(place, chips):
    place = place % chips
    return jnp.where(place < chips // 2, 2 * place, 2 * (chips - 1 - place) + 1)


def ring_place(chip, chips):
    return jnp.where(chip % 2 == 0, chip // 2, chips - 1 - chip // 2)


class Ring:
    def __init__(self):
        self.n = lax.axis_size("dp")
        self.chips = self.n // 2
        order = [2 * i for i in range(self.chips // 2)]
        order = order + [c + 1 for c in reversed(order)]
        pairs = [
            (order[i] * 2 + k, order[(i + 1) % self.chips] * 2 + k)
            for i in range(self.chips)
            for k in (0, 1)
        ]
        self.right = pairs
        self.left = [(b, a) for a, b in pairs]
        self.swap = [(i, i ^ 1) for i in range(self.n)]
        index = lax.axis_index("dp")
        self.core = index % 2
        self.long = self.chips > LONGEST
        self.place = ring_place(index // 2, self.chips)
        reach = self.chips // 2
        self.distances = [0] + [d for s in range(1, reach) for d in (-s, s)] + [reach]
        self.slots = [reach] + [d for s in range(reach - 1, 0, -1) for d in (s, -s)] + [0]

    def other_core(self, x):
        return lax.ppermute(x, "dp", self.swap)

    def by_core(self, own, other, axis):
        return jnp.where(
            self.core == 0,
            jnp.concatenate([own, other], axis=axis),
            jnp.concatenate([other, own], axis=axis),
        )

    def slot_chips(self):
        return jnp.stack([self.chip_at(d) for d in self.slots])

    def chip_at(self, distance):
        return ring_chip(self.place + distance + self.chips, self.chips)


class Gather:
    def __init__(self, ring, shard, halves):
        self.ring, self.shard, self.halves = ring, shard, halves
        self.reach = ring.chips // 2
        self.pieces = [shard]
        self.sent = (shard, shard)
        self.steps = 0

    def step(self, *deps):
        ring, half = self.ring, self.shard.shape[1] // 2
        self.steps += 1
        r, l = after(self.sent, deps)
        if self.steps < self.reach:
            self.sent = (lax.ppermute(r, "dp", ring.right), lax.ppermute(l, "dp", ring.left))
        elif self.halves:
            r, l = left_and_right(r, l)
            self.sent = (
                lax.ppermute(r, "dp", ring.right),
                lax.ppermute(l, "dp", ring.left),
            )
        else:
            self.sent = (lax.ppermute(r, "dp", ring.right),)
        self.pieces += self.sent
        return self.sent

    def owners(self, begin=0, end=None):
        return jnp.stack([self.ring.chip_at(d) for d in self.ring.distances[begin:end]])


class Scatter:
    def __init__(self, ring, terms, rows):
        self.ring, self.rows = ring, rows
        self.reach = ring.chips // 2
        self.steps = 0
        self.slots = ring.slots
        self.terms = terms
        self.each = len(self.terms) > 2
        self.got = None if self.each else ring.other_core(self.terms[1])

    def blocks(self, distance):
        at = self.slots.index(distance)
        return [(self.terms[at], 0)] if self.each else [(self.terms[0], at), (self.got, at)]

    def step(self, *deps):
        ring = self.ring
        distance = self.reach - self.steps
        self.steps += 1
        if distance == self.reach:
            r, l = ring_far(self.blocks(distance), self.rows, self.each)
        else:
            sent = after(self.sent, deps)
            r, l = ring_add(
                self.blocks(distance), self.blocks(-distance), sent, self.rows, self.each
            )
        self.going = (r, l)
        self.sent = (lax.ppermute(r, "dp", ring.right), lax.ppermute(l, "dp", ring.left))
        return self.sent

    def total(self):
        r, l = self.sent
        terms = [
            x[at * self.rows : (at + 1) * self.rows].astype(F32) for x, at in self.blocks(0)
        ]
        return sum(terms) + r.astype(F32) + l.astype(F32)


def outer(pairs, owners, rows, counts):
    height = pairs[0][0].shape[1]
    widths = [rhs.shape[1] for _, rhs in pairs]
    width = sum(widths)
    tile = 768

    def kernel(owners_ref, *refs):
        ins, outs, held_ref = refs[: 2 * len(pairs)], refs[2 * len(pairs) : -1], refs[-1]
        at = 0
        for i, wide in enumerate(widths):
            lhs = ins[2 * i][...]
            for start in range(0, wide, tile):
                size = min(tile, wide - start)
                held_ref[:, pl.ds(at, size)] = dot32(
                    lhs, ins[2 * i + 1][:, pl.ds(start, size)], TN
                ).astype(BF)
                at += size
        slot = 0
        for ref, number in zip(outs, counts):
            for to in range(number):
                source = pl.multiple_of(owners_ref[slot] * rows, 16)
                ref[pl.ds(to * rows, rows), :] = held_ref[pl.ds(source, rows), :]
                slot += 1

    inside = pl.BlockSpec(memory_space=pltpu.VMEM)
    return pl.pallas_call(
        kernel,
        out_shape=[jax.ShapeDtypeStruct((number * rows, width), BF) for number in counts],
        in_specs=[pl.BlockSpec(memory_space=pltpu.SMEM)] + [inside] * (2 * len(pairs)),
        out_specs=[inside] * len(counts),
        scratch_shapes=[pltpu.VMEM((height, width), BF)],
        compiler_params=pltpu.CompilerParams(vmem_limit_bytes=VMEM_BYTES),
        cost_estimate=SMALL,
        name="outer",
    )(owners, *[x for pair in pairs for x in pair])


def left_and_right(r, l):
    rows, width = r.shape
    half = width // 2

    def kernel(r_ref, l_ref, r_out, l_out):
        r_out[...] = r_ref[:, pl.ds(0, half)]
        l_out[...] = l_ref[:, pl.ds(half, half)]

    inside = pl.BlockSpec(memory_space=pltpu.VMEM)
    return pl.pallas_call(
        kernel,
        out_shape=[jax.ShapeDtypeStruct((rows, half), BF)] * 2,
        in_specs=[inside] * 2,
        out_specs=[inside] * 2,
        compiler_params=pltpu.CompilerParams(vmem_limit_bytes=RING_VMEM_BYTES),
        cost_estimate=SMALL,
        name="left_and_right",
    )(r, l)


def after(values, deps):
    if not deps:
        return values
    return lax.optimization_barrier((tuple(values), deps))[0]


def fetch(refs, places, rows, held_ref, sems):
    copies = [
        pltpu.make_async_copy(ref.at[pl.ds(at * rows, rows)], held_ref.at[i], sems.at[i])
        for i, (ref, at) in enumerate(zip(refs, places))
    ]
    for copy in copies:
        copy.start()
    for copy in copies:
        copy.wait()


def terms_spec(each):
    return pl.BlockSpec(memory_space=pltpu.HBM if each else pl.ANY)


def ring_far(blocks, rows, each):
    width = blocks[0][0].shape[1]
    half = width // 2
    number = len(blocks)

    def kernel(*refs):
        ins, (r_ref, l_ref, held_ref, sems) = refs[:number], refs[number:]
        fetch(ins, [at for _, at in blocks], rows, held_ref, sems)
        for k, ref in enumerate((r_ref, l_ref)):
            cols = pl.ds(k * half, half)
            ref[...] = sum(held_ref[i, :, cols].astype(F32) for i in range(number)).astype(BF)

    inside = pl.BlockSpec(memory_space=pltpu.VMEM)
    return pl.pallas_call(
        kernel,
        out_shape=[jax.ShapeDtypeStruct((rows, half), BF)] * 2,
        in_specs=[terms_spec(each)] * number,
        out_specs=[inside] * 2,
        scratch_shapes=[
            pltpu.VMEM((number, rows, width), BF), pltpu.SemaphoreType.DMA((number,))
        ],
        compiler_params=pltpu.CompilerParams(vmem_limit_bytes=RING_VMEM_BYTES),
        cost_estimate=SMALL,
        name="ring_far",
    )(*[x for x, _ in blocks])


def ring_add(right, left, sent, rows, each):
    width = right[0][0].shape[1]
    arrived = sent[0].shape[1]
    number = len(right)
    blocks = right + left

    def kernel(*refs):
        ins, got = refs[: 2 * number], refs[2 * number : 2 * number + 2]
        outs, (held_ref, sems) = refs[2 * number + 2 : 2 * number + 4], refs[2 * number + 4 :]
        fetch(ins, [at for _, at in blocks], rows, held_ref, sems)
        for k, out_ref in enumerate(outs):
            for part in range(width // arrived):
                cols = pl.ds(part * arrived, arrived)
                total = sum(
                    held_ref[k * number + i, :, cols].astype(F32) for i in range(number)
                )
                if arrived == width or part == k:
                    total = total + got[k][...].astype(F32)
                out_ref[:, cols] = total.astype(BF)

    inside = pl.BlockSpec(memory_space=pltpu.VMEM)
    return pl.pallas_call(
        kernel,
        out_shape=[jax.ShapeDtypeStruct((rows, width), BF)] * 2,
        in_specs=[terms_spec(each)] * (2 * number) + [inside] * 2,
        out_specs=[inside] * 2,
        scratch_shapes=[
            pltpu.VMEM((2 * number, rows, width), BF), pltpu.SemaphoreType.DMA((2 * number,))
        ],
        compiler_params=pltpu.CompilerParams(vmem_limit_bytes=RING_VMEM_BYTES),
        cost_estimate=SMALL,
        name="ring_add",
    )(*[x for x, _ in blocks], *sent)


def ring_total(block, sent, core):
    rows, width = sent[0].shape
    half = rows // 2

    def kernel(core_ref, own_ref, r_ref, l_ref, mine_ref, away_ref, held_ref, sems):
        fetch([own_ref], [block[1]], rows, held_ref, sems)
        begin = pl.multiple_of(core_ref[0] * half, 16)
        for at, out_ref in ((begin, mine_ref), (pl.multiple_of(half - begin, 16), away_ref)):
            here = pl.ds(at, half)
            out_ref[...] = (
                held_ref[0, here, :].astype(F32)
                + r_ref[here, :].astype(F32)
                + l_ref[here, :].astype(F32)
            )

    inside = pl.BlockSpec(memory_space=pltpu.VMEM)
    return pl.pallas_call(
        kernel,
        out_shape=[jax.ShapeDtypeStruct((half, width), F32)] * 2,
        in_specs=[pl.BlockSpec(memory_space=pltpu.SMEM), terms_spec(True), inside, inside],
        out_specs=[inside] * 2,
        scratch_shapes=[pltpu.VMEM((1, rows, width), BF), pltpu.SemaphoreType.DMA((1,))],
        compiler_params=pltpu.CompilerParams(vmem_limit_bytes=RING_VMEM_BYTES),
        cost_estimate=SMALL,
        name="ring_total",
    )(core[None], block[0], *sent)


def combine(mine, got, core):
    rows, width = mine.shape
    split = width // 2 // EXPERTS

    def kernel(core_ref, mine_ref, got_ref, *outs):
        for k, ref in enumerate((mine_ref, got_ref)):
            first = (1 - core_ref[0]) if k else core_ref[0]
            at = pl.ds(pl.multiple_of(first * split, 128), split)
            for i, out_ref in enumerate(outs):
                for e in range(EXPERTS):
                    out_ref[:, e, at] = ref[:, pl.ds((i * EXPERTS + e) * split, split)]

    inside = pl.BlockSpec(memory_space=pltpu.VMEM)
    return pl.pallas_call(
        kernel,
        out_shape=[jax.ShapeDtypeStruct((rows, EXPERTS, 2 * split), F32)] * 2,
        in_specs=[pl.BlockSpec(memory_space=pltpu.SMEM)] + [inside] * 2,
        out_specs=[inside] * 2,
        compiler_params=pltpu.CompilerParams(vmem_limit_bytes=VMEM_BYTES),
        cost_estimate=SMALL,
        name="combine",
    )(core[None], mine, got)


def place(pieces, owners, chips):
    rows, width = pieces[0].shape
    half = width // 2
    number = len(pieces)

    def kernel(owners_ref, *refs):
        ins, outs, sems = refs[:number], refs[number:-1], refs[-1]
        copies = []
        for i, ref in enumerate(ins):
            target = pl.ds(pl.multiple_of(owners_ref[i] * rows, 16), rows)
            for k, out_ref in enumerate(outs):
                source = ref.at[:, pl.ds(k * half, half)]
                copies.append(
                    pltpu.make_async_copy(source, out_ref.at[target], sems.at[len(copies)])
                )
        for copy in copies:
            copy.start()
        for copy in copies:
            copy.wait()

    return pl.pallas_call(
        kernel,
        out_shape=[jax.ShapeDtypeStruct((chips * rows, half), BF)] * 2,
        in_specs=[pl.BlockSpec(memory_space=pltpu.SMEM)]
        + [pl.BlockSpec(memory_space=pl.ANY)] * number,
        out_specs=[pl.BlockSpec(memory_space=pltpu.VMEM)] * 2,
        scratch_shapes=[pltpu.SemaphoreType.DMA((2 * number,))],
        compiler_params=pltpu.CompilerParams(vmem_limit_bytes=RING_VMEM_BYTES),
        cost_estimate=SMALL,
        name="place",
    )(owners, *pieces)


def assemble(pieces, owners):
    rows, width = pieces[0].shape
    number = len(pieces)

    def kernel(owners_ref, *refs):
        out_ref, sems = refs[number:]
        copies = []
        for i in range(number):
            target = out_ref.at[pl.ds(pl.multiple_of(owners_ref[i] * rows, 16), rows)]
            copies.append(pltpu.make_async_copy(refs[i], target, sems.at[i]))
        for copy in copies:
            copy.start()
        for copy in copies:
            copy.wait()

    return pl.pallas_call(
        kernel,
        out_shape=jax.ShapeDtypeStruct((number * rows, width), BF),
        in_specs=[pl.BlockSpec(memory_space=pltpu.SMEM)]
        + [pl.BlockSpec(memory_space=pl.ANY)] * number,
        out_specs=pl.BlockSpec(memory_space=pltpu.VMEM),
        scratch_shapes=[pltpu.SemaphoreType.DMA((number,))],
        compiler_params=pltpu.CompilerParams(vmem_limit_bytes=VMEM_BYTES),
        cost_estimate=SMALL,
        name="assemble",
    )(owners, *pieces)


def gelu_and_slope(v):
    c = 0.7978845608028654
    t = jnp.tanh(c * (v + 0.044715 * (v * v * v)))
    slope = 0.5 * (1.0 + t) + 0.5 * v * (1.0 - t * t) * c * (1.0 + 3 * 0.044715 * (v * v))
    return 0.5 * v * (1.0 + t), slope


def expert_rows(own_ref, got_ref, e, begin, width):
    at = (pl.ds(e * CAP, CAP), pl.ds(begin, width))
    return jnp.concatenate([own_ref[at], got_ref[at]], axis=0)


def expert_layers(own, got, state, last, last_owner, slots, rows_out):
    filled, d = own.shape[0], own.shape[1] // 2
    width = 2 * state[0].shape[1]
    units = width // 2 // EXPERTS
    chips = slots.shape[0]
    number = len(last)

    def kernel(last_ref, slots_ref, own_hbm, got_hbm, *refs):
        ins, refs = refs[2 : 2 + number], refs[2 + number :]
        mine_ref, away_ref, outs, refs = refs[0], refs[1], refs[2 : 2 + chips], refs[2 + chips :]
        in_ref, down_ref, own_ref, got_ref, held_ref, sems, out_sems = refs
        weights = (in_ref, down_ref)
        pairs = ((own_hbm, own_ref), (got_hbm, got_ref))
        copies = [pltpu.make_async_copy(*pair, sems.at[i]) for i, pair in enumerate(pairs)]
        for copy in copies:
            copy.start()
        for copy in copies:
            copy.wait()
        for ref, weight in zip(ins, weights):
            rows = ref.shape[0]
            weight[pl.ds(pl.multiple_of(last_ref[0] * rows, 16), rows), :] = ref[...]
        for e in range(EXPERTS):
            cols = pl.ds(e * units, units)
            w_i, w_d = in_ref[:, cols], down_ref[:, cols]
            x, g = (expert_rows(own_ref, got_ref, e, k * d, d) for k in range(2))
            active, slope = gelu_and_slope(dot32(x, w_i, NN))
            active = active.astype(BF)
            grad_pre = (dot32(g, w_d, NN) * slope).astype(BF)
            back = dot32(active, w_d, NT).astype(BF)
            sent = dot32(grad_pre, w_i, NT).astype(BF)
            for k, ref in enumerate((mine_ref, away_ref)):
                ref[pl.ds(e * CAP, CAP), pl.ds(0, d)] = back[k * CAP : (k + 1) * CAP]
                ref[pl.ds(e * CAP, CAP), pl.ds(d, d)] = sent[k * CAP : (k + 1) * CAP]
            held_ref[:, pl.ds(e * units, units)] = dot32(x, grad_pre, TN).astype(BF)
            held_ref[:, pl.ds((EXPERTS + e) * units, units)] = dot32(g, active, TN).astype(BF)
        copies = []
        for slot in range(chips):
            begin = pl.multiple_of(slots_ref[slot] * rows_out, 16)
            source = held_ref.at[pl.ds(begin, rows_out)]
            copies.append(pltpu.make_async_copy(source, outs[slot], out_sems.at[slot]))
        for copy in copies:
            copy.start()
        for copy in copies:
            copy.wait()

    inside = pl.BlockSpec(memory_space=pltpu.VMEM)
    outside = pl.BlockSpec(memory_space=pltpu.HBM)
    scalars = pl.BlockSpec(memory_space=pltpu.SMEM)
    mine, away, *terms, _, _ = pl.pallas_call(
        kernel,
        out_shape=[jax.ShapeDtypeStruct((filled, 2 * d), BF)] * 2
        + [jax.ShapeDtypeStruct((rows_out, width), BF)] * chips
        + [jax.ShapeDtypeStruct((d, width // 2), BF)] * 2,
        in_specs=[scalars] * 2 + [outside] * 2 + [inside] * (2 + number),
        out_specs=[inside] * 2 + [outside] * chips + [inside] * 2,
        input_output_aliases={4: 2 + chips, 5: 3 + chips},
        scratch_shapes=[pltpu.VMEM((filled, 2 * d), BF)] * 2
        + [
            pltpu.VMEM((d, width), BF),
            pltpu.SemaphoreType.DMA((2,)),
            pltpu.SemaphoreType.DMA((chips,)),
        ],
        compiler_params=pltpu.CompilerParams(vmem_limit_bytes=EXPERT_VMEM_BYTES),
        cost_estimate=SMALL,
        name="expert_layers",
    )(last_owner[None], slots, own, got, *state, *last)
    return mine, away, terms


def interleave(own, other, core, rows):
    chips, width = own.shape[0] // rows, own.shape[1]

    def kernel(core_ref, own_ref, other_ref, out_ref):
        for k, ref in enumerate((own_ref, other_ref)):
            first = (1 - core_ref[0]) if k else core_ref[0]
            for chip in range(chips):
                target = pl.multiple_of((2 * chip + first) * rows, 16)
                out_ref[pl.ds(target, rows), :] = ref[pl.ds(chip * rows, rows), :]

    inside = pl.BlockSpec(memory_space=pltpu.VMEM)
    return pl.pallas_call(
        kernel,
        out_shape=jax.ShapeDtypeStruct((2 * chips * rows, width), BF),
        in_specs=[pl.BlockSpec(memory_space=pltpu.SMEM), inside, inside],
        out_specs=inside,
        compiler_params=pltpu.CompilerParams(vmem_limit_bytes=VMEM_BYTES),
        cost_estimate=SMALL,
        name="interleave",
    )(core[None], own, other)


def swap_tensor(x):
    return lax.ppermute(x, "tensor", [(0, 1), (1, 0)])


def whole_rows(own, other, rank):
    return jnp.where(
        rank == 0, jnp.concatenate([own, other], axis=0), jnp.concatenate([other, own], axis=0)
    )


def sum_pairs(x, step):
    pairs = [(i, i ^ step) for i in range(lax.axis_size("dp"))]
    return x + lax.ppermute(x, "dp", pairs)


def rms_scale(rows):
    return lax.rsqrt(jnp.mean(rows * rows, axis=-1, keepdims=True) + EPS)


def norm_back(grad, normed, scale, gain):
    weighted = grad * gain
    return scale * (weighted - normed * jnp.mean(weighted * normed, axis=-1, keepdims=True))


def dot32(a, b, dims):
    return lax.dot_general(a, b, (dims, ((), ())), preferred_element_type=F32)


NN = ((1,), (0,))
NT = ((1,), (1,))
TN = ((0,), (0,))


def attention_forward(x, gain, weights, by_offset, seq_col, seq_row):
    count, d = x.shape
    head_cols = weights.shape[1] // 4
    heads = head_cols // HEAD_DIM
    scale = HEAD_DIM ** (-0.5)
    lanes = by_offset.shape[1]

    def kernel(x_ref, gain_ref, w_ref, off_ref, col_ref, row_ref, *outs):
        normed_ref, scale_ref, proj_ref, p_ref, context_ref, part_ref = outs
        rows = x_ref[...].astype(F32)
        r = lax.rsqrt(jnp.mean(rows * rows, axis=-1, keepdims=True) + EPS)
        scale_ref[...] = r
        normed = (rows * r * gain_ref[...]).astype(BF)
        normed_ref[...] = normed
        for s in range(3):
            at = pl.ds(s * head_cols, head_cols)
            proj_ref[:, at] = dot32(normed, w_ref[:, at], NN).astype(BF)
        same = col_ref[...] == row_ref[...]
        for h in range(heads):
            q = proj_ref[:, pl.ds(h * HEAD_DIM, HEAD_DIM)]
            k = proj_ref[:, pl.ds(head_cols + h * HEAD_DIM, HEAD_DIM)]
            v = proj_ref[:, pl.ds(2 * head_cols + h * HEAD_DIM, HEAD_DIM)]
            line = jnp.broadcast_to(off_ref[pl.ds(h, 1), :], (count, lanes))
            bias = pltpu.roll(line, lanes - (count - 1), 1, stride=1, stride_axis=0)[:, :count]
            scores = jnp.where(same, dot32(q, k, NT) * scale + bias, NEG)
            expo = jnp.exp(scores - jnp.max(scores, axis=-1, keepdims=True))
            p = expo / jnp.sum(expo, axis=-1, keepdims=True)
            p_ref[h] = p
            context_ref[:, pl.ds(h * HEAD_DIM, HEAD_DIM)] = dot32(p.astype(BF), v, NN).astype(BF)
        out_w = w_ref[:, pl.ds(3 * head_cols, head_cols)]
        part_ref[...] = dot32(context_ref[...], out_w, NT).astype(BF)

    inside = pl.BlockSpec(memory_space=pltpu.VMEM)
    return pl.pallas_call(
        kernel,
        out_shape=(
            jax.ShapeDtypeStruct((count, d), BF),
            jax.ShapeDtypeStruct((count, 1), F32),
            jax.ShapeDtypeStruct((count, 3 * head_cols), BF),
            jax.ShapeDtypeStruct((heads, count, count), F32),
            jax.ShapeDtypeStruct((count, head_cols), BF),
            jax.ShapeDtypeStruct((count, d), BF),
        ),
        in_specs=[inside] * 6,
        out_specs=(inside,) * 6,
        compiler_params=pltpu.CompilerParams(vmem_limit_bytes=VMEM_BYTES),
        cost_estimate=SMALL,
        name="attention_forward",
    )(x, gain, weights, by_offset, seq_col, seq_row)


def attention_backward(low, other, hidden, scales, gain, out_grad, weights, proj, p_full, lanes):
    count, d = low.shape
    head_cols = weights.shape[1] // 4
    heads = head_cols // HEAD_DIM
    scale = HEAD_DIM ** (-0.5)

    def kernel(low_ref, other_ref, hidden_ref, scales_ref, gain_ref, g_ref, w_ref, proj_ref, p_ref,
               hidden_grad_ref, grad_ref, out_ref, sums_ref, gc_ref):
        r2 = scales_ref[:, 3:4]
        n = hidden_ref[...] * r2
        u = (low_ref[...].astype(F32) + other_ref[...].astype(F32)) * gain_ref[...]
        total = g_ref[...].astype(F32) + r2 * (u - n * jnp.mean(u * n, axis=-1, keepdims=True))
        hidden_grad_ref[...] = total
        grad_ref[...] = total.astype(BF)
        out_w = w_ref[:, pl.ds(3 * head_cols, head_cols)]
        gc_ref[...] = dot32(grad_ref[...], out_w, NN).astype(BF)
        down = lax.broadcasted_iota(jnp.int32, (count, count), 0)
        across = lax.broadcasted_iota(jnp.int32, (count, count), 1)
        flip = (down + across == count - 1).astype(F32).astype(BF)
        for h in range(heads):
            at = [pl.ds(s * head_cols + h * HEAD_DIM, HEAD_DIM) for s in range(3)]
            q, k, v = proj_ref[:, at[0]], proj_ref[:, at[1]], proj_ref[:, at[2]]
            p = p_ref[h]
            gc = gc_ref[:, at[0]]
            dp = dot32(gc, v, NT)
            ds = (p * (dp - jnp.sum(p * dp, axis=-1, keepdims=True))).astype(BF)
            out_ref[:, at[0]] = (dot32(ds, k, NN) * scale).astype(BF)
            out_ref[:, at[1]] = (dot32(ds, q, TN) * scale).astype(BF)
            out_ref[:, at[2]] = dot32(p.astype(BF), gc, TN).astype(BF)
            turned = dot32(ds, flip, TN)
            wide = jnp.concatenate([turned, jnp.zeros((count, lanes - count), F32)], axis=1)
            rolled = pltpu.roll(wide, 0, 1, stride=1, stride_axis=0)
            sums_ref[pl.ds(h, 1), :] = jnp.sum(rolled, axis=0, keepdims=True)

    inside = pl.BlockSpec(memory_space=pltpu.VMEM)
    return pl.pallas_call(
        kernel,
        out_shape=(
            jax.ShapeDtypeStruct((count, d), F32),
            jax.ShapeDtypeStruct((count, d), BF),
            jax.ShapeDtypeStruct((count, 3 * head_cols), BF),
            jax.ShapeDtypeStruct((heads, lanes), F32),
        ),
        in_specs=[inside] * 9,
        out_specs=(inside,) * 4,
        scratch_shapes=[pltpu.VMEM((count, head_cols), BF)],
        compiler_params=pltpu.CompilerParams(vmem_limit_bytes=VMEM_BYTES),
        cost_estimate=SMALL,
        name="attention_backward",
    )(low, other, hidden, scales, gain, out_grad, weights, proj, p_full)


def route(x, part, other, gain, w_router, expert_col, flat, out_grad):
    count, d = x.shape

    def kernel(x_ref, part_ref, other_ref, gain_ref, w_ref, expert_ref, flat_ref, g_ref,
               hidden_ref, out_ref, scales_ref, blocks_ref, sem):
        hidden = x_ref[...].astype(F32) + (part_ref[...].astype(F32) + other_ref[...].astype(F32))
        hidden_ref[...] = hidden
        r2 = lax.rsqrt(jnp.mean(hidden * hidden, axis=-1, keepdims=True) + EPS)
        mixed = hidden * r2 * gain_ref[...]
        logits = [
            jnp.sum(mixed * w_ref[e : e + 1, :], axis=-1, keepdims=True) for e in range(EXPERTS)
        ]
        top = jnp.maximum(logits[0], logits[1])
        expo = [jnp.exp(v - top) for v in logits]
        probs = [v / (expo[0] + expo[1]) for v in expo]
        hits = [(expert_ref[...] == e).astype(F32) for e in range(EXPERTS)]
        gate = probs[0] * hits[0] + probs[1] * hits[1]
        lane = lax.broadcasted_iota(jnp.int32, (count, 128), 1)
        columns = [gate] + [gate * (h - p) for h, p in zip(hits, probs)] + [r2]
        scales_ref[...] = sum(jnp.where(lane == i, v, 0.0) for i, v in enumerate(columns))
        slots = lax.broadcasted_iota(jnp.int32, (EXPERTS * CAP, count), 0)
        chosen = (slots == flat_ref[...]).astype(F32).astype(BF)
        blocks_ref[:, pl.ds(0, d)] = dot32(chosen, mixed.astype(BF), NN).astype(BF)
        grad_routed = (gate * g_ref[...].astype(F32)).astype(BF)
        blocks_ref[:, pl.ds(d, d)] = dot32(chosen, grad_routed, NN).astype(BF)
        copy = pltpu.make_async_copy(blocks_ref, out_ref, sem)
        copy.start()
        copy.wait()

    inside = pl.BlockSpec(memory_space=pltpu.VMEM)
    return pl.pallas_call(
        kernel,
        out_shape=(
            jax.ShapeDtypeStruct((count, d), F32),
            jax.ShapeDtypeStruct((EXPERTS * CAP, 2 * d), BF),
            jax.ShapeDtypeStruct((count, 128), F32),
        ),
        in_specs=[inside] * 8,
        out_specs=(inside, pl.BlockSpec(memory_space=pltpu.HBM), inside),
        scratch_shapes=[pltpu.VMEM((EXPERTS * CAP, 2 * d), BF), pltpu.SemaphoreType.DMA],
        compiler_params=pltpu.CompilerParams(vmem_limit_bytes=VMEM_BYTES),
        cost_estimate=SMALL,
        name="route",
    )(x, part, other, gain, w_router, expert_col, flat, out_grad)


def rows_back(mine, got, hidden, scales, gain, w_router, flat, out_grad):
    count, d = hidden.shape

    def kernel(mine_ref, got_ref, hidden_ref, scales_ref, gain_ref, w_ref, flat_ref, g_ref,
               mixed_ref, routed_ref, gains_ref):
        sums = (mine_ref[...].astype(F32) + got_ref[...].astype(F32)).astype(BF)
        slots = lax.broadcasted_iota(jnp.int32, (count, EXPERTS * CAP), 1)
        chosen = (slots == flat_ref[...]).astype(F32).astype(BF)
        routed = dot32(chosen, sums[:, :d], NN)
        gate, r2 = scales_ref[:, 0:1], scales_ref[:, 3:4]
        routed_ref[...] = (gate * routed).astype(BF)
        gate_part = jnp.sum(g_ref[...].astype(F32) * routed, axis=-1, keepdims=True)
        grad_logits = [gate_part * scales_ref[:, 1 + e : 2 + e] for e in range(EXPERTS)]
        part = dot32(chosen, sums[:, d:], NN)
        part = part + sum(grad_logits[e] * w_ref[e : e + 1, :] for e in range(EXPERTS))
        mixed_ref[...] = part.astype(BF)
        n = hidden_ref[...] * r2
        gains_ref[0:1, :] = jnp.sum(part * n, axis=0, keepdims=True)
        mixed = n * gain_ref[...]
        for e in range(EXPERTS):
            gains_ref[1 + e : 2 + e, :] = jnp.sum(mixed * grad_logits[e], axis=0, keepdims=True)
        gains_ref[1 + EXPERTS :, :] = jnp.zeros((7 - EXPERTS, d), F32)

    inside = pl.BlockSpec(memory_space=pltpu.VMEM)
    return pl.pallas_call(
        kernel,
        out_shape=(
            jax.ShapeDtypeStruct((count, d), BF),
            jax.ShapeDtypeStruct((count, d), BF),
            jax.ShapeDtypeStruct((8, d), F32),
        ),
        in_specs=[inside] * 8,
        out_specs=(inside,) * 3,
        compiler_params=pltpu.CompilerParams(vmem_limit_bytes=VMEM_BYTES),
        cost_estimate=SMALL,
        name="rows_back",
    )(mine, got, hidden, scales, gain, w_router, flat, out_grad)


def input_back(grad, weights, x, sums, bucket_hits, gains, rank):
    count, d = x.shape
    heads, lanes = sums.shape
    buckets = bucket_hits.shape[1]
    each = d // 128

    def kernel(rank_ref, grad_ref, w_ref, x_ref, sums_ref, hits_ref, gains_ref, low_ref, line_ref):
        part = dot32(grad_ref[...], w_ref[:, pl.ds(0, grad_ref.shape[1])], NT)
        low_ref[...] = part.astype(BF)
        rows = x_ref[...].astype(F32)
        n = rows * lax.rsqrt(jnp.mean(rows * rows, axis=-1, keepdims=True) + EPS)
        vectors = [jnp.sum(part * n, axis=0, keepdims=True)]
        vectors += [gains_ref[k : k + 1, :] for k in range(1 + EXPERTS)]
        for k, vector in enumerate(vectors):
            for j in range(each):
                line_ref[pl.ds(16 + k * each + j, 1), :] = vector[:, j * 128 : (j + 1) * 128]
        rel = jnp.dot(sums_ref[...], hits_ref[...], precision=HIGH, preferred_element_type=F32)
        rel = jnp.concatenate([rel, jnp.zeros((heads, 128 - buckets), F32)], axis=1)
        line_ref[0:16, :] = jnp.zeros((16, 128), F32)
        for k in range(2):
            line_ref[pl.ds(k * heads, heads), :] = jnp.where(rank_ref[0] == k, rel, 0.0)

    inside = pl.BlockSpec(memory_space=pltpu.VMEM)
    return pl.pallas_call(
        kernel,
        out_shape=(
            jax.ShapeDtypeStruct((count, d), BF),
            jax.ShapeDtypeStruct((16 + (2 + EXPERTS) * each, 128), F32),
        ),
        in_specs=[pl.BlockSpec(memory_space=pltpu.SMEM)] + [inside] * 6,
        out_specs=(inside,) * 2,
        compiler_params=pltpu.CompilerParams(vmem_limit_bytes=VMEM_BYTES),
        cost_estimate=SMALL,
        name="input_back",
    )(rank[None], grad, weights, x, sums, bucket_hits, gains)


def body(
    block_in,
    attn_gain,
    w_qkv,
    w_out,
    rel_bias,
    moe_gain,
    w_router,
    w_in,
    w_down,
    seq_lengths,
    expert_ids,
    rel_table,
    out_grad,
):
    rows_local, width = block_in.shape
    rank = lax.axis_index("tensor")
    ring = Ring()
    shard = w_out.shape[0]
    head_cols = w_out.shape[1]
    units = w_in.shape[2]
    heads_local = head_cols // HEAD_DIM
    count = 2 * rows_local

    attn_shard = jnp.concatenate([w_qkv.reshape(shard, 3 * head_cols), w_out], axis=1)
    x_other, g_other = swap_tensor(block_in), swap_tensor(out_grad)
    split = units // 2

    def unit_half(w, core):
        return lax.dynamic_slice_in_dim(w, core * split, split, axis=2)

    if not ring.long:
        ring_a = Gather(ring, attn_shard, False)
        a1 = ring_a.step()
        own_half, other_half = (
            jnp.concatenate(
                [unit_half(w, core).reshape(shard, EXPERTS * split) for w in (w_in, w_down)],
                axis=1,
            )
            for core in (ring.core, 1 - ring.core)
        )
        got_half = ring.other_core(other_half)
        a2 = ring_a.step()
        ring_b = Gather(ring, ring.by_core(own_half, got_half, 0), True)
        a3 = ring_a.step()
        a4 = ring_a.step()
        ring_b.step(*a3, x_other, g_other)
        own_a = assemble(ring_a.pieces, ring_a.owners())
        other_a = ring.other_core(own_a)
        attn_all = interleave(own_a, other_a, ring.core, shard)
    else:
        attn_all = lax.all_gather(attn_shard, "dp", axis=0, tiled=True)
        in_all, down_all = (
            unit_half(lax.all_gather(w, "dp", axis=0, tiled=True), ring.core).reshape(
                -1, EXPERTS * split
            )
            for w in (w_in, w_down)
        )
    x_low = whole_rows(block_in, x_other, rank)
    g_low = whole_rows(out_grad, g_other, rank)

    places = jnp.arange(count, dtype=jnp.int32)
    ends = jnp.cumsum(seq_lengths[0])
    seq_ids = jnp.sum((places[:, None] >= ends[None, :]).astype(jnp.int32), axis=1)
    bias_local = lax.dynamic_slice_in_dim(rel_bias, rank * heads_local, heads_local, 1)
    bucket_hits = (
        rel_table[:, None] == jnp.arange(rel_bias.shape[0], dtype=jnp.int32)[None, :]
    ).astype(F32)
    by_offset = jnp.dot(bucket_hits, bias_local, precision=HIGH)
    lanes = 2 * count
    by_offset = jnp.pad(by_offset.T, ((0, 0), (0, lanes - by_offset.shape[0])))
    normed_one, _, projected, p_full, context, attn_part = attention_forward(
        x_low, attn_gain[None, :], attn_all, by_offset, seq_ids[:, None], seq_ids[None, :]
    )
    if not ring.long:
        ring_b.step()
        ring_b.step(attn_part)
    attn_other = swap_tensor(attn_part)
    expert_col = expert_ids[:, 0]
    hits = (
        expert_col[:, None] == jnp.arange(EXPERTS, dtype=jnp.int32)[None, :]
    ).astype(jnp.int32)
    flat = expert_col * CAP + jnp.sum(jnp.cumsum(hits, axis=0) * hits, axis=1) - 1
    gain_row, router_rows = moe_gain[None, :], w_router.T
    hidden, own_blocks, scales = route(
        x_low, attn_part, attn_other, gain_row, router_rows, expert_ids, flat[None, :], g_low
    )
    if not ring.long:
        got_blocks = ring.other_core(own_blocks)
        state = place(ring_b.pieces, ring_b.owners(0, ring.chips - 1), ring.chips)
        last = ring_b.step(got_blocks)
        mine, away, terms = expert_layers(
            own_blocks,
            got_blocks,
            state,
            last,
            ring.chip_at(ring.chips // 2),
            ring.slot_chips(),
            2 * shard,
        )
        send = Scatter(ring, terms, 2 * shard)
        c1 = send.step()
    else:
        first = jnp.zeros((1,), jnp.int32)
        mine, away, terms = expert_layers(
            own_blocks,
            ring.other_core(own_blocks),
            (in_all, down_all),
            (),
            first[0],
            first,
            width,
        )
    got_sums = ring.other_core(away)
    mixed_low, routed_low, gains = rows_back(
        mine, got_sums, hidden, scales, gain_row, router_rows, flat[:, None], g_low
    )
    if not ring.long:
        c2 = send.step(mixed_low)
    mixed_other = swap_tensor(mixed_low)
    if not ring.long:
        (mixed_other,) = after((mixed_other,), c1)

    def own_rows(x):
        return lax.dynamic_slice_in_dim(x, rank * rows_local, rows_local, 0)

    def other_rows(x):
        return lax.dynamic_slice_in_dim(x, (1 - rank) * rows_local, rows_local, 0)

    routed_other = swap_tensor(other_rows(routed_low))
    result = own_rows(hidden) + (
        own_rows(routed_low).astype(F32) + routed_other.astype(F32)
    )
    grad_hidden, grad_attended, grad_projected, offset_sums = attention_backward(
        mixed_low, mixed_other, hidden, scales, gain_row, g_low, attn_all, projected, p_full, lanes
    )

    attn_pairs = [(normed_one, grad_projected), (grad_attended, context)]
    if not ring.long:
        attn_pairs[0] = (normed_one, after((grad_projected,), c2)[0])
        chips = ring.slot_chips()
        owners = jnp.concatenate([chips * 2 + ring.core, chips * 2 + 1 - ring.core])
        send_a = Scatter(ring, outer(attn_pairs, owners, shard, [ring.chips] * 2), shard)
        c3 = send.step()
        a1 = send_a.step()
    hits_wide = jnp.pad(bucket_hits, ((0, lanes - bucket_hits.shape[0]), (0, 0)))
    normed_low, line = input_back(
        grad_projected, attn_all, x_low, offset_sums, hits_wide, gains, rank
    )
    normed_other = swap_tensor(other_rows(normed_low))
    line = line + swap_tensor(line)
    line = line + ring.other_core(line)
    if not ring.long:
        c4 = send.step(*a1)
        a2 = send_a.step(*c3)
        a3 = send_a.step(*c4)
        (line,) = after((line,), c4)
        line = sum_pairs(line, 2)
        line = sum_pairs(line, 4)
        (line,) = after((line,), a3)
    else:
        line = sum_pairs(sum_pairs(line, 2), 4)
    step = 8
    while step < ring.n:
        line = sum_pairs(line, step)
        step *= 2
    summed = line
    grad_normed = own_rows(normed_low).astype(F32) + normed_other.astype(F32)
    x_own = block_in.astype(F32)
    scale_own = rms_scale(x_own)
    grad_block = own_rows(grad_hidden) + norm_back(
        grad_normed, x_own * scale_own, scale_own, attn_gain
    )
    if ring.long:
        zeros = jnp.zeros((width, 2 * EXPERTS, units), BF)
        terms = terms[0].reshape(width, 2 * EXPERTS, split)
        terms = lax.dynamic_update_slice_in_dim(zeros, terms, ring.core * split, 2)
        sums = lax.psum_scatter(terms, "dp", scatter_dimension=0, tiled=True).astype(F32)
        grad_w_in_mine, grad_w_down_mine = sums[:, :EXPERTS], sums[:, EXPERTS:]
        terms = jnp.concatenate([dot32(x, y, TN).astype(BF) for x, y in attn_pairs], axis=1)
        attn_mine = lax.psum_scatter(terms, "dp", scatter_dimension=0, tiled=True)
        attn_mine = attn_mine.astype(F32)
    else:
        send_a.step()
        sent = after(send.sent, send_a.going)
        mine, away = ring_total(send.blocks(0)[0], sent, ring.core)
        grad_w_in_mine, grad_w_down_mine = combine(mine, ring.other_core(away), ring.core)
        attn_mine = send_a.total()
    summed_rel = summed[: rel_bias.shape[1], : rel_bias.shape[0]].T
    summed = summed[16:].reshape(2 + EXPERTS, width)
    return (
        result.astype(BF),
        grad_block,
        summed[0],
        attn_mine[:, : 3 * head_cols].reshape(w_qkv.shape),
        attn_mine[:, 3 * head_cols :],
        summed_rel,
        summed[1],
        summed[2:].T,
        grad_w_in_mine,
        grad_w_down_mine,
    )


def solution(mesh):
    placed = (
        P(("dp", "tensor"), None),
        P(),
        P("dp", None, "tensor"),
        P("dp", "tensor"),
        P(),
        P(),
        P(),
        P("dp", None, "tensor"),
        P("dp", None, "tensor"),
        P("dp", None),
        P("dp", None),
        P(),
        P(("dp", "tensor"), None),
    )
    return jax.shard_map(
        body,
        mesh=mesh,
        in_specs=placed,
        out_specs=(
            P(("dp", "tensor"), None),
            P(("dp", "tensor"), None),
            P(),
            P("dp", None, "tensor"),
            P("dp", "tensor"),
            P(),
            P(),
            P(),
            P("dp", None, "tensor"),
            P("dp", None, "tensor"),
        ),
        check_vma=False,
    )
```
